1024 devices in a mesh: slab: 32 (over z_lo, y, core), plane: 32 (over x, z_hi).
Axes of the slice: x: 8, y: 8, z: 8 (z_hi: 4, z_lo: 2; z = z_hi * 2 + z_lo), core: 2. Of those that a mesh axis runs over, the one named last changes fastest.
Arguments:
- start_disp: float32 [3, 512, 512, 128], P(None, 'slab', 'plane'), may hold values from -6 to 6
- load: float32 [3, 512, 512, 128], P(None, 'slab', 'plane'), may hold values from -6 to 6
- shift: float32 [512, 512, 128], P('slab', 'plane'), may hold values from 0.25 to 2
- coarse: float32 [3, 256, 256, 128], P(None, 'slab', 'plane'), may hold values from -6 to 6
- aggregate: int32 [512, 512], P('slab', 'plane'), may hold values from 0 to 65535, as said below
- consistency: float32 [512, 512, 128], P('slab', 'plane'), may hold values from 0.5 to 2
Outputs:
- displacement: float32 [3, 512, 512, 128], P(None, 'slab', 'plane')
- recovered: float32 [6, 512, 512, 128], P(None, 'slab', 'plane')
- indicator: float32 [512, 512, 128], P('slab', 'plane')
The draws below stay inside these ranges and needn't reach their ends.
Inputs may be any that keep to these rules, and one draw needn't show every extreme that they name: aggregate[i, j] = a * 256 + b with |a - i // 2| <= 1 and |b - j // 2| <= 1.
All inputs are finite; a program needn't handle non-finite values.
Results may differ from the reference program's by a relative error of at most 0.000029.
Values sent between devices are 32-bit elements; how exact they have to be, the bound alone decides.
No kernel may reach another device: no remote copies, remote signals or barrier semaphores. Data moves between devices by JAX's collectives and lax.ppermute only.
A program may use at most 32 MiB of HBM per device.

```python
import math
import jax
import jax.numpy as jnp

CZ = 128
DEGREE = 4
NX = 512
NY = 512
KX = 256
KY = 256


def draw_aggregate(key, part):
    key = jax.random.fold_in(key, 7)
    key_a, key_b = jax.random.split(key)
    ix = jnp.arange(NX)[:, None]
    iy = jnp.arange(NY)[None, :]
    step_a = jax.random.randint(key_a, (NX, NY), -1, 2)
    step_b = jax.random.randint(key_b, (NX, NY), -1, 2)
    corner = (ix == 0) & (iy == 0) | (ix == NX - 1) & (iy == NY - 1)
    step_a = jnp.where(corner, 0, step_a)
    step_b = jnp.where(corner, 0, step_b)
    row_a = jnp.clip(ix // 2 + step_a, 0, NX // 2 - 1)
    row_b = jnp.clip(iy // 2 + step_b, 0, NY // 2 - 1)
    return (row_a * (NY // 2) + row_b).astype(jnp.int32)


def levels(stream_key, extent, cuts, smallest, high):
    def one(dim, parts):
        heights = jax.random.uniform(jax.random.fold_in(jax.random.fold_in(stream_key, 6), dim), (parts,), jnp.float32, smallest / len(cuts), high / len(cuts))
        return jnp.repeat(jnp.exp(heights), extent[dim] // parts).reshape((-1,) + (1,) * (len(extent) - dim - 1))

    factor_of = one(*cuts[0])
    for cut in cuts[1:]:
        factor_of = factor_of * one(*cut)
    return factor_of


def bell_draw(own_key, dims, width, bound, shards=(), kind=jnp.bfloat16):
    values = width * jax.random.normal(own_key, dims, jnp.float32)
    if shards:
        values = values * levels(own_key, dims, shards, -0.22, 0.18)
    return jnp.clip(values, -bound, bound).astype(kind)


def setup_inputs(seed: int = 0) -> dict:
    splits = jax.random.split(jax.random.key(seed), 7)
    return {
        "start_disp": bell_draw(splits[0], (3, NX, NY, CZ), 1.0, 6.0, ((1, 32), (2, 32)), jnp.float32),
        "load": bell_draw(splits[1], (3, NX, NY, CZ), 1.0, 6.0, ((1, 32), (2, 32)), jnp.float32),
        "shift": jnp.clip(0.25 + 1.75 * jax.random.uniform(splits[2], (NX, NY, CZ), jnp.float32) ** levels(splits[2], (NX, NY, CZ), ((0, 32), (1, 32)), -0.2, 0.2), 0.25, 2.0),
        "coarse": bell_draw(splits[3], (3, KX, KY, CZ), 1.0, 6.0, ((1, 32), (2, 32)), jnp.float32),
        "aggregate": draw_aggregate(jax.random.fold_in(splits[6], 71), 0),
        "consistency": jnp.clip(jnp.exp(math.log(2.0) - 1.3862944 * jax.random.uniform(splits[5], (NX, NY, CZ), jnp.float32) ** levels(splits[5], (NX, NY, CZ), ((0, 32), (1, 32)), -0.2, 0.2)), 0.5, 2.0),
    }


THETA = 4.5
DELTA_C = 3.5


def stiff_apply(padded, shift_part):
    zpad = jnp.pad(padded, ((0, 0), (0, 0), (0, 0), (1, 1)))
    along_z = zpad[..., :-2] + zpad[..., 1:-1] + zpad[..., 2:]
    along_x = along_z[:, :-2] + along_z[:, 1:-1] + along_z[:, 2:]
    boxed = along_x[:, :, :-2] + along_x[:, :, 1:-1] + along_x[:, :, 2:]
    centre = padded[:, 1:-1, 1:-1]
    return (3.0 + shift_part) * centre - boxed / 3.0


def element_stress(corners, consist):
    zpad = jnp.pad(corners, ((0, 0), (0, 0), (0, 0), (0, 1)))
    diff_x = zpad[:, 1:] - zpad[:, :-1]
    grad_x = 0.25 * (diff_x[:, :, :-1, :-1] + diff_x[:, :, 1:, :-1] + diff_x[:, :, :-1, 1:] + diff_x[:, :, 1:, 1:])
    diff_y = zpad[:, :, 1:] - zpad[:, :, :-1]
    grad_y = 0.25 * (diff_y[:, :-1, :, :-1] + diff_y[:, 1:, :, :-1] + diff_y[:, :-1, :, 1:] + diff_y[:, 1:, :, 1:])
    diff_z = zpad[..., 1:] - zpad[..., :-1]
    grad_z = 0.25 * (diff_z[:, :-1, :-1] + diff_z[:, 1:, :-1] + diff_z[:, :-1, 1:] + diff_z[:, 1:, 1:])
    exx = grad_x[0]
    eyy = grad_y[1]
    ezz = grad_z[2]
    exy = 0.5 * (grad_y[0] + grad_x[1])
    eyz = 0.5 * (grad_z[1] + grad_y[2])
    ezx = 0.5 * (grad_x[2] + grad_z[0])
    trace = exx + eyy + ezz
    sxx = exx - trace / 3.0
    syy = eyy - trace / 3.0
    szz = ezz - trace / 3.0
    equiv = (2.0 / 3.0) * (sxx * sxx + syy * syy + szz * szz + 2.0 * (exy * exy + eyz * eyz + ezx * ezx))
    visc = consist * (0.01 + 3.0 * equiv) ** ((0.15 - 1.0) / 2.0)
    sig = [2.0 * visc * sxx + 4.0 * trace, 2.0 * visc * syy + 4.0 * trace, 2.0 * visc * szz + 4.0 * trace,
           2.0 * visc * exy, 2.0 * visc * eyz, 2.0 * visc * ezx]
    norm_sq = sig[0] * sig[0] + sig[1] * sig[1] + sig[2] * sig[2] + 2.0 * (sig[3] * sig[3] + sig[4] * sig[4] + sig[5] * sig[5])
    return jnp.stack(sig + [norm_sq], 0)


def finish_nodes(total, count):
    rec = total[:6] / count
    norm_rec = rec[0] * rec[0] + rec[1] * rec[1] + rec[2] * rec[2] + 2.0 * (rec[3] * rec[3] + rec[4] * rec[4] + rec[5] * rec[5])
    return rec, total[6] / count - norm_rec


def reference(start_disp, load, shift, coarse, aggregate, consistency):
    table = coarse.reshape(3, KX * KY, CZ)
    moved = jnp.take(table, aggregate.reshape(-1), axis=1).reshape(3, NX, NY, CZ)
    disp = start_disp + moved
    pad_xy = ((0, 0), (1, 1), (1, 1), (0, 0))

    def stiff(field):
        return stiff_apply(jnp.pad(field, pad_xy), shift)

    sigma = THETA / DELTA_C
    resid = load - stiff(disp)
    direction = resid / THETA
    rho = 1.0 / sigma
    for step in range(DEGREE):
        disp = disp + direction
        if step < DEGREE - 1:
            resid = resid - stiff(direction)
            rho_new = 1.0 / (2.0 * sigma - rho)
            direction = (rho_new * rho) * direction + (2.0 * rho_new / DELTA_C) * resid
            rho = rho_new
    corners = jnp.pad(disp, ((0, 0), (0, 1), (0, 1), (0, 0)))
    ix = jnp.arange(NX)[:, None, None]
    iy = jnp.arange(NY)[None, :, None]
    iz = jnp.arange(CZ)[None, None, :]
    valid = ((ix <= NX - 2) & (iy <= NY - 2) & (iz <= CZ - 2)).astype(jnp.float32)
    elem = element_stress(corners, consistency) * valid
    front = jnp.pad(elem, ((0, 0), (1, 0), (1, 0), (1, 0)))
    sum_x = front[:, 1:] + front[:, :-1]
    sum_y = sum_x[:, :, 1:] + sum_x[:, :, :-1]
    total = sum_y[..., 1:] + sum_y[..., :-1]
    count = (((ix >= 1).astype(jnp.float32) + (ix <= NX - 2).astype(jnp.float32))
             * ((iy >= 1).astype(jnp.float32) + (iy <= NY - 2).astype(jnp.float32))
             * ((iz >= 1).astype(jnp.float32) + (iz <= CZ - 2).astype(jnp.float32)))
    rec, indic = finish_nodes(total, count)
    return disp, rec, indic
```

```python
import functools

import jax
import jax.numpy as jnp
from jax import lax
from jax.experimental import pallas as pl
from jax.experimental.pallas import tpu as pltpu
from jax.sharding import PartitionSpec as P

B = 16
CB = 8
Z = 128
W = 24
ROWS = 26

DEGREE = 4
THETA = 4.5
DELTA_C = 3.5
F32 = jnp.float32

PS, PL_, PH, PK, PA, PC = 0, 240, 432, 496, 592, 608
PF_ROWS, PB_ROWS = 624, 608

QS, QL, QH, QC, QK, QX, QA = 0, 360, 648, 744, 768, 960, 1008
Q_ROWS = 1016


def place(col):
    index = col + 4
    return (index % 3) * 8 + index // 3


def pack_kernel(start, load, shift, cons, coarse, agg, fwd, bwd):
    slab = lax.axis_index("slab")
    plane = lax.axis_index("plane")
    coarse_cols = CB * lax.axis_size("plane")
    for c in range(3):
        for w in range(5):
            row = PS + 16 * (5 * c + w)
            fwd[row : row + 16, :] = start[pl.ds(256 * c + 11 + w, 16, stride=16), :]
            bwd[row : row + 16, :] = start[pl.ds(256 * c + w, 16, stride=16), :]
        for w in range(4):
            row = PL_ + 16 * (4 * c + w)
            fwd[row : row + 16, :] = load[pl.ds(256 * c + 12 + w, 16, stride=16), :]
            bwd[row : row + 16, :] = load[pl.ds(256 * c + w, 16, stride=16), :]
            row = PK + 8 * (4 * c + w)
            fwd[row : row + 8, :] = coarse[pl.ds(64 * c + 4 + w, 8, stride=8), :]
            bwd[row : row + 8, :] = coarse[pl.ds(64 * c + w, 8, stride=8), :]
    for w in range(4):
        row = PH + 16 * w
        fwd[row : row + 16, :] = shift[pl.ds(12 + w, 16, stride=16), :]
        bwd[row : row + 16, :] = shift[pl.ds(w, 16, stride=16), :]
    fwd[PC : PC + 16, :] = cons[pl.ds(15, 16, stride=16), :]
    value = agg[...]
    step_a = value // coarse_cols - (slab * CB + lax.broadcasted_iota(jnp.int32, (B, B), 0) // 2) + 1
    step_b = value % coarse_cols - (plane * CB + lax.broadcasted_iota(jnp.int32, (B, B), 1) // 2) + 1
    code = (1 + 16 * step_a + step_b).astype(F32)
    for out in (fwd, bwd):
        out[PA : PA + 16, :] = jnp.zeros((16, Z), F32)
        out[PA : PA + 16, 0:B] = code


OWN = ((0, 2, 2, 5), (1, 1, 0, 6), (2, 1, 1, 5))


def own_kernel(start, load, shift, cons, coarse, fwd, es, el, eh, ec, ek, ea):
    def rows(ci, carry):
        for l, s0, j0, n in OWN:
            for src, dst in ((start, es), (load, el)):
                dst[ci, 8 * l + s0 : 8 * l + s0 + n, :] = src[ci, pl.ds(j0, n, stride=3), :]
        return carry

    lax.fori_loop(0, 3 * B, rows, 0, unroll=4)

    def rows1(ci, carry):
        for l, s0, j0, n in OWN:
            for src, dst in ((shift, eh), (cons, ec)):
                dst[ci, 8 * l + s0 : 8 * l + s0 + n, :] = src[ci, pl.ds(j0, n, stride=3), :]
        return carry

    lax.fori_loop(0, B, rows1, 0, unroll=4)
    for ca in range(3 * CB):
        ek[ca, 4:12, :] = coarse[ca]
    ea[...] = pltpu.roll(fwd[PA : PA + 16, :], 5, 1)


def join_kernel(low, high, es, el, eh, ec, ek, ea, es_o, el_o, eh_o, ec_o, ek_o, ea_o, ex_o, on, off):
    del es, el, eh, ec, ek
    for c in range(3):
        for w in range(5):
            row = PS + 16 * (5 * c + w)
            if w > 0:
                es_o[pl.ds(384 * c + place(w - 5), 16, stride=24), :] = low[row : row + 16, :]
            else:
                ex_o[2 * c] = low[row : row + 16, :]
            if w < 4:
                es_o[pl.ds(384 * c + place(16 + w), 16, stride=24), :] = high[row : row + 16, :]
            else:
                ex_o[2 * c + 1] = high[row : row + 16, :]
        for w in range(4):
            row = PL_ + 16 * (4 * c + w)
            el_o[pl.ds(384 * c + place(w - 4), 16, stride=24), :] = low[row : row + 16, :]
            el_o[pl.ds(384 * c + place(16 + w), 16, stride=24), :] = high[row : row + 16, :]
            row = PK + 8 * (4 * c + w)
            ek_o[pl.ds(128 * c + w, 8, stride=16), :] = low[row : row + 8, :]
            ek_o[pl.ds(128 * c + 12 + w, 8, stride=16), :] = high[row : row + 8, :]
    for w in range(4):
        row = PH + 16 * w
        eh_o[pl.ds(place(w - 4), 16, stride=24), :] = low[row : row + 16, :]
        eh_o[pl.ds(place(16 + w), 16, stride=24), :] = high[row : row + 16, :]
    ec_o[pl.ds(place(-1), 16, stride=24), :] = low[PC : PC + 16, :]
    lane = lax.broadcasted_iota(jnp.int32, (B, Z), 1)
    left = pltpu.roll(low[PA : PA + 16, :], Z - 11, 1)
    right = pltpu.roll(high[PA : PA + 16, :], 21, 1)
    code = jnp.where(lane < 5, left, jnp.where(lane < 21, ea[...], jnp.where(lane < 26, right, 0.0)))
    ea_o[...] = code
    odd = lax.axis_index("slab") % 2
    for out, top in ((on, 1 - odd), (off, odd)):
        for c in range(3):
            out[QS + 120 * c : QS + 120 * (c + 1), :] = es_o[
                pl.ds(pl.multiple_of(384 * c + top * (11 * W), 8), 120), :
            ]
            out[QL + 96 * c : QL + 96 * (c + 1), :] = el_o[
                pl.ds(pl.multiple_of(384 * c + top * (12 * W), 8), 96), :
            ]
            out[QK + 64 * c : QK + 64 * (c + 1), :] = ek_o[
                pl.ds(pl.multiple_of(128 * c + top * 64, 8), 64), :
            ]
        out[QH : QH + 96, :] = eh_o[pl.ds(pl.multiple_of(top * (12 * W), 8), 96), :]
        out[QC : QC + 24, :] = ec_o[pl.ds(pl.multiple_of(top * (15 * W), 8), 24), :]
        for q in range(6):
            out[QX + 8 * q : QX + 8 * (q + 1), :] = ex_o[q, pl.ds(pl.multiple_of(top * 8, 8), 8), :]
        out[QA : QA + 8, :] = ea_o[pl.ds(pl.multiple_of(top * 8, 8), 8), :]


def smooth_kernel(
    on, off, es, el, eh, ec, ek, ea, ex,
    disp, rec, ind,
    fd, fr, fh, fc, fk, fx, fa, d0, d1, d2, d3, gx, ey, st,
):
    slab = lax.axis_index("slab")
    plane = lax.axis_index("plane")
    n_slab = lax.axis_size("slab")
    n_plane = lax.axis_size("plane")
    odd = slab % 2

    def aligned(index):
        return pl.multiple_of(index, 8)

    for c in range(3):
        fd[c, 5 * W : 21 * W, :] = es[384 * c : 384 * (c + 1), :]
        fr[c, 5 * W : 21 * W, :] = el[384 * c : 384 * (c + 1), :]
        fk[c, 64:192, :] = ek[128 * c : 128 * (c + 1), :]
    fh[5 * W : 21 * W, :] = eh[...]
    fc[5 * W : 21 * W, :] = ec[...]
    for q in range(6):
        fx[q, 8:24, :] = ex[q]
    fa[8:24, :] = ea[...]
    for src, below in ((on.at[1 - odd], odd), (off, 1 - odd)):
        above = 1 - below
        for c in range(3):
            fd[c, pl.ds(aligned(above * (21 * W)), 120), :] = src[QS + 120 * c : QS + 120 * (c + 1), :]
            fr[c, pl.ds(aligned(W + above * (20 * W)), 96), :] = src[QL + 96 * c : QL + 96 * (c + 1), :]
            fk[c, pl.ds(aligned(above * 192), 64), :] = src[QK + 64 * c : QK + 64 * (c + 1), :]
        fh[pl.ds(aligned(W + above * (20 * W)), 96), :] = src[QH : QH + 96, :]
        fc[pl.ds(aligned(4 * W + above * (17 * W)), 24), :] = src[QC : QC + 24, :]
        for q in range(6):
            fx[q, pl.ds(aligned(above * 24), 8), :] = src[QX + 8 * q : QX + 8 * (q + 1), :]
        fa[pl.ds(aligned(above * 24), 8), :] = src[QA : QA + 8, :]

    row = lax.broadcasted_iota(jnp.int32, (32, Z), 0)
    lane = lax.broadcasted_iota(jnp.int32, (32, Z), 1)
    code = fa[...]
    base = 16 * ((row - 8 + 16) // 2 - 8 + 3) + ((lane - 5 + 16) // 2 - 8 + 3) - 1
    inside = (row >= 3) & (row <= 28) & (lane < 26) & (code > 0.0)
    fa[...] = jnp.where(inside, code + base.astype(F32), -1.0)
    sub = lax.broadcasted_iota(jnp.int32, (W, Z), 0)
    lane_w = lax.broadcasted_iota(jnp.int32, (W, Z), 1)
    here = lane_w == 3 * (sub % 8) + sub // 8 + 1
    index = fa[...]
    spread = [jnp.where(here, jnp.broadcast_to(index[e + 3 : e + 4, :], (W, Z)), 0.0) for e in range(ROWS)]
    spread += [jnp.where(lane == 25 * q, index, 0.0) for q in range(2)]
    spread = jnp.concatenate(spread, axis=0).astype(jnp.bfloat16)
    columns = 2 * Z
    wide = jnp.dot(spread, jnp.ones((Z, columns), jnp.bfloat16), preferred_element_type=F32)
    count_nodes = ROWS * W + 64
    which = lax.broadcasted_iota(jnp.int32, (count_nodes, columns), 1).astype(F32)
    hot = (wide == which).astype(F32).astype(jnp.bfloat16)
    for c in range(3):
        table = fk[c]
        high = table.astype(jnp.bfloat16)
        rest = table - high.astype(F32)
        mid = rest.astype(jnp.bfloat16)
        low = (rest - mid.astype(F32)).astype(jnp.bfloat16)
        moved = (
            jnp.dot(hot, high, preferred_element_type=F32)
            + jnp.dot(hot, mid, preferred_element_type=F32)
            + jnp.dot(hot, low, preferred_element_type=F32)
        )
        fd[c] = fd[c] + moved[0 : ROWS * W]
        for q in range(2):
            fx[2 * c + q] = fx[2 * c + q] + moved[ROWS * W + 32 * q : ROWS * W + 32 * (q + 1)]

    place_s = lax.broadcasted_iota(jnp.int32, (8, Z), 0)
    place_z = lax.broadcasted_iota(jnp.int32, (8, Z), 1)
    first_z = place_z == 0
    last_z = place_z == Z - 1
    cols = [plane * B + 3 * place_s + l - 4 for l in range(3)]
    total_y = n_plane * B
    total_x = n_slab * B
    col_in = [((g >= 0) & (g < total_y)).astype(F32) for g in cols]

    def boxed(src, c, e, extra):
        v0, v1, v2 = (src[c, pl.ds(aligned(e * W + 8 * l), 8), :] for l in range(3))
        up = pltpu.roll(v2, 1, 0)
        down = pltpu.roll(v0, 7, 0)
        if extra is not None:
            up = jnp.where(place_s == 0, extra[2 * c, pl.ds(e + 3, 1), :], up)
            down = jnp.where(place_s == 7, extra[2 * c + 1, pl.ds(e + 3, 1), :], down)
        pair = v0 + v1
        out = []
        for t in (pair + up, pair + v2, v1 + v2 + down):
            out.append(
                t
                + jnp.where(first_z, 0.0, pltpu.roll(t, 1, 1))
                + jnp.where(last_z, 0.0, pltpu.roll(t, Z - 1, 1))
            )
        return out

    def stage(src, dst, extra, first, last, keep, gain):
        def sums(e):
            return [boxed(src, c, e, extra) for c in range(3)]

        def step(e, carry):
            before, mid = carry
            after = sums(e + 1)
            row_in = jnp.where((slab * B + e - 5 >= 0) & (slab * B + e - 5 < total_x), gain, 0.0)
            for l in range(3):
                at = pl.ds(aligned(e * W + 8 * l), 8)
                diagonal = 3.0 + fh[at, :]
                weight = col_in[l] * row_in
                for c in range(3):
                    here_v = src[c, at, :]
                    box = before[c][l] + mid[c][l] + after[c][l]
                    r = fr[c, at, :] - (diagonal * here_v - box * (1.0 / 3.0))
                    fr[c, at, :] = r
                    if keep is None:
                        dst[c, at, :] = weight * r
                    else:
                        dst[c, at, :] = keep * here_v + weight * r
            return mid, after

        lax.fori_loop(first, last + 1, step, (sums(first - 1), sums(first)), unroll=2)

    sigma = THETA / DELTA_C
    rho = 1.0 / sigma
    steps = []
    for _ in range(DEGREE - 1):
        rho_new = 1.0 / (2.0 * sigma - rho)
        steps.append((rho_new * rho, 2.0 * rho_new / DELTA_C))
        rho = rho_new
    stage(fd, d0, fx, 1, 24, None, 1.0 / THETA)
    stage(d0, d1, None, 2, 23, *steps[0])
    stage(d1, d2, None, 3, 22, *steps[1])
    stage(d2, d3, None, 4, 21, *steps[2])

    def gather_row(e, carry):
        for c in range(3):
            v = []
            for l in range(3):
                at = pl.ds(aligned(e * W + 8 * l), 8)
                u = fd[c, at, :] + d0[c, at, :] + d1[c, at, :] + d2[c, at, :] + d3[c, at, :]
                st[c * 18 + e - 4, pl.ds(l, 8, stride=3), :] = u
                v.append(u)
            nxt = [v[1], v[2], pltpu.roll(v[0], 7, 0)]
            for l in range(3):
                both = v[l] + nxt[l]
                diff = nxt[l] - v[l]
                both_z = pltpu.roll(both, Z - 1, 1)
                at = pl.ds(aligned((e - 4) * W + 8 * l), 8)
                gx[c, at, :] = both + both_z
                gx[3 + c, at, :] = diff + pltpu.roll(diff, Z - 1, 1)
                gx[6 + c, at, :] = both_z - both
        return carry

    lax.fori_loop(4, 22, gather_row, 0, unroll=2)

    col_ok = [((g >= 0) & (g <= total_y - 2) & (place_z <= Z - 2)).astype(F32) for g in cols]

    def element_row(n, carry):
        gi = slab * B + n - 1
        row_ok = jnp.where((gi >= 0) & (gi <= total_x - 2), 1.0, 0.0)
        made = []
        for l in range(3):
            at = pl.ds(aligned(n * W + 8 * l), 8)
            at_next = pl.ds(aligned((n + 1) * W + 8 * l), 8)
            grad = [[None] * 3 for _ in range(3)]
            for c in range(3):
                grad[c][0] = gx[c, at_next, :] - gx[c, at, :]
                grad[c][1] = gx[3 + c, at_next, :] + gx[3 + c, at, :]
                grad[c][2] = gx[6 + c, at_next, :] + gx[6 + c, at, :]
            exx = 0.25 * grad[0][0]
            eyy = 0.25 * grad[1][1]
            ezz = 0.25 * grad[2][2]
            exy = 0.125 * (grad[0][1] + grad[1][0])
            eyz = 0.125 * (grad[1][2] + grad[2][1])
            ezx = 0.125 * (grad[2][0] + grad[0][2])
            trace = exx + eyy + ezz
            third = trace * (1.0 / 3.0)
            sxx, syy, szz = exx - third, eyy - third, ezz - third
            equiv = (2.0 / 3.0) * (
                sxx * sxx + syy * syy + szz * szz + 2.0 * (exy * exy + eyz * eyz + ezx * ezx)
            )
            ok = col_ok[l] * row_ok
            cons = fc[pl.ds(aligned((n + 4) * W + 8 * l), 8), :]
            power = jnp.exp(((0.15 - 1.0) / 2.0) * jnp.log(0.01 + 3.0 * equiv))
            visc = (2.0 * ok) * (cons * power)
            bulk = (4.0 * ok) * trace
            sig = [
                jnp.where(ok > 0.0, visc * sxx + bulk, 0.0),
                jnp.where(ok > 0.0, visc * syy + bulk, 0.0),
                jnp.where(ok > 0.0, visc * szz + bulk, 0.0),
                jnp.where(ok > 0.0, visc * exy, 0.0),
                jnp.where(ok > 0.0, visc * eyz, 0.0),
                jnp.where(ok > 0.0, visc * ezx, 0.0),
            ]
            norm = (
                sig[0] * sig[0]
                + sig[1] * sig[1]
                + sig[2] * sig[2]
                + 2.0 * (sig[3] * sig[3] + sig[4] * sig[4] + sig[5] * sig[5])
            )
            made.append(sig + [norm])
        for q in range(7):
            a, b, c_ = made[0][q], made[1][q], made[2][q]
            for l, t in enumerate((a + pltpu.roll(c_, 1, 0), a + b, b + c_)):
                ey[q, pl.ds(aligned(n * W + 8 * l), 8), :] = t + pltpu.roll(t, 1, 1)
        return carry

    lax.fori_loop(0, 17, element_row, 0)

    half_z = jnp.where(first_z | last_z, 1.0, 0.5)
    col_half = [jnp.where((g == 0) | (g == total_y - 1), half_z, 0.5 * half_z) for g in cols]

    def node_row(i, carry):
        gi = slab * B + i
        row_half = jnp.where((gi == 0) | (gi == total_x - 1), 1.0, 0.5)
        for l in range(3):
            inverse = col_half[l] * row_half
            at = pl.ds(aligned(i * W + 8 * l), 8)
            at_next = pl.ds(aligned((i + 1) * W + 8 * l), 8)
            mean = [(ey[q, at, :] + ey[q, at_next, :]) * inverse for q in range(7)]
            norm = (
                mean[0] * mean[0]
                + mean[1] * mean[1]
                + mean[2] * mean[2]
                + 2.0 * (mean[3] * mean[3] + mean[4] * mean[4] + mean[5] * mean[5])
            )
            mean[6] = mean[6] - norm
            for q in range(7):
                st[54 + q * 16 + i, pl.ds(l, 8, stride=3), :] = mean[q]
        return carry

    lax.fori_loop(0, B, node_row, 0)

    def put(i, carry):
        for c in range(3):
            disp[c * 16 + i] = st[c * 18 + i + 1, 4:20, :]
        for q in range(6):
            rec[q * 16 + i] = st[54 + q * 16 + i, 4:20, :]
        ind[i] = st[54 + 96 + i, 4:20, :]
        return carry

    lax.fori_loop(0, B, put, 0, unroll=2)


def call(kernel, outs, args, scratch=(), aliases=None, cost=0):
    params = pltpu.CompilerParams(vmem_limit_bytes=48 * 1024 * 1024)
    whole = pl.BlockSpec(memory_space=pltpu.VMEM)
    return pl.pallas_call(
        kernel,
        out_shape=[jax.ShapeDtypeStruct(s, F32) for s in outs],
        in_specs=[whole] * len(args),
        out_specs=[whole] * len(outs),
        scratch_shapes=list(scratch),
        input_output_aliases=aliases or {},
        compiler_params=params,
        cost_estimate=pl.CostEstimate(flops=cost, bytes_accessed=2_000_000, transcendentals=0),
    )(*args)


def body(start_disp, load, shift, coarse, aggregate, consistency):
    start = start_disp.reshape(3 * B * B, Z)
    load2 = load.reshape(3 * B * B, Z)
    shift2 = shift.reshape(B * B, Z)
    cons2 = consistency.reshape(B * B, Z)
    coarse2 = coarse.reshape(3 * CB * CB, Z)
    n_plane = lax.axis_size("plane")
    n_slab = lax.axis_size("slab")
    forward = [(i, i + 1) for i in range(n_plane - 1)]
    backward = [(b, a) for a, b in forward]
    fwd, bwd = call(
        pack_kernel,
        [(PF_ROWS, Z), (PB_ROWS, Z)],
        [start, load2, shift2, cons2, coarse2, aggregate],
        cost=1_000_000,
    )
    low = lax.ppermute(fwd, "plane", forward)
    high = lax.ppermute(bwd, "plane", backward)
    own = call(
        own_kernel,
        [(48, W, Z), (48, W, Z), (16, W, Z), (16, W, Z), (24, 16, Z), (16, Z)],
        [
            start.reshape(48, B, Z),
            load2.reshape(48, B, Z),
            shift2.reshape(B, B, Z),
            cons2.reshape(B, B, Z),
            coarse2.reshape(24, CB, Z),
            fwd,
        ],
        cost=1_000_000,
    )
    flat = [a.reshape(-1, Z) for a in own]
    *ext, ex, on, off = call(
        join_kernel,
        [a.shape for a in flat] + [(6, 16, Z), (Q_ROWS, Z), (Q_ROWS, Z)],
        [low, high, *flat],
        aliases={2 + k: k for k in range(6)},
        cost=1_000_000,
    )
    pairs = [(i, i + 1) for i in range(1, n_slab - 1, 2)]
    pairs += [(b, a) for a, b in pairs]
    off = lax.ppermute(off, "slab", pairs)
    on = lax.all_gather(on, "slab", axis_index_groups=[[i, i + 1] for i in range(0, n_slab, 2)])
    field = (3, ROWS * W, Z)
    disp, rec, ind = call(
        smooth_kernel,
        [(48, B, Z), (96, B, Z), (B, B, Z)],
        [on, off, *ext, ex],
        scratch=[
            pltpu.VMEM(field, F32),
            pltpu.VMEM(field, F32),
            pltpu.VMEM((ROWS * W, Z), F32),
            pltpu.VMEM((ROWS * W, Z), F32),
            pltpu.VMEM((3, 256, Z), F32),
            pltpu.VMEM((6, 32, Z), F32),
            pltpu.VMEM((32, Z), F32),
            pltpu.VMEM(field, F32),
            pltpu.VMEM(field, F32),
            pltpu.VMEM(field, F32),
            pltpu.VMEM(field, F32),
            pltpu.VMEM((9, 18 * W, Z), F32),
            pltpu.VMEM((7, 17 * W, Z), F32),
            pltpu.VMEM((54 + 112, W, Z), F32),
        ],
        cost=50_000_000,
    )
    return disp.reshape(3, B, B, Z), rec.reshape(6, B, B, Z), ind


def solution(mesh):
    in_specs = (
        P(None, "slab", "plane", None),
        P(None, "slab", "plane", None),
        P("slab", "plane", None),
        P(None, "slab", "plane", None),
        P("slab", "plane"),
        P("slab", "plane", None),
    )
    out_specs = (
        P(None, "slab", "plane", None),
        P(None, "slab", "plane", None),
        P("slab", "plane", None),
    )
    return jax.shard_map(body, mesh=mesh, in_specs=in_specs, out_specs=out_specs, check_vma=False)
```

```python
import jax
import jax.numpy as jnp
from jax import lax
from jax.experimental import pallas as pl
from jax.experimental.pallas import tpu as pltpu
from jax.sharding import PartitionSpec as P

B = 16
CB = 8
Z = 128
W = 24
ROWS = 26

DEGREE = 4
THETA = 4.5
DELTA_C = 3.5
F32 = jnp.float32
FULL = 60 * 1024 * 1024

PS, PL_, PH, PK, PA, PC = 0, 240, 432, 496, 592, 608
PF_ROWS, PB_ROWS = 624, 608

QS, QL, QH, QC, QK, QX, QA = 0, 360, 648, 744, 768, 960, 1008
Q_ROWS = 1016
TS, TL, TH, TK, TC, TA = 0, 152, 248, 280, 376, 384
T_ROWS = 392


def place(col):
    index = col + 4
    return (index % 3) * 8 + index // 3


def fetch(sources, targets, sems):
    copies = [pltpu.make_async_copy(a, b, sems.at[k]) for k, (a, b) in enumerate(zip(sources, targets))]
    for copy in copies:
        copy.start()
    for copy in copies:
        copy.wait()


def pack_kernel(
    start_h, load_h, shift_h, cons_h, coarse_h, agg_h, fwd, bwd, code_o, start, load, shift, cons, coarse, agg, sems
):
    fetch(
        (start_h, load_h, shift_h, cons_h, coarse_h, agg_h), (start, load, shift, cons, coarse, agg), sems
    )
    slab = lax.axis_index("slab")
    plane = lax.axis_index("plane")
    coarse_cols = CB * lax.axis_size("plane")
    for c in range(3):
        for w in range(5):
            row = PS + 16 * (5 * c + w)
            fwd[row : row + 16, :] = start[pl.ds(256 * c + 11 + w, 16, stride=16), :]
            bwd[row : row + 16, :] = start[pl.ds(256 * c + w, 16, stride=16), :]
        for w in range(4):
            row = PL_ + 16 * (4 * c + w)
            fwd[row : row + 16, :] = load[pl.ds(256 * c + 12 + w, 16, stride=16), :]
            bwd[row : row + 16, :] = load[pl.ds(256 * c + w, 16, stride=16), :]
            row = PK + 8 * (4 * c + w)
            fwd[row : row + 8, :] = coarse[pl.ds(64 * c + 4 + w, 8, stride=8), :]
            bwd[row : row + 8, :] = coarse[pl.ds(64 * c + w, 8, stride=8), :]
    for w in range(4):
        row = PH + 16 * w
        fwd[row : row + 16, :] = shift[pl.ds(12 + w, 16, stride=16), :]
        bwd[row : row + 16, :] = shift[pl.ds(w, 16, stride=16), :]
    fwd[PC : PC + 16, :] = cons[pl.ds(15, 16, stride=16), :]
    value = agg[...]
    step_a = value // coarse_cols - (slab * CB + lax.broadcasted_iota(jnp.int32, (B, B), 0) // 2) + 1
    step_b = value % coarse_cols - (plane * CB + lax.broadcasted_iota(jnp.int32, (B, B), 1) // 2) + 1
    code = (1 + 16 * step_a + step_b).astype(F32)
    for out, row in ((fwd, PA), (bwd, PA), (code_o, 0)):
        out[row : row + 16, :] = jnp.zeros((16, Z), F32)
        out[row : row + 16, 0:B] = code


OWN = ((0, 2, 2, 5), (1, 1, 0, 6), (2, 1, 1, 5))


def top_rows(top, src, c, rows, width, size):
    return src[pl.ds(pl.multiple_of(c * rows * width + top * (rows * width - size), 8), size), :]


def own_kernel(
    start_h, load_h, shift_h, cons_h, coarse_h, code, es, el, eh, ec, ek, ea, off, start, load, shift, cons, coarse, sems
):
    fetch((start_h, load_h, shift_h, cons_h, coarse_h), (start, load, shift, cons, coarse), sems)

    for ci in range(3 * B):
        for l, s0, j0, n in OWN:
            at = ci * W + 8 * l + s0
            for src, dst in ((start, es), (load, el)) + (((shift, eh), (cons, ec)) if ci < B else ()):
                dst[at : at + n, :] = src[pl.ds(ci * B + j0, n, stride=3), :]
    for ca in range(3 * CB):
        ek[16 * ca + 4 : 16 * ca + 12, :] = coarse[8 * ca : 8 * ca + 8, :]
    ea[...] = pltpu.roll(code[...], 5, 1)
    top = lax.axis_index("slab") % 2
    whole_rows(top, off, es, el, eh, ec, ek)


def whole_rows(top, out, es, el, eh, ec, ek):
    for c in range(3):
        out[QS + 120 * c : QS + 120 * (c + 1), :] = top_rows(top, es, c, B, W, 120)
        out[QL + 96 * c : QL + 96 * (c + 1), :] = top_rows(top, el, c, B, W, 96)
        out[QK + 64 * c : QK + 64 * (c + 1), :] = top_rows(top, ek, c, CB, 16, 64)
    out[QH : QH + 96, :] = top_rows(top, eh, 0, B, W, 96)
    out[QC : QC + 24, :] = top_rows(top, ec, 0, B, W, 24)


def halo_columns(low, high):
    for side, src in ((0, low), (1, high)):
        for c in range(3):
            for w in range(5):
                yield src, PS + 16 * (5 * c + w), "start", c, w - 5 + 21 * side
            for w in range(4):
                yield src, PL_ + 16 * (4 * c + w), "load", c, w - 4 + 20 * side
                yield src, PK + 8 * (4 * c + w), "coarse", c, w + 12 * side
        for w in range(4):
            yield src, PH + 16 * w, "shift", 0, w - 4 + 20 * side
    yield low, PC, "cons", 0, -1


def join_kernel(low, high, es, el, eh, ec, ek, ea, code_o, on, off):
    lane = lax.broadcasted_iota(jnp.int32, (B, Z), 1)
    left = pltpu.roll(low[PA : PA + 16, :], Z - 11, 1)
    right = pltpu.roll(high[PA : PA + 16, :], 21, 1)
    code = jnp.where(lane < 5, left, jnp.where(lane < 21, ea[...], jnp.where(lane < 26, right, 0.0)))
    code_o[...] = code
    odd = lax.axis_index("slab") % 2
    whole_rows(1 - odd, on, es, el, eh, ec, ek)
    for on_top in (0, 1):

        @pl.when(odd == 1 - on_top)
        def _(on_top=on_top):
            on[QA : QA + 8, :] = code[8 * on_top : 8 * on_top + 8, :]
            off[TA : TA + 8, :] = code[8 * (1 - on_top) : 8 * (1 - on_top) + 8, :]
            at = {"start": TS, "load": TL, "shift": TH, "coarse": TK, "cons": TC}
            for src, row, kind, c, col in halo_columns(low, high):
                rows = CB if kind == "coarse" else B
                n = {"start": 5, "cons": 1}.get(kind, 4)
                first_on = row + (rows - n) * on_top
                first_off = row + (rows - n) * (1 - on_top)
                off[at[kind] : at[kind] + n, :] = src[first_off : first_off + n, :]
                at[kind] += n
                if kind == "coarse":
                    on[pl.ds(QK + 64 * c + col, n, stride=16), :] = src[first_on : first_on + n, :]
                elif kind == "start" and col in (-5, 20):
                    x = QX + 8 * (2 * c + (col > 0))
                    on[x : x + 8, :] = src[row + 8 * on_top : row + 8 * on_top + 8, :]
                else:
                    base = {"start": QS + 120 * c, "load": QL + 96 * c, "shift": QH, "cons": QC}[kind]
                    on[pl.ds(base + place(col), n, stride=W), :] = src[first_on : first_on + n, :]


def smooth_kernel(
    on, off, corner, low, high, es, el, eh, ec, ek, code_own,
    disp, rec, ind,
    fd, fr, fh, fc, fk, fx, fa, d0, d1, d2, d3, gx, ey, st,
):
    slab = lax.axis_index("slab")
    plane = lax.axis_index("plane")
    n_slab = lax.axis_size("slab")
    n_plane = lax.axis_size("plane")
    odd = slab % 2

    def aligned(index):
        return pl.multiple_of(index, 8)

    for c in range(3):
        fd[c, 5 * W : 21 * W, :] = es[384 * c : 384 * (c + 1), :]
        fr[c, 5 * W : 21 * W, :] = el[384 * c : 384 * (c + 1), :]
        fk[c, 64:192, :] = ek[128 * c : 128 * (c + 1), :]
    fh[5 * W : 21 * W, :] = eh[...]
    fc[5 * W : 21 * W, :] = ec[...]
    fa[8:24, :] = code_own[...]
    for src, below in ((on.at[1 - odd], odd), (off, 1 - odd)):
        above = 1 - below
        for c in range(3):
            fd[c, pl.ds(aligned(above * (21 * W)), 120), :] = src[QS + 120 * c : QS + 120 * (c + 1), :]
            fr[c, pl.ds(aligned(W + above * (20 * W)), 96), :] = src[QL + 96 * c : QL + 96 * (c + 1), :]
            fk[c, pl.ds(aligned(above * 192), 64), :] = src[QK + 64 * c : QK + 64 * (c + 1), :]
        fh[pl.ds(aligned(W + above * (20 * W)), 96), :] = src[QH : QH + 96, :]
        fc[pl.ds(aligned(4 * W + above * (17 * W)), 24), :] = src[QC : QC + 24, :]
    for q in range(6):
        fx[q, pl.ds(aligned((1 - odd) * 24), 8), :] = on[1 - odd, QX + 8 * q : QX + 8 * (q + 1), :]
    fa[pl.ds(aligned((1 - odd) * 24), 8), :] = on[1 - odd, QA : QA + 8, :]
    fa[pl.ds(aligned(odd * 24), 8), :] = corner[TA : TA + 8, :]

    def put_column(kind, c, col, row, n, value):
        if kind == "coarse":
            fk[c, pl.ds(16 * (row + 4) + col, n, stride=16), :] = value
        elif kind == "start" and col in (-5, 20):
            fx[2 * c + (col > 0), row + 8 : row + 8 + n, :] = value
        elif kind in ("start", "load"):
            {"start": fd, "load": fr}[kind][c, pl.ds((row + 5) * W + place(col), n, stride=W), :] = value
        else:
            {"shift": fh, "cons": fc}[kind][pl.ds((row + 5) * W + place(col), n, stride=W), :] = value

    for src, row, kind, c, col in halo_columns(low, high):
        n = CB if kind == "coarse" else B
        put_column(kind, c, col, 0, n, src[row : row + n, :])
    for off_below in (0, 1):

        @pl.when(odd == 1 - off_below)
        def _(off_below=off_below):
            at = {"start": TS, "load": TL, "shift": TH, "coarse": TK, "cons": TC}
            for _, _, kind, c, col in halo_columns(low, high):
                rows = CB if kind == "coarse" else B
                n = {"start": 5, "cons": 1}.get(kind, 4)
                put_column(kind, c, col, -n if off_below else rows, n, corner[at[kind] : at[kind] + n, :])
                at[kind] += n

    row = lax.broadcasted_iota(jnp.int32, (32, Z), 0)
    lane = lax.broadcasted_iota(jnp.int32, (32, Z), 1)
    code = fa[...]
    base = 16 * ((row - 8 + 16) // 2 - 8 + 3) + ((lane - 5 + 16) // 2 - 8 + 3) - 1
    inside = (row >= 3) & (row <= 28) & (lane < 26) & (code > 0.0)
    fa[...] = jnp.where(inside, code + base.astype(F32), -1.0)
    sub = lax.broadcasted_iota(jnp.int32, (W, Z), 0)
    lane_w = lax.broadcasted_iota(jnp.int32, (W, Z), 1)
    here = lane_w == 3 * (sub % 8) + sub // 8 + 1
    index = fa[...]
    spread = [jnp.where(here, jnp.broadcast_to(index[e + 3 : e + 4, :], (W, Z)), 0.0) for e in range(ROWS)]
    spread += [jnp.where(lane == 25 * q, index, 0.0) for q in range(2)]
    spread = jnp.concatenate(spread, axis=0).astype(jnp.bfloat16)
    columns = 2 * Z
    wide = jnp.dot(spread, jnp.ones((Z, columns), jnp.bfloat16), preferred_element_type=F32)
    count_nodes = ROWS * W + 64
    which = lax.broadcasted_iota(jnp.int32, (count_nodes, columns), 1).astype(F32)
    hot = (wide == which).astype(F32).astype(jnp.bfloat16)
    for c in range(3):
        table = fk[c]
        high = table.astype(jnp.bfloat16)
        rest = table - high.astype(F32)
        mid = rest.astype(jnp.bfloat16)
        low = (rest - mid.astype(F32)).astype(jnp.bfloat16)
        moved = (
            jnp.dot(hot, high, preferred_element_type=F32)
            + jnp.dot(hot, mid, preferred_element_type=F32)
            + jnp.dot(hot, low, preferred_element_type=F32)
        )
        fd[c] = fd[c] + moved[0 : ROWS * W]
        for q in range(2):
            fx[2 * c + q] = fx[2 * c + q] + moved[ROWS * W + 32 * q : ROWS * W + 32 * (q + 1)]

    place_s = lax.broadcasted_iota(jnp.int32, (8, Z), 0)
    place_z = lax.broadcasted_iota(jnp.int32, (8, Z), 1)
    first_z = place_z == 0
    last_z = place_z == Z - 1
    cols = [plane * B + 3 * place_s + l - 4 for l in range(3)]
    total_y = n_plane * B
    total_x = n_slab * B
    col_in = [((g >= 0) & (g < total_y)).astype(F32) for g in cols]

    def boxed(src, c, e, extra):
        v0, v1, v2 = (src[c, pl.ds(aligned(e * W + 8 * l), 8), :] for l in range(3))
        up = pltpu.roll(v2, 1, 0)
        down = pltpu.roll(v0, 7, 0)
        if extra is not None:
            up = jnp.where(place_s == 0, extra[2 * c, pl.ds(e + 3, 1), :], up)
            down = jnp.where(place_s == 7, extra[2 * c + 1, pl.ds(e + 3, 1), :], down)
        pair = v0 + v1
        out = []
        for t in (pair + up, pair + v2, v1 + v2 + down):
            out.append(
                t
                + jnp.where(first_z, 0.0, pltpu.roll(t, 1, 1))
                + jnp.where(last_z, 0.0, pltpu.roll(t, Z - 1, 1))
            )
        return out

    def stage(src, dst, extra, first, last, keep, gain):
        def sums(e):
            return [boxed(src, c, e, extra) for c in range(3)]

        def step(e, carry):
            before, mid = carry
            after = sums(e + 1)
            row_in = jnp.where((slab * B + e - 5 >= 0) & (slab * B + e - 5 < total_x), gain, 0.0)
            for l in range(3):
                at = pl.ds(aligned(e * W + 8 * l), 8)
                diagonal = 3.0 + fh[at, :]
                weight = col_in[l] * row_in
                for c in range(3):
                    here_v = src[c, at, :]
                    box = before[c][l] + mid[c][l] + after[c][l]
                    r = fr[c, at, :] - (diagonal * here_v - box * (1.0 / 3.0))
                    fr[c, at, :] = r
                    if keep is None:
                        dst[c, at, :] = weight * r
                    else:
                        dst[c, at, :] = keep * here_v + weight * r
            return mid, after

        lax.fori_loop(first, last + 1, step, (sums(first - 1), sums(first)), unroll=8)

    sigma = THETA / DELTA_C
    rho = 1.0 / sigma
    steps = []
    for _ in range(DEGREE - 1):
        rho_new = 1.0 / (2.0 * sigma - rho)
        steps.append((rho_new * rho, 2.0 * rho_new / DELTA_C))
        rho = rho_new
    stage(fd, d0, fx, 1, 24, None, 1.0 / THETA)
    stage(d0, d1, None, 2, 23, *steps[0])
    stage(d1, d2, None, 3, 22, *steps[1])
    stage(d2, d3, None, 4, 21, *steps[2])

    def gather_row(e, carry):
        for c in range(3):
            v = []
            for l in range(3):
                at = pl.ds(aligned(e * W + 8 * l), 8)
                u = fd[c, at, :] + d0[c, at, :] + d1[c, at, :] + d2[c, at, :] + d3[c, at, :]
                st[c * 18 + e - 4, pl.ds(l, 8, stride=3), :] = u
                v.append(u)
            nxt = [v[1], v[2], pltpu.roll(v[0], 7, 0)]
            for l in range(3):
                both = v[l] + nxt[l]
                diff = nxt[l] - v[l]
                both_z = pltpu.roll(both, Z - 1, 1)
                at = pl.ds(aligned((e - 4) * W + 8 * l), 8)
                gx[c, at, :] = both + both_z
                gx[3 + c, at, :] = diff + pltpu.roll(diff, Z - 1, 1)
                gx[6 + c, at, :] = both_z - both
        return carry

    lax.fori_loop(4, 22, gather_row, 0, unroll=6)

    col_ok = [((g >= 0) & (g <= total_y - 2) & (place_z <= Z - 2)).astype(F32) for g in cols]

    def element_row(n, carry):
        gi = slab * B + n - 1
        row_ok = jnp.where((gi >= 0) & (gi <= total_x - 2), 1.0, 0.0)
        made = []
        for l in range(3):
            at = pl.ds(aligned(n * W + 8 * l), 8)
            at_next = pl.ds(aligned((n + 1) * W + 8 * l), 8)
            grad = [[None] * 3 for _ in range(3)]
            for c in range(3):
                grad[c][0] = gx[c, at_next, :] - gx[c, at, :]
                grad[c][1] = gx[3 + c, at_next, :] + gx[3 + c, at, :]
                grad[c][2] = gx[6 + c, at_next, :] + gx[6 + c, at, :]
            exx = 0.25 * grad[0][0]
            eyy = 0.25 * grad[1][1]
            ezz = 0.25 * grad[2][2]
            exy = 0.125 * (grad[0][1] + grad[1][0])
            eyz = 0.125 * (grad[1][2] + grad[2][1])
            ezx = 0.125 * (grad[2][0] + grad[0][2])
            trace = exx + eyy + ezz
            third = trace * (1.0 / 3.0)
            sxx, syy, szz = exx - third, eyy - third, ezz - third
            equiv = (2.0 / 3.0) * (
                sxx * sxx + syy * syy + szz * szz + 2.0 * (exy * exy + eyz * eyz + ezx * ezx)
            )
            ok = col_ok[l] * row_ok
            cons = fc[pl.ds(aligned((n + 4) * W + 8 * l), 8), :]
            power = jnp.exp(((0.15 - 1.0) / 2.0) * jnp.log(0.01 + 3.0 * equiv))
            visc = (2.0 * ok) * (cons * power)
            bulk = (4.0 * ok) * trace
            sig = [
                jnp.where(ok > 0.0, visc * sxx + bulk, 0.0),
                jnp.where(ok > 0.0, visc * syy + bulk, 0.0),
                jnp.where(ok > 0.0, visc * szz + bulk, 0.0),
                jnp.where(ok > 0.0, visc * exy, 0.0),
                jnp.where(ok > 0.0, visc * eyz, 0.0),
                jnp.where(ok > 0.0, visc * ezx, 0.0),
            ]
            norm = (
                sig[0] * sig[0]
                + sig[1] * sig[1]
                + sig[2] * sig[2]
                + 2.0 * (sig[3] * sig[3] + sig[4] * sig[4] + sig[5] * sig[5])
            )
            made.append(sig + [norm])
        for q in range(7):
            a, b, c_ = made[0][q], made[1][q], made[2][q]
            for l, t in enumerate((a + pltpu.roll(c_, 1, 0), a + b, b + c_)):
                ey[q, pl.ds(aligned(n * W + 8 * l), 8), :] = t + pltpu.roll(t, 1, 1)
        return carry

    lax.fori_loop(0, 17, element_row, 0, unroll=4)

    half_z = jnp.where(first_z | last_z, 1.0, 0.5)
    col_half = [jnp.where((g == 0) | (g == total_y - 1), half_z, 0.5 * half_z) for g in cols]

    def node_row(i, carry):
        gi = slab * B + i
        row_half = jnp.where((gi == 0) | (gi == total_x - 1), 1.0, 0.5)
        for l in range(3):
            inverse = col_half[l] * row_half
            at = pl.ds(aligned(i * W + 8 * l), 8)
            at_next = pl.ds(aligned((i + 1) * W + 8 * l), 8)
            mean = [(ey[q, at, :] + ey[q, at_next, :]) * inverse for q in range(7)]
            norm = (
                mean[0] * mean[0]
                + mean[1] * mean[1]
                + mean[2] * mean[2]
                + 2.0 * (mean[3] * mean[3] + mean[4] * mean[4] + mean[5] * mean[5])
            )
            mean[6] = mean[6] - norm
            for q in range(7):
                st[54 + q * 16 + i, pl.ds(l, 8, stride=3), :] = mean[q]
        return carry

    lax.fori_loop(0, B, node_row, 0, unroll=4)

    def put(i, carry):
        for c in range(3):
            disp[c * 16 + i] = st[c * 18 + i + 1, 4:20, :]
        for q in range(6):
            rec[q * 16 + i] = st[54 + q * 16 + i, 4:20, :]
        ind[i] = st[54 + 96 + i, 4:20, :]
        return carry

    lax.fori_loop(0, B, put, 0, unroll=2)


def call(kernel, outs, args, scratch=(), in_hbm=0, cost=0, vmem=48 * 1024 * 1024):
    whole = pl.BlockSpec(memory_space=pltpu.VMEM)
    return pl.pallas_call(
        kernel,
        out_shape=[jax.ShapeDtypeStruct(s, F32) for s in outs],
        in_specs=[pl.BlockSpec(memory_space=pltpu.HBM)] * in_hbm + [whole] * (len(args) - in_hbm),
        out_specs=[whole] * len(outs),
        scratch_shapes=list(scratch),
        compiler_params=pltpu.CompilerParams(vmem_limit_bytes=vmem),
        cost_estimate=pl.CostEstimate(flops=cost, bytes_accessed=2_000_000, transcendentals=0),
    )(*args)


def landing(args):
    return [pltpu.VMEM(a.shape, a.dtype) for a in args] + [pltpu.SemaphoreType.DMA((len(args),))]


def body(start_disp, load, shift, coarse, aggregate, consistency):
    fields = [
        start_disp.reshape(3 * B * B, Z),
        load.reshape(3 * B * B, Z),
        shift.reshape(B * B, Z),
        consistency.reshape(B * B, Z),
        coarse.reshape(3 * CB * CB, Z),
    ]
    n_plane = lax.axis_size("plane")
    n_slab = lax.axis_size("slab")
    forward = [(i, i + 1) for i in range(n_plane - 1)]
    backward = [(b, a) for a, b in forward]
    swap = [(i, i + 1) for i in range(1, n_slab - 1, 2)]
    swap += [(b, a) for a, b in swap]

    args = [*fields, aggregate]
    fwd, bwd, code = call(
        pack_kernel,
        [(PF_ROWS, Z), (PB_ROWS, Z), (16, Z)],
        args,
        landing(args),
        in_hbm=6,
        cost=1_000_000,
        vmem=FULL,
    )
    low = lax.ppermute(fwd, "plane", forward)
    high = lax.ppermute(bwd, "plane", backward)
    *own, off = call(
        own_kernel,
        [(1152, Z), (1152, Z), (384, Z), (384, Z), (384, Z), (16, Z), (QX, Z)],
        [*fields, code],
        landing(fields),
        in_hbm=5,
        cost=1_000_000,
    )
    off = lax.ppermute(off, "slab", swap)
    code, on, corner = call(
        join_kernel, [(16, Z), (Q_ROWS, Z), (T_ROWS, Z)], [low, high, *own], cost=1_000_000
    )
    corner = lax.ppermute(corner, "slab", swap)
    on = lax.all_gather(on, "slab", axis_index_groups=[[i, i + 1] for i in range(0, n_slab, 2)])
    field = (3, ROWS * W, Z)
    shapes = [field, field, (ROWS * W, Z), (ROWS * W, Z), (3, 256, Z), (6, 32, Z), (32, Z)]
    shapes += [field] * 4 + [(9, 18 * W, Z), (7, 17 * W, Z), (54 + 112, W, Z)]
    disp, rec, ind = call(
        smooth_kernel,
        [(48, B, Z), (96, B, Z), (B, B, Z)],
        [on, off, corner, low, high, *own[:5], code],
        [pltpu.VMEM(shape, F32) for shape in shapes],
        cost=50_000_000,
    )
    return disp.reshape(3, B, B, Z), rec.reshape(6, B, B, Z), ind


def solution(mesh):
    in_specs = (
        P(None, "slab", "plane", None),
        P(None, "slab", "plane", None),
        P("slab", "plane", None),
        P(None, "slab", "plane", None),
        P("slab", "plane"),
        P("slab", "plane", None),
    )
    out_specs = (
        P(None, "slab", "plane", None),
        P(None, "slab", "plane", None),
        P("slab", "plane", None),
    )
    return jax.shard_map(body, mesh=mesh, in_specs=in_specs, out_specs=out_specs, check_vma=False)
```

```python
import jax
import jax.numpy as jnp
from jax import lax
from jax.experimental import pallas as pl
from jax.experimental.pallas import tpu as pltpu
from jax.sharding import PartitionSpec as P

B = 16
CB = 8
Z = 128
W = 24
ROWS = 26

DEGREE = 4
THETA = 4.5
DELTA_C = 3.5
F32 = jnp.float32
FULL = 60 * 1024 * 1024

PS, PL_, PH, PK, PA, PC = 0, 240, 432, 496, 592, 608
PF_ROWS, PB_ROWS = 624, 608

QS, QL, QH, QC, QK = 0, 360, 648, 744, 768
Q_ROWS = 960
TS, TL, TH, TK, TC, TA = 0, 152, 248, 280, 376, 384
T_ROWS = 392


def place(col):
    index = col + 4
    return (index % 3) * 8 + index // 3


def fetch(sources, targets, sems):
    copies = [pltpu.make_async_copy(a, b, sems.at[k]) for k, (a, b) in enumerate(zip(sources, targets))]
    for copy in copies:
        copy.start()
    return copies


def pack_kernel(
    start_h, load_h, shift_h, cons_h, coarse_h, agg_h, fwd_h, bwd_h, code_o,
    start, load, shift, cons, coarse, agg, sems, fwd, bwd, sems_out,
):
    slab = lax.axis_index("slab")
    plane = lax.axis_index("plane")
    coarse_cols = CB * lax.axis_size("plane")
    arrived = fetch(
        (agg_h, start_h, load_h, shift_h, coarse_h, cons_h), (agg, start, load, shift, coarse, cons), sems
    )
    sent = []

    def send(first, last):
        for scratch, out in ((fwd, fwd_h), (bwd, bwd_h)):
            size = min(last, scratch.shape[0]) - first
            if size > 0:
                at = pl.ds(first, size)
                copy = pltpu.make_async_copy(scratch.at[at], out.at[at], sems_out.at[len(sent)])
                copy.start()
                sent.append(copy)

    arrived[0].wait()
    value = agg[...]
    step_a = value // coarse_cols - (slab * CB + lax.broadcasted_iota(jnp.int32, (B, B), 0) // 2) + 1
    step_b = value % coarse_cols - (plane * CB + lax.broadcasted_iota(jnp.int32, (B, B), 1) // 2) + 1
    code = (1 + 16 * step_a + step_b).astype(F32)
    for out, row in ((fwd, PA), (bwd, PA), (code_o, 0)):
        out[row : row + 16, :] = jnp.zeros((16, Z), F32)
        out[row : row + 16, 0:B] = code
    arrived[1].wait()
    for c in range(3):
        for w in range(5):
            row = PS + 16 * (5 * c + w)
            fwd[row : row + 16, :] = start[pl.ds(256 * c + 11 + w, 16, stride=16), :]
            bwd[row : row + 16, :] = start[pl.ds(256 * c + w, 16, stride=16), :]
    send(PS, PL_)
    arrived[2].wait()
    for c in range(3):
        for w in range(4):
            row = PL_ + 16 * (4 * c + w)
            fwd[row : row + 16, :] = load[pl.ds(256 * c + 12 + w, 16, stride=16), :]
            bwd[row : row + 16, :] = load[pl.ds(256 * c + w, 16, stride=16), :]
    send(PL_, PH)
    for copy in arrived[3:]:
        copy.wait()
    for c in range(3):
        for w in range(4):
            row = PK + 8 * (4 * c + w)
            fwd[row : row + 8, :] = coarse[pl.ds(64 * c + 4 + w, 8, stride=8), :]
            bwd[row : row + 8, :] = coarse[pl.ds(64 * c + w, 8, stride=8), :]
    for w in range(4):
        row = PH + 16 * w
        fwd[row : row + 16, :] = shift[pl.ds(12 + w, 16, stride=16), :]
        bwd[row : row + 16, :] = shift[pl.ds(w, 16, stride=16), :]
    fwd[PC : PC + 16, :] = cons[pl.ds(15, 16, stride=16), :]
    send(PH, PF_ROWS)
    for copy in sent:
        copy.wait()


OWN = ((0, 2, 2, 5), (1, 1, 0, 6), (2, 1, 1, 5))


def top_rows(top, src, c, rows, width, size):
    return src[pl.ds(pl.multiple_of(c * rows * width + top * (rows * width - size), 8), size), :]


def own_kernel(
    start_h, load_h, shift_h, cons_h, coarse_h, code, es, el, eh, ec, ek, ea, on, off,
    start, load, shift, cons, coarse, sems,
):
    for copy in fetch((start_h, load_h, shift_h, cons_h, coarse_h), (start, load, shift, cons, coarse), sems):
        copy.wait()

    for ci in range(3 * B):
        for l, s0, j0, n in OWN:
            at = ci * W + 8 * l + s0
            for src, dst in ((start, es), (load, el)) + (((shift, eh), (cons, ec)) if ci < B else ()):
                dst[at : at + n, :] = src[pl.ds(ci * B + j0, n, stride=3), :]
    for ca in range(3 * CB):
        ek[16 * ca + 4 : 16 * ca + 12, :] = coarse[8 * ca : 8 * ca + 8, :]
    ea[...] = pltpu.roll(code[...], 5, 1)
    odd = lax.axis_index("slab") % 2
    for out, top in ((on, 1 - odd), (off, odd)):
        whole_rows(top, out, es, el, eh, ec, ek)


def whole_rows(top, out, es, el, eh, ec, ek):
    for c in range(3):
        out[QS + 120 * c : QS + 120 * (c + 1), :] = top_rows(top, es, c, B, W, 120)
        out[QL + 96 * c : QL + 96 * (c + 1), :] = top_rows(top, el, c, B, W, 96)
        out[QK + 64 * c : QK + 64 * (c + 1), :] = top_rows(top, ek, c, CB, 16, 64)
    out[QH : QH + 96, :] = top_rows(top, eh, 0, B, W, 96)
    out[QC : QC + 24, :] = top_rows(top, ec, 0, B, W, 24)


def halo_columns(low, high):
    for side, src in ((0, low), (1, high)):
        for c in range(3):
            for w in range(5):
                yield src, PS + 16 * (5 * c + w), "start", c, w - 5 + 21 * side
            for w in range(4):
                yield src, PL_ + 16 * (4 * c + w), "load", c, w - 4 + 20 * side
                yield src, PK + 8 * (4 * c + w), "coarse", c, w + 12 * side
        for w in range(4):
            yield src, PH + 16 * w, "shift", 0, w - 4 + 20 * side
    yield low, PC, "cons", 0, -1


def corner_columns(low, high):
    at = {"start": TS, "load": TL, "shift": TH, "coarse": TK, "cons": TC}
    for src, row, kind, c, col in halo_columns(low, high):
        n = {"start": 5, "cons": 1}.get(kind, 4)
        yield src, row, kind, c, col, at[kind], n
        at[kind] += n


def join_kernel(low, high, ea, code_o, on, off):
    lane = lax.broadcasted_iota(jnp.int32, (B, Z), 1)
    left = pltpu.roll(low[PA : PA + 16, :], Z - 11, 1)
    right = pltpu.roll(high[PA : PA + 16, :], 21, 1)
    code = jnp.where(lane < 5, left, jnp.where(lane < 21, ea[...], jnp.where(lane < 26, right, 0.0)))
    code_o[...] = code
    odd = lax.axis_index("slab") % 2
    for on_top in (0, 1):

        @pl.when(odd == 1 - on_top)
        def _(on_top=on_top):
            for out, top in ((on, on_top), (off, 1 - on_top)):
                out[TA : TA + 8, :] = code[8 * top : 8 * top + 8, :]
                for src, row, kind, _, _, at, n in corner_columns(low, high):
                    first = row + ((CB if kind == "coarse" else B) - n) * top
                    out[at : at + n, :] = src[first : first + n, :]


def smooth_kernel(
    on, off, on_corner, off_corner, low, high, es, el, eh, ec, ek, code_own,
    disp, rec, ind,
    fd, fr, fh, fc, fk, fx, fa, d0, d1, d2, d3, gx, ey, st,
):
    slab = lax.axis_index("slab")
    plane = lax.axis_index("plane")
    n_slab = lax.axis_size("slab")
    n_plane = lax.axis_size("plane")
    odd = slab % 2

    def aligned(index):
        return pl.multiple_of(index, 8)

    for c in range(3):
        fd[c, 5 * W : 21 * W, :] = es[384 * c : 384 * (c + 1), :]
        fr[c, 5 * W : 21 * W, :] = el[384 * c : 384 * (c + 1), :]
        fk[c, 64:192, :] = ek[128 * c : 128 * (c + 1), :]
    fh[5 * W : 21 * W, :] = eh[...]
    fc[5 * W : 21 * W, :] = ec[...]
    fa[8:24, :] = code_own[...]
    for src, below in ((on.at[1 - odd], odd), (off, 1 - odd)):
        above = 1 - below
        for c in range(3):
            fd[c, pl.ds(aligned(above * (21 * W)), 120), :] = src[QS + 120 * c : QS + 120 * (c + 1), :]
            fr[c, pl.ds(aligned(W + above * (20 * W)), 96), :] = src[QL + 96 * c : QL + 96 * (c + 1), :]
            fk[c, pl.ds(aligned(above * 192), 64), :] = src[QK + 64 * c : QK + 64 * (c + 1), :]
        fh[pl.ds(aligned(W + above * (20 * W)), 96), :] = src[QH : QH + 96, :]
        fc[pl.ds(aligned(4 * W + above * (17 * W)), 24), :] = src[QC : QC + 24, :]
    fa[pl.ds(aligned((1 - odd) * 24), 8), :] = on_corner[1 - odd, TA : TA + 8, :]
    fa[pl.ds(aligned(odd * 24), 8), :] = off_corner[TA : TA + 8, :]

    def put_column(kind, c, col, row, n, value):
        if kind == "coarse":
            fk[c, pl.ds(16 * (row + 4) + col, n, stride=16), :] = value
        elif kind == "start" and col in (-5, 20):
            fx[2 * c + (col > 0), row + 8 : row + 8 + n, :] = value
        elif kind in ("start", "load"):
            {"start": fd, "load": fr}[kind][c, pl.ds((row + 5) * W + place(col), n, stride=W), :] = value
        else:
            {"shift": fh, "cons": fc}[kind][pl.ds((row + 5) * W + place(col), n, stride=W), :] = value

    for src, row, kind, c, col in halo_columns(low, high):
        n = CB if kind == "coarse" else B
        put_column(kind, c, col, 0, n, src[row : row + n, :])
    for off_below in (0, 1):

        @pl.when(odd == 1 - off_below)
        def _(off_below=off_below):
            for corner, below in ((on_corner.at[off_below], 1 - off_below), (off_corner, off_below)):
                for _, _, kind, c, col, at, n in corner_columns(low, high):
                    first = -n if below else (CB if kind == "coarse" else B)
                    put_column(kind, c, col, first, n, corner[at : at + n, :])

    row = lax.broadcasted_iota(jnp.int32, (32, Z), 0)
    lane = lax.broadcasted_iota(jnp.int32, (32, Z), 1)
    code = fa[...]
    base = 16 * ((row - 8 + 16) // 2 - 8 + 3) + ((lane - 5 + 16) // 2 - 8 + 3) - 1
    inside = (row >= 3) & (row <= 28) & (lane < 26) & (code > 0.0)
    fa[...] = jnp.where(inside, code + base.astype(F32), -1.0)
    sub = lax.broadcasted_iota(jnp.int32, (W, Z), 0)
    lane_w = lax.broadcasted_iota(jnp.int32, (W, Z), 1)
    here = lane_w == 3 * (sub % 8) + sub // 8 + 1
    index = fa[...]
    spread = [jnp.where(here, jnp.broadcast_to(index[e + 3 : e + 4, :], (W, Z)), 0.0) for e in range(ROWS)]
    spread += [jnp.where(lane == 25 * q, index, 0.0) for q in range(2)]
    spread = jnp.concatenate(spread, axis=0).astype(jnp.bfloat16)
    columns = 2 * Z
    wide = jnp.dot(spread, jnp.ones((Z, columns), jnp.bfloat16), preferred_element_type=F32)
    count_nodes = ROWS * W + 64
    which = lax.broadcasted_iota(jnp.int32, (count_nodes, columns), 1).astype(F32)
    hot = (wide == which).astype(F32).astype(jnp.bfloat16)
    for c in range(3):
        table = fk[c]
        high = table.astype(jnp.bfloat16)
        rest = table - high.astype(F32)
        mid = rest.astype(jnp.bfloat16)
        low = (rest - mid.astype(F32)).astype(jnp.bfloat16)
        moved = (
            jnp.dot(hot, high, preferred_element_type=F32)
            + jnp.dot(hot, mid, preferred_element_type=F32)
            + jnp.dot(hot, low, preferred_element_type=F32)
        )
        fd[c] = fd[c] + moved[0 : ROWS * W]
        for q in range(2):
            fx[2 * c + q] = fx[2 * c + q] + moved[ROWS * W + 32 * q : ROWS * W + 32 * (q + 1)]

    place_s = lax.broadcasted_iota(jnp.int32, (8, Z), 0)
    place_z = lax.broadcasted_iota(jnp.int32, (8, Z), 1)
    first_z = place_z == 0
    last_z = place_z == Z - 1
    cols = [plane * B + 3 * place_s + l - 4 for l in range(3)]
    total_y = n_plane * B
    total_x = n_slab * B
    col_in = [((g >= 0) & (g < total_y)).astype(F32) for g in cols]

    def boxed(src, c, e, extra):
        v0, v1, v2 = (src[c, pl.ds(aligned(e * W + 8 * l), 8), :] for l in range(3))
        up = pltpu.roll(v2, 1, 0)
        down = pltpu.roll(v0, 7, 0)
        if extra is not None:
            up = jnp.where(place_s == 0, extra[2 * c, pl.ds(e + 3, 1), :], up)
            down = jnp.where(place_s == 7, extra[2 * c + 1, pl.ds(e + 3, 1), :], down)
        pair = v0 + v1
        out = []
        for t in (pair + up, pair + v2, v1 + v2 + down):
            out.append(
                t
                + jnp.where(first_z, 0.0, pltpu.roll(t, 1, 1))
                + jnp.where(last_z, 0.0, pltpu.roll(t, Z - 1, 1))
            )
        return out

    def stage(src, dst, extra, first, last, keep, gain):
        def sums(e):
            return [boxed(src, c, e, extra) for c in range(3)]

        def step(e, carry):
            before, mid = carry
            after = sums(e + 1)
            row_in = jnp.where((slab * B + e - 5 >= 0) & (slab * B + e - 5 < total_x), gain, 0.0)
            for l in range(3):
                at = pl.ds(aligned(e * W + 8 * l), 8)
                diagonal = 3.0 + fh[at, :]
                weight = col_in[l] * row_in
                for c in range(3):
                    here_v = src[c, at, :]
                    box = before[c][l] + mid[c][l] + after[c][l]
                    r = fr[c, at, :] - (diagonal * here_v - box * (1.0 / 3.0))
                    fr[c, at, :] = r
                    if keep is None:
                        dst[c, at, :] = weight * r
                    else:
                        dst[c, at, :] = keep * here_v + weight * r
            return mid, after

        lax.fori_loop(first, last + 1, step, (sums(first - 1), sums(first)), unroll=8)

    sigma = THETA / DELTA_C
    rho = 1.0 / sigma
    steps = []
    for _ in range(DEGREE - 1):
        rho_new = 1.0 / (2.0 * sigma - rho)
        steps.append((rho_new * rho, 2.0 * rho_new / DELTA_C))
        rho = rho_new
    stage(fd, d0, fx, 1, 24, None, 1.0 / THETA)
    stage(d0, d1, None, 2, 23, *steps[0])
    stage(d1, d2, None, 3, 22, *steps[1])
    stage(d2, d3, None, 4, 21, *steps[2])

    def gather_row(e, carry):
        for c in range(3):
            v = []
            for l in range(3):
                at = pl.ds(aligned(e * W + 8 * l), 8)
                u = fd[c, at, :] + d0[c, at, :] + d1[c, at, :] + d2[c, at, :] + d3[c, at, :]
                st[c * 18 + e - 4, pl.ds(l, 8, stride=3), :] = u
                v.append(u)
            nxt = [v[1], v[2], pltpu.roll(v[0], 7, 0)]
            for l in range(3):
                both = v[l] + nxt[l]
                diff = nxt[l] - v[l]
                both_z = pltpu.roll(both, Z - 1, 1)
                at = pl.ds(aligned((e - 4) * W + 8 * l), 8)
                gx[c, at, :] = both + both_z
                gx[3 + c, at, :] = diff + pltpu.roll(diff, Z - 1, 1)
                gx[6 + c, at, :] = both_z - both
        return carry

    lax.fori_loop(4, 22, gather_row, 0, unroll=6)

    col_ok = [((g >= 0) & (g <= total_y - 2) & (place_z <= Z - 2)).astype(F32) for g in cols]

    def element_row(n, carry):
        gi = slab * B + n - 1
        row_ok = jnp.where((gi >= 0) & (gi <= total_x - 2), 1.0, 0.0)
        made = []
        for l in range(3):
            at = pl.ds(aligned(n * W + 8 * l), 8)
            at_next = pl.ds(aligned((n + 1) * W + 8 * l), 8)
            grad = [[None] * 3 for _ in range(3)]
            for c in range(3):
                grad[c][0] = gx[c, at_next, :] - gx[c, at, :]
                grad[c][1] = gx[3 + c, at_next, :] + gx[3 + c, at, :]
                grad[c][2] = gx[6 + c, at_next, :] + gx[6 + c, at, :]
            exx = 0.25 * grad[0][0]
            eyy = 0.25 * grad[1][1]
            ezz = 0.25 * grad[2][2]
            exy = 0.125 * (grad[0][1] + grad[1][0])
            eyz = 0.125 * (grad[1][2] + grad[2][1])
            ezx = 0.125 * (grad[2][0] + grad[0][2])
            trace = exx + eyy + ezz
            third = trace * (1.0 / 3.0)
            sxx, syy, szz = exx - third, eyy - third, ezz - third
            equiv = (2.0 / 3.0) * (
                sxx * sxx + syy * syy + szz * szz + 2.0 * (exy * exy + eyz * eyz + ezx * ezx)
            )
            ok = col_ok[l] * row_ok
            cons = fc[pl.ds(aligned((n + 4) * W + 8 * l), 8), :]
            power = jnp.exp(((0.15 - 1.0) / 2.0) * jnp.log(0.01 + 3.0 * equiv))
            visc = (2.0 * ok) * (cons * power)
            bulk = (4.0 * ok) * trace
            sig = [
                jnp.where(ok > 0.0, visc * sxx + bulk, 0.0),
                jnp.where(ok > 0.0, visc * syy + bulk, 0.0),
                jnp.where(ok > 0.0, visc * szz + bulk, 0.0),
                jnp.where(ok > 0.0, visc * exy, 0.0),
                jnp.where(ok > 0.0, visc * eyz, 0.0),
                jnp.where(ok > 0.0, visc * ezx, 0.0),
            ]
            norm = (
                sig[0] * sig[0]
                + sig[1] * sig[1]
                + sig[2] * sig[2]
                + 2.0 * (sig[3] * sig[3] + sig[4] * sig[4] + sig[5] * sig[5])
            )
            made.append(sig + [norm])
        for q in range(7):
            a, b, c_ = made[0][q], made[1][q], made[2][q]
            for l, t in enumerate((a + pltpu.roll(c_, 1, 0), a + b, b + c_)):
                ey[q, pl.ds(aligned(n * W + 8 * l), 8), :] = t + pltpu.roll(t, 1, 1)
        return carry

    lax.fori_loop(0, 17, element_row, 0, unroll=4)

    half_z = jnp.where(first_z | last_z, 1.0, 0.5)
    col_half = [jnp.where((g == 0) | (g == total_y - 1), half_z, 0.5 * half_z) for g in cols]

    def node_row(i, carry):
        gi = slab * B + i
        row_half = jnp.where((gi == 0) | (gi == total_x - 1), 1.0, 0.5)
        for l in range(3):
            inverse = col_half[l] * row_half
            at = pl.ds(aligned(i * W + 8 * l), 8)
            at_next = pl.ds(aligned((i + 1) * W + 8 * l), 8)
            mean = [(ey[q, at, :] + ey[q, at_next, :]) * inverse for q in range(7)]
            norm = (
                mean[0] * mean[0]
                + mean[1] * mean[1]
                + mean[2] * mean[2]
                + 2.0 * (mean[3] * mean[3] + mean[4] * mean[4] + mean[5] * mean[5])
            )
            mean[6] = mean[6] - norm
            for q in range(7):
                st[54 + q * 16 + i, pl.ds(l, 8, stride=3), :] = mean[q]
        return carry

    lax.fori_loop(0, B, node_row, 0, unroll=4)

    def put(i, carry):
        for c in range(3):
            disp[c * 16 + i] = st[c * 18 + i + 1, 4:20, :]
        for q in range(6):
            rec[q * 16 + i] = st[54 + q * 16 + i, 4:20, :]
        ind[i] = st[54 + 96 + i, 4:20, :]
        return carry

    lax.fori_loop(0, B, put, 0, unroll=2)


def call(kernel, outs, args, scratch=(), in_hbm=0, out_hbm=0, cost=0, vmem=48 * 1024 * 1024):
    hbm = pl.BlockSpec(memory_space=pltpu.HBM)
    whole = pl.BlockSpec(memory_space=pltpu.VMEM)
    return pl.pallas_call(
        kernel,
        out_shape=[jax.ShapeDtypeStruct(s, F32) for s in outs],
        in_specs=[hbm] * in_hbm + [whole] * (len(args) - in_hbm),
        out_specs=[hbm] * out_hbm + [whole] * (len(outs) - out_hbm),
        scratch_shapes=list(scratch),
        compiler_params=pltpu.CompilerParams(vmem_limit_bytes=vmem),
        cost_estimate=pl.CostEstimate(flops=cost, bytes_accessed=2_000_000, transcendentals=0),
    )(*args)


def landing(args):
    return [pltpu.VMEM(a.shape, a.dtype) for a in args] + [pltpu.SemaphoreType.DMA((len(args),))]


def body(start_disp, load, shift, coarse, aggregate, consistency):
    fields = [
        start_disp.reshape(3 * B * B, Z),
        load.reshape(3 * B * B, Z),
        shift.reshape(B * B, Z),
        consistency.reshape(B * B, Z),
        coarse.reshape(3 * CB * CB, Z),
    ]
    n_plane = lax.axis_size("plane")
    n_slab = lax.axis_size("slab")
    forward = [(i, i + 1) for i in range(n_plane - 1)]
    backward = [(b, a) for a, b in forward]
    swap = [(i, i + 1) for i in range(1, n_slab - 1, 2)]
    swap += [(b, a) for a, b in swap]

    args = [*fields, aggregate]
    fwd, bwd, code = call(
        pack_kernel,
        [(PF_ROWS, Z), (PB_ROWS, Z), (16, Z)],
        args,
        [
            *landing(args),
            pltpu.VMEM((PF_ROWS, Z), F32),
            pltpu.VMEM((PB_ROWS, Z), F32),
            pltpu.SemaphoreType.DMA((6,)),
        ],
        in_hbm=6,
        out_hbm=2,
        cost=1_000_000,
        vmem=FULL,
    )
    low = lax.ppermute(fwd, "plane", forward)
    high = lax.ppermute(bwd, "plane", backward)
    *own, on, off = call(
        own_kernel,
        [(1152, Z), (1152, Z), (384, Z), (384, Z), (384, Z), (16, Z), (Q_ROWS, Z), (Q_ROWS, Z)],
        [*fields, code],
        landing(fields),
        in_hbm=5,
        cost=1_000_000,
    )
    cores = [[i, i + 1] for i in range(0, n_slab, 2)]
    off = lax.ppermute(off, "slab", swap)
    on = lax.all_gather(on, "slab", axis_index_groups=cores)
    low, high, on = lax.optimization_barrier((low, high, on))
    code, on_corner, off_corner = call(
        join_kernel, [(16, Z), (T_ROWS, Z), (T_ROWS, Z)], [low, high, own[5]], cost=1_000_000
    )
    off_corner = lax.ppermute(off_corner, "slab", swap)
    on_corner = lax.all_gather(on_corner, "slab", axis_index_groups=cores)
    field = (3, ROWS * W, Z)
    shapes = [field, field, (ROWS * W, Z), (ROWS * W, Z), (3, 256, Z), (6, 32, Z), (32, Z)]
    shapes += [field] * 4 + [(9, 18 * W, Z), (7, 17 * W, Z), (54 + 112, W, Z)]
    disp, rec, ind = call(
        smooth_kernel,
        [(48, B, Z), (96, B, Z), (B, B, Z)],
        [on, off, on_corner, off_corner, low, high, *own[:5], code],
        [pltpu.VMEM(shape, F32) for shape in shapes],
        cost=50_000_000,
    )
    return disp.reshape(3, B, B, Z), rec.reshape(6, B, B, Z), ind


def solution(mesh):
    in_specs = (
        P(None, "slab", "plane", None),
        P(None, "slab", "plane", None),
        P("slab", "plane", None),
        P(None, "slab", "plane", None),
        P("slab", "plane"),
        P("slab", "plane", None),
    )
    out_specs = (
        P(None, "slab", "plane", None),
        P(None, "slab", "plane", None),
        P("slab", "plane", None),
    )
    return jax.shard_map(body, mesh=mesh, in_specs=in_specs, out_specs=out_specs, check_vma=False)
```

```python
import jax
import jax.numpy as jnp
from jax import lax
from jax.experimental import pallas as pl
from jax.experimental.pallas import tpu as pltpu
from jax.sharding import PartitionSpec as P

B = 16
CB = 8
Z = 128
W = 24
ROWS = 26

DEGREE = 4
THETA = 4.5
DELTA_C = 3.5
F32 = jnp.float32
FULL = 60 * 1024 * 1024

PS, PL_, PH, PK, PA, PC = 0, 240, 432, 496, 592, 608
P_ROWS = 624

QS, QL, QH, QC, QK = 0, 360, 648, 744, 768
Q_ROWS = 960
TS, TL, TH, TK, TC, TA = 0, 152, 248, 280, 376, 384
T_ROWS = 392


def place(col):
    index = col + 4
    return (index % 3) * 8 + index // 3


def fetch(sources, targets, sems):
    copies = [pltpu.make_async_copy(a, b, sems.at[k]) for k, (a, b) in enumerate(zip(sources, targets))]
    for copy in copies:
        copy.start()
    for copy in copies:
        copy.wait()


def by_side(first, second, run):
    odd = lax.axis_index("plane") % 2
    for side in (0, 1):

        @pl.when(odd == side)
        def _(side=side):
            run(*((first, second) if side else (second, first)))


def pack_kernel(
    start_h, load_h, shift_h, cons_h, coarse_h, agg_h, first, second, code_o,
    start, load, shift, cons, coarse, agg, sems,
):
    slab = lax.axis_index("slab")
    plane = lax.axis_index("plane")
    coarse_cols = CB * lax.axis_size("plane")
    fetch(
        (start_h, load_h, shift_h, cons_h, coarse_h, agg_h), (start, load, shift, cons, coarse, agg), sems
    )
    value = agg[...]
    step_a = value // coarse_cols - (slab * CB + lax.broadcasted_iota(jnp.int32, (B, B), 0) // 2) + 1
    step_b = value % coarse_cols - (plane * CB + lax.broadcasted_iota(jnp.int32, (B, B), 1) // 2) + 1
    code = (1 + 16 * step_a + step_b).astype(F32)
    for out, row in ((first, PA), (second, PA), (code_o, 0)):
        out[row : row + 16, :] = jnp.zeros((16, Z), F32)
        out[row : row + 16, 0:B] = code

    def pack(bwd, fwd):
        for c in range(3):
            for w in range(5):
                row = PS + 16 * (5 * c + w)
                fwd[row : row + 16, :] = start[pl.ds(256 * c + 11 + w, 16, stride=16), :]
                bwd[row : row + 16, :] = start[pl.ds(256 * c + w, 16, stride=16), :]
            for w in range(4):
                row = PL_ + 16 * (4 * c + w)
                fwd[row : row + 16, :] = load[pl.ds(256 * c + 12 + w, 16, stride=16), :]
                bwd[row : row + 16, :] = load[pl.ds(256 * c + w, 16, stride=16), :]
                row = PK + 8 * (4 * c + w)
                fwd[row : row + 8, :] = coarse[pl.ds(64 * c + 4 + w, 8, stride=8), :]
                bwd[row : row + 8, :] = coarse[pl.ds(64 * c + w, 8, stride=8), :]
        for w in range(4):
            row = PH + 16 * w
            fwd[row : row + 16, :] = shift[pl.ds(12 + w, 16, stride=16), :]
            bwd[row : row + 16, :] = shift[pl.ds(w, 16, stride=16), :]
        fwd[PC : PC + 16, :] = cons[pl.ds(15, 16, stride=16), :]
        bwd[PC : PC + 16, :] = cons[pl.ds(0, 16, stride=16), :]

    by_side(first, second, pack)


OWN = ((0, 2, 2, 5), (1, 1, 0, 6), (2, 1, 1, 5))


def top_rows(top, src, c, rows, width, size):
    return src[pl.ds(pl.multiple_of(c * rows * width + top * (rows * width - size), 8), size), :]


def own_kernel(
    start_h, load_h, shift_h, cons_h, coarse_h, code, es, el, eh, ec, ek, ea, on, off,
    start, load, shift, cons, coarse, sems,
):
    fetch((start_h, load_h, shift_h, cons_h, coarse_h), (start, load, shift, cons, coarse), sems)

    for ci in range(3 * B):
        for l, s0, j0, n in OWN:
            at = ci * W + 8 * l + s0
            for src, dst in ((start, es), (load, el)) + (((shift, eh), (cons, ec)) if ci < B else ()):
                dst[at : at + n, :] = src[pl.ds(ci * B + j0, n, stride=3), :]
    for ca in range(3 * CB):
        ek[16 * ca + 4 : 16 * ca + 12, :] = coarse[8 * ca : 8 * ca + 8, :]
    ea[...] = pltpu.roll(code[...], 5, 1)
    odd = lax.axis_index("slab") % 2
    for out, top in ((on, 1 - odd), (off, odd)):
        whole_rows(top, out, es, el, eh, ec, ek)


def whole_rows(top, out, es, el, eh, ec, ek):
    for c in range(3):
        out[QS + 120 * c : QS + 120 * (c + 1), :] = top_rows(top, es, c, B, W, 120)
        out[QL + 96 * c : QL + 96 * (c + 1), :] = top_rows(top, el, c, B, W, 96)
        out[QK + 64 * c : QK + 64 * (c + 1), :] = top_rows(top, ek, c, CB, 16, 64)
    out[QH : QH + 96, :] = top_rows(top, eh, 0, B, W, 96)
    out[QC : QC + 24, :] = top_rows(top, ec, 0, B, W, 24)


def halo_columns(low, high):
    for side, src in ((0, low), (1, high)):
        for c in range(3):
            for w in range(5):
                yield src, PS + 16 * (5 * c + w), "start", c, w - 5 + 21 * side
            for w in range(4):
                yield src, PL_ + 16 * (4 * c + w), "load", c, w - 4 + 20 * side
                yield src, PK + 8 * (4 * c + w), "coarse", c, w + 12 * side
        for w in range(4):
            yield src, PH + 16 * w, "shift", 0, w - 4 + 20 * side
    yield low, PC, "cons", 0, -1


def corner_columns(low, high):
    at = {"start": TS, "load": TL, "shift": TH, "coarse": TK, "cons": TC}
    for src, row, kind, c, col in halo_columns(low, high):
        n = {"start": 5, "cons": 1}.get(kind, 4)
        yield src, row, kind, c, col, at[kind], n
        at[kind] += n


def join_kernel(first, second, ea, code_o, on, off):
    odd = lax.axis_index("slab") % 2

    def join(low, high):
        lane = lax.broadcasted_iota(jnp.int32, (B, Z), 1)
        left = pltpu.roll(low[PA : PA + 16, :], Z - 11, 1)
        right = pltpu.roll(high[PA : PA + 16, :], 21, 1)
        code = jnp.where(lane < 5, left, jnp.where(lane < 21, ea[...], jnp.where(lane < 26, right, 0.0)))
        code_o[...] = code
        for on_top in (0, 1):

            @pl.when(odd == 1 - on_top)
            def _(on_top=on_top):
                for out, top in ((on, on_top), (off, 1 - on_top)):
                    out[TA : TA + 8, :] = code[8 * top : 8 * top + 8, :]
                    for src, row, kind, _, _, at, n in corner_columns(low, high):
                        begin = row + ((CB if kind == "coarse" else B) - n) * top
                        out[at : at + n, :] = src[begin : begin + n, :]

    by_side(first, second, join)


def smooth_kernel(
    on, off, on_corner, off_corner, swap_first, swap_second, es, el, eh, ec, ek, code_own,
    disp, rec, ind,
    fd, fr, fh, fc, fk, fx, fa, d0, d1, d2, d3, gx, ey, st,
):
    slab = lax.axis_index("slab")
    plane = lax.axis_index("plane")
    n_slab = lax.axis_size("slab")
    n_plane = lax.axis_size("plane")
    odd = slab % 2

    def aligned(index):
        return pl.multiple_of(index, 8)

    for c in range(3):
        fd[c, 5 * W : 21 * W, :] = es[384 * c : 384 * (c + 1), :]
        fr[c, 5 * W : 21 * W, :] = el[384 * c : 384 * (c + 1), :]
        fk[c, 64:192, :] = ek[128 * c : 128 * (c + 1), :]
    fh[5 * W : 21 * W, :] = eh[...]
    fc[5 * W : 21 * W, :] = ec[...]
    fa[8:24, :] = code_own[...]
    for src, below in ((on.at[1 - odd], odd), (off, 1 - odd)):
        above = 1 - below
        for c in range(3):
            fd[c, pl.ds(aligned(above * (21 * W)), 120), :] = src[QS + 120 * c : QS + 120 * (c + 1), :]
            fr[c, pl.ds(aligned(W + above * (20 * W)), 96), :] = src[QL + 96 * c : QL + 96 * (c + 1), :]
            fk[c, pl.ds(aligned(above * 192), 64), :] = src[QK + 64 * c : QK + 64 * (c + 1), :]
        fh[pl.ds(aligned(W + above * (20 * W)), 96), :] = src[QH : QH + 96, :]
        fc[pl.ds(aligned(4 * W + above * (17 * W)), 24), :] = src[QC : QC + 24, :]
    fa[pl.ds(aligned((1 - odd) * 24), 8), :] = on_corner[1 - odd, TA : TA + 8, :]
    fa[pl.ds(aligned(odd * 24), 8), :] = off_corner[TA : TA + 8, :]

    def put_column(kind, c, col, row, n, value):
        if kind == "coarse":
            fk[c, pl.ds(16 * (row + 4) + col, n, stride=16), :] = value
        elif kind == "start" and col in (-5, 20):
            fx[2 * c + (col > 0), row + 8 : row + 8 + n, :] = value
        elif kind in ("start", "load"):
            {"start": fd, "load": fr}[kind][c, pl.ds((row + 5) * W + place(col), n, stride=W), :] = value
        else:
            {"shift": fh, "cons": fc}[kind][pl.ds((row + 5) * W + place(col), n, stride=W), :] = value

    def put_columns(low, high):
        for src, row, kind, c, col in halo_columns(low, high):
            n = CB if kind == "coarse" else B
            put_column(kind, c, col, 0, n, src[row : row + n, :])

    by_side(swap_first, swap_second, put_columns)
    for off_below in (0, 1):

        @pl.when(odd == 1 - off_below)
        def _(off_below=off_below):
            for corner, below in ((on_corner.at[off_below], 1 - off_below), (off_corner, off_below)):
                for _, _, kind, c, col, at, n in corner_columns(None, None):
                    first = -n if below else (CB if kind == "coarse" else B)
                    put_column(kind, c, col, first, n, corner[at : at + n, :])

    row = lax.broadcasted_iota(jnp.int32, (32, Z), 0)
    lane = lax.broadcasted_iota(jnp.int32, (32, Z), 1)
    code = fa[...]
    base = 16 * ((row - 8 + 16) // 2 - 8 + 3) + ((lane - 5 + 16) // 2 - 8 + 3) - 1
    inside = (row >= 3) & (row <= 28) & (lane < 26) & (code > 0.0)
    fa[...] = jnp.where(inside, code + base.astype(F32), -1.0)
    sub = lax.broadcasted_iota(jnp.int32, (W, Z), 0)
    lane_w = lax.broadcasted_iota(jnp.int32, (W, Z), 1)
    here = lane_w == 3 * (sub % 8) + sub // 8 + 1
    index = fa[...]
    spread = [jnp.where(here, jnp.broadcast_to(index[e + 3 : e + 4, :], (W, Z)), 0.0) for e in range(ROWS)]
    spread += [jnp.where(lane == 25 * q, index, 0.0) for q in range(2)]
    spread = jnp.concatenate(spread, axis=0).astype(jnp.bfloat16)
    columns = 2 * Z
    wide = jnp.dot(spread, jnp.ones((Z, columns), jnp.bfloat16), preferred_element_type=F32)
    count_nodes = ROWS * W + 64
    which = lax.broadcasted_iota(jnp.int32, (count_nodes, columns), 1).astype(F32)
    hot = (wide == which).astype(F32).astype(jnp.bfloat16)
    for c in range(3):
        table = fk[c]
        high = table.astype(jnp.bfloat16)
        rest = table - high.astype(F32)
        mid = rest.astype(jnp.bfloat16)
        low = (rest - mid.astype(F32)).astype(jnp.bfloat16)
        moved = (
            jnp.dot(hot, high, preferred_element_type=F32)
            + jnp.dot(hot, mid, preferred_element_type=F32)
            + jnp.dot(hot, low, preferred_element_type=F32)
        )
        fd[c] = fd[c] + moved[0 : ROWS * W]
        for q in range(2):
            fx[2 * c + q] = fx[2 * c + q] + moved[ROWS * W + 32 * q : ROWS * W + 32 * (q + 1)]

    place_s = lax.broadcasted_iota(jnp.int32, (8, Z), 0)
    place_z = lax.broadcasted_iota(jnp.int32, (8, Z), 1)
    first_z = place_z == 0
    last_z = place_z == Z - 1
    cols = [plane * B + 3 * place_s + l - 4 for l in range(3)]
    total_y = n_plane * B
    total_x = n_slab * B
    col_in = [((g >= 0) & (g < total_y)).astype(F32) for g in cols]

    def boxed(src, c, e, extra):
        v0, v1, v2 = (src[c, pl.ds(aligned(e * W + 8 * l), 8), :] for l in range(3))
        up = pltpu.roll(v2, 1, 0)
        down = pltpu.roll(v0, 7, 0)
        if extra is not None:
            up = jnp.where(place_s == 0, extra[2 * c, pl.ds(e + 3, 1), :], up)
            down = jnp.where(place_s == 7, extra[2 * c + 1, pl.ds(e + 3, 1), :], down)
        pair = v0 + v1
        out = []
        for t in (pair + up, pair + v2, v1 + v2 + down):
            out.append(
                t
                + jnp.where(first_z, 0.0, pltpu.roll(t, 1, 1))
                + jnp.where(last_z, 0.0, pltpu.roll(t, Z - 1, 1))
            )
        return out

    def stage(src, dst, extra, first, last, keep, gain):
        def sums(e):
            return [boxed(src, c, e, extra) for c in range(3)]

        def step(e, carry):
            before, mid = carry
            after = sums(e + 1)
            row_in = jnp.where((slab * B + e - 5 >= 0) & (slab * B + e - 5 < total_x), gain, 0.0)
            for l in range(3):
                at = pl.ds(aligned(e * W + 8 * l), 8)
                diagonal = 3.0 + fh[at, :]
                weight = col_in[l] * row_in
                for c in range(3):
                    here_v = src[c, at, :]
                    box = before[c][l] + mid[c][l] + after[c][l]
                    r = fr[c, at, :] - (diagonal * here_v - box * (1.0 / 3.0))
                    fr[c, at, :] = r
                    if keep is None:
                        dst[c, at, :] = weight * r
                    else:
                        dst[c, at, :] = keep * here_v + weight * r
            return mid, after

        lax.fori_loop(first, last + 1, step, (sums(first - 1), sums(first)), unroll=8)

    sigma = THETA / DELTA_C
    rho = 1.0 / sigma
    steps = []
    for _ in range(DEGREE - 1):
        rho_new = 1.0 / (2.0 * sigma - rho)
        steps.append((rho_new * rho, 2.0 * rho_new / DELTA_C))
        rho = rho_new
    stage(fd, d0, fx, 1, 24, None, 1.0 / THETA)
    stage(d0, d1, None, 2, 23, *steps[0])
    stage(d1, d2, None, 3, 22, *steps[1])
    stage(d2, d3, None, 4, 21, *steps[2])

    def gather_row(e, carry):
        for c in range(3):
            v = []
            for l in range(3):
                at = pl.ds(aligned(e * W + 8 * l), 8)
                u = fd[c, at, :] + d0[c, at, :] + d1[c, at, :] + d2[c, at, :] + d3[c, at, :]
                st[c * 18 + e - 4, pl.ds(l, 8, stride=3), :] = u
                v.append(u)
            nxt = [v[1], v[2], pltpu.roll(v[0], 7, 0)]
            for l in range(3):
                both = v[l] + nxt[l]
                diff = nxt[l] - v[l]
                both_z = pltpu.roll(both, Z - 1, 1)
                at = pl.ds(aligned((e - 4) * W + 8 * l), 8)
                gx[c, at, :] = both + both_z
                gx[3 + c, at, :] = diff + pltpu.roll(diff, Z - 1, 1)
                gx[6 + c, at, :] = both_z - both
        return carry

    lax.fori_loop(4, 22, gather_row, 0, unroll=6)

    col_ok = [((g >= 0) & (g <= total_y - 2) & (place_z <= Z - 2)).astype(F32) for g in cols]

    def element_row(n, carry):
        gi = slab * B + n - 1
        row_ok = jnp.where((gi >= 0) & (gi <= total_x - 2), 1.0, 0.0)
        made = []
        for l in range(3):
            at = pl.ds(aligned(n * W + 8 * l), 8)
            at_next = pl.ds(aligned((n + 1) * W + 8 * l), 8)
            grad = [[None] * 3 for _ in range(3)]
            for c in range(3):
                grad[c][0] = gx[c, at_next, :] - gx[c, at, :]
                grad[c][1] = gx[3 + c, at_next, :] + gx[3 + c, at, :]
                grad[c][2] = gx[6 + c, at_next, :] + gx[6 + c, at, :]
            exx = 0.25 * grad[0][0]
            eyy = 0.25 * grad[1][1]
            ezz = 0.25 * grad[2][2]
            exy = 0.125 * (grad[0][1] + grad[1][0])
            eyz = 0.125 * (grad[1][2] + grad[2][1])
            ezx = 0.125 * (grad[2][0] + grad[0][2])
            trace = exx + eyy + ezz
            third = trace * (1.0 / 3.0)
            sxx, syy, szz = exx - third, eyy - third, ezz - third
            equiv = (2.0 / 3.0) * (
                sxx * sxx + syy * syy + szz * szz + 2.0 * (exy * exy + eyz * eyz + ezx * ezx)
            )
            ok = col_ok[l] * row_ok
            cons = fc[pl.ds(aligned((n + 4) * W + 8 * l), 8), :]
            power = jnp.exp(((0.15 - 1.0) / 2.0) * jnp.log(0.01 + 3.0 * equiv))
            visc = (2.0 * ok) * (cons * power)
            bulk = (4.0 * ok) * trace
            sig = [
                jnp.where(ok > 0.0, visc * sxx + bulk, 0.0),
                jnp.where(ok > 0.0, visc * syy + bulk, 0.0),
                jnp.where(ok > 0.0, visc * szz + bulk, 0.0),
                jnp.where(ok > 0.0, visc * exy, 0.0),
                jnp.where(ok > 0.0, visc * eyz, 0.0),
                jnp.where(ok > 0.0, visc * ezx, 0.0),
            ]
            norm = (
                sig[0] * sig[0]
                + sig[1] * sig[1]
                + sig[2] * sig[2]
                + 2.0 * (sig[3] * sig[3] + sig[4] * sig[4] + sig[5] * sig[5])
            )
            made.append(sig + [norm])
        for q in range(7):
            a, b, c_ = made[0][q], made[1][q], made[2][q]
            for l, t in enumerate((a + pltpu.roll(c_, 1, 0), a + b, b + c_)):
                ey[q, pl.ds(aligned(n * W + 8 * l), 8), :] = t + pltpu.roll(t, 1, 1)
        return carry

    lax.fori_loop(0, 17, element_row, 0, unroll=4)

    half_z = jnp.where(first_z | last_z, 1.0, 0.5)
    col_half = [jnp.where((g == 0) | (g == total_y - 1), half_z, 0.5 * half_z) for g in cols]

    def node_row(i, carry):
        gi = slab * B + i
        row_half = jnp.where((gi == 0) | (gi == total_x - 1), 1.0, 0.5)
        for l in range(3):
            inverse = col_half[l] * row_half
            at = pl.ds(aligned(i * W + 8 * l), 8)
            at_next = pl.ds(aligned((i + 1) * W + 8 * l), 8)
            mean = [(ey[q, at, :] + ey[q, at_next, :]) * inverse for q in range(7)]
            norm = (
                mean[0] * mean[0]
                + mean[1] * mean[1]
                + mean[2] * mean[2]
                + 2.0 * (mean[3] * mean[3] + mean[4] * mean[4] + mean[5] * mean[5])
            )
            mean[6] = mean[6] - norm
            for q in range(7):
                st[54 + q * 16 + i, pl.ds(l, 8, stride=3), :] = mean[q]
        return carry

    lax.fori_loop(0, B, node_row, 0, unroll=4)

    def put(i, carry):
        for c in range(3):
            disp[c * 16 + i] = st[c * 18 + i + 1, 4:20, :]
        for q in range(6):
            rec[q * 16 + i] = st[54 + q * 16 + i, 4:20, :]
        ind[i] = st[54 + 96 + i, 4:20, :]
        return carry

    lax.fori_loop(0, B, put, 0, unroll=2)


def call(kernel, outs, args, scratch=(), in_hbm=0, cost=0, vmem=48 * 1024 * 1024):
    hbm = pl.BlockSpec(memory_space=pltpu.HBM)
    whole = pl.BlockSpec(memory_space=pltpu.VMEM)
    return pl.pallas_call(
        kernel,
        out_shape=[jax.ShapeDtypeStruct(s, F32) for s in outs],
        in_specs=[hbm] * in_hbm + [whole] * (len(args) - in_hbm),
        out_specs=[whole] * len(outs),
        scratch_shapes=list(scratch),
        compiler_params=pltpu.CompilerParams(vmem_limit_bytes=vmem),
        cost_estimate=pl.CostEstimate(flops=cost, bytes_accessed=2_000_000, transcendentals=0),
    )(*args)


def landing(args):
    return [pltpu.VMEM(a.shape, a.dtype) for a in args] + [pltpu.SemaphoreType.DMA((len(args),))]


def body(start_disp, load, shift, coarse, aggregate, consistency):
    fields = [
        start_disp.reshape(3 * B * B, Z),
        load.reshape(3 * B * B, Z),
        shift.reshape(B * B, Z),
        consistency.reshape(B * B, Z),
        coarse.reshape(3 * CB * CB, Z),
    ]
    n_plane = lax.axis_size("plane")
    n_slab = lax.axis_size("slab")

    def swaps(first, count):
        pairs = [(i, i + 1) for i in range(first, count - 1, 2)]
        return pairs + [(b, a) for a, b in pairs]

    args = [*fields, aggregate]
    first, second, code = call(
        pack_kernel,
        [(P_ROWS, Z), (P_ROWS, Z), (16, Z)],
        args,
        landing(args),
        in_hbm=6,
        cost=1_000_000,
        vmem=FULL,
    )
    first = lax.ppermute(first, "plane", swaps(0, n_plane))
    second = lax.ppermute(second, "plane", swaps(1, n_plane))
    *own, on, off = call(
        own_kernel,
        [(1152, Z), (1152, Z), (384, Z), (384, Z), (384, Z), (16, Z), (Q_ROWS, Z), (Q_ROWS, Z)],
        [*fields, code],
        landing(fields),
        in_hbm=5,
        cost=1_000_000,
    )
    cores = [[i, i + 1] for i in range(0, n_slab, 2)]
    off = lax.ppermute(off, "slab", swaps(1, n_slab))
    on = lax.all_gather(on, "slab", axis_index_groups=cores)
    first, second, on = lax.optimization_barrier((first, second, on))
    code, on_corner, off_corner = call(
        join_kernel, [(16, Z), (T_ROWS, Z), (T_ROWS, Z)], [first, second, own[5]], cost=1_000_000
    )
    off_corner = lax.ppermute(off_corner, "slab", swaps(1, n_slab))
    on_corner = lax.all_gather(on_corner, "slab", axis_index_groups=cores)
    field = (3, ROWS * W, Z)
    shapes = [field, field, (ROWS * W, Z), (ROWS * W, Z), (3, 256, Z), (6, 32, Z), (32, Z)]
    shapes += [field] * 4 + [(9, 18 * W, Z), (7, 17 * W, Z), (54 + 112, W, Z)]
    disp, rec, ind = call(
        smooth_kernel,
        [(48, B, Z), (96, B, Z), (B, B, Z)],
        [on, off, on_corner, off_corner, first, second, *own[:5], code],
        [pltpu.VMEM(shape, F32) for shape in shapes],
        cost=50_000_000,
    )
    return disp.reshape(3, B, B, Z), rec.reshape(6, B, B, Z), ind


def solution(mesh):
    in_specs = (
        P(None, "slab", "plane", None),
        P(None, "slab", "plane", None),
        P("slab", "plane", None),
        P(None, "slab", "plane", None),
        P("slab", "plane"),
        P("slab", "plane", None),
    )
    out_specs = (
        P(None, "slab", "plane", None),
        P(None, "slab", "plane", None),
        P("slab", "plane", None),
    )
    return jax.shard_map(body, mesh=mesh, in_specs=in_specs, out_specs=out_specs, check_vma=False)
```

```python
import jax
import jax.numpy as jnp
from jax import lax
from jax.experimental import pallas as pl
from jax.experimental.pallas import tpu as pltpu
from jax.sharding import PartitionSpec as P

B = 16
CB = 8
Z = 128
W = 24
ROWS = 26

DEGREE = 4
THETA = 4.5
DELTA_C = 3.5
F32 = jnp.float32
FULL = 60 * 1024 * 1024

PS, PL_, PH, PK, PA, PC = 0, 240, 432, 496, 592, 608
P_ROWS = 624
US, UL, UH, UK, UC, UA = 0, 152, 248, 280, 376, 384
U_ROWS = 400
VS, VL, VH, VC = 0, 96, 192, 224
V_ROWS = 240
CORNER = {"start": 5, "load": 4, "shift": 4, "cons": 1, "coarse": 4}

QS, QL, QH, QC, QK = 0, 360, 648, 744, 768
Q_ROWS = 960
TS, TL, TH, TK, TC, TA = 0, 152, 248, 280, 376, 384
T_ROWS = 392


def place(col):
    index = col + 4
    return (index % 3) * 8 + index // 3


def fetch(sources, targets, sems):
    copies = [pltpu.make_async_copy(a, b.at[0 : a.shape[0]], sems.at[k]) for k, (a, b) in enumerate(zip(sources, targets))]
    for copy in copies:
        copy.start()
    for copy in copies:
        copy.wait()


class Whole:
    def __init__(self, ref):
        self.ref = ref
        self.code = ref.at[PA : PA + 16]

    def pieces(self, kind, c, w):
        row = {"start": PS + 80 * c, "load": PL_ + 64 * c, "shift": PH, "cons": PC, "coarse": PK + 32 * c}[kind]
        size = CB if kind == "coarse" else B
        return [(self.ref, row + size * w, 0, size)]


class Split:
    def __init__(self, ends, middle):
        self.ends = ends
        self.middle = middle
        self.code = ends.at[UA : UA + 16]

    def pieces(self, kind, c, w):
        n = CORNER[kind]
        row = {"start": US + 50 * c, "load": UL + 32 * c, "shift": UH, "cons": UC, "coarse": UK + 32 * c}[kind]
        row += 2 * n * w
        if kind == "coarse":
            return [(self.ends, row, 0, CB)]
        between = {"start": VS + 30 * c, "load": VL + 32 * c, "shift": VH, "cons": VC}[kind]
        size = B - 2 * n
        return [
            (self.ends, row, 0, n),
            (self.ends, row + n, B - n, n),
            (self.middle, between + size * w, n, size),
        ]


def corner(payload, kind, c, w, top):
    n = CORNER[kind]
    want = ((CB if kind == "coarse" else B) - n) * top
    for ref, row, begin, size in payload.pieces(kind, c, w):
        if begin <= want and want + n <= begin + size:
            return ref[row + want - begin : row + want - begin + n, :]


def by_side(first, second, run):
    odd = lax.axis_index("plane") % 2
    for side in (0, 1):

        @pl.when(odd == side)
        def _(side=side):
            run(*((first, second) if side else (second, first)))


def pack_kernel(
    start_h, load_h, shift_h, cons_h, coarse_h, agg_h, first, ends, middle, code_o,
    start, load, shift, cons, coarse, agg, sems,
):
    slab = lax.axis_index("slab")
    plane = lax.axis_index("plane")
    coarse_cols = CB * lax.axis_size("plane")
    fetch(
        (start_h, load_h, shift_h, cons_h, coarse_h, agg_h), (start, load, shift, cons, coarse, agg), sems
    )
    value = agg[...]
    step_a = value // coarse_cols - (slab * CB + lax.broadcasted_iota(jnp.int32, (B, B), 0) // 2) + 1
    step_b = value % coarse_cols - (plane * CB + lax.broadcasted_iota(jnp.int32, (B, B), 1) // 2) + 1
    code = (1 + 16 * step_a + step_b).astype(F32)
    for out, row in ((first, PA), (ends, UA), (code_o, 0)):
        out[row : row + 16, :] = jnp.zeros((16, Z), F32)
        out[row : row + 16, 0:B] = code

    arrays = {"start": start, "load": load, "shift": shift, "cons": cons, "coarse": coarse}

    def pack(below, above):
        for payload, side in ((below, 1), (above, 0)):
            for kind, c, w, col in side_columns(side):
                size = CB if kind == "coarse" else B
                own_col = col - size if side else col + size
                column = arrays[kind][pl.ds(size * size * c + own_col, size, stride=size), :]
                for ref, row, begin, n in payload.pieces(kind, c, w):
                    ref[row : row + n, :] = column[begin : begin + n]

    by_side(Whole(first), Split(ends, middle), pack)


OWN = ((0, 2, 2, 5), (1, 1, 0, 6), (2, 1, 1, 5))


def top_rows(top, src, c, rows, width, size):
    return src[pl.ds(pl.multiple_of(c * rows * width + top * (rows * width - size), 8), size), :]


def own_kernel(
    start_h, load_h, shift_h, cons_h, coarse_h, code, es, el, eh, ec, ek, ea, on, off,
    start, load, shift, cons, coarse, sems,
):
    fetch((start_h, load_h, shift_h, cons_h, coarse_h), (start, load, shift, cons, coarse), sems)

    for ci in range(3 * B):
        for l, s0, j0, n in OWN:
            at = ci * W + 8 * l + s0
            for src, dst in ((start, es), (load, el)) + (((shift, eh), (cons, ec)) if ci < B else ()):
                dst[at : at + n, :] = src[pl.ds(ci * B + j0, n, stride=3), :]
    for ca in range(3 * CB):
        ek[16 * ca + 4 : 16 * ca + 12, :] = coarse[8 * ca : 8 * ca + 8, :]
    ea[...] = pltpu.roll(code[...], 5, 1)
    odd = lax.axis_index("slab") % 2
    for out, top in ((on, 1 - odd), (off, odd)):
        whole_rows(top, out, es, el, eh, ec, ek)


def whole_rows(top, out, es, el, eh, ec, ek):
    for c in range(3):
        out[QS + 120 * c : QS + 120 * (c + 1), :] = top_rows(top, es, c, B, W, 120)
        out[QL + 96 * c : QL + 96 * (c + 1), :] = top_rows(top, el, c, B, W, 96)
        out[QK + 64 * c : QK + 64 * (c + 1), :] = top_rows(top, ek, c, CB, 16, 64)
    out[QH : QH + 96, :] = top_rows(top, eh, 0, B, W, 96)
    out[QC : QC + 24, :] = top_rows(top, ec, 0, B, W, 24)


def side_columns(side):
    for c in range(3):
        for w in range(5):
            yield "start", c, w, w - 5 + 21 * side
        for w in range(4):
            yield "load", c, w, w - 4 + 20 * side
            yield "coarse", c, w, w - 4 + 12 * side
    for w in range(4):
        yield "shift", 0, w, w - 4 + 20 * side
    if side == 0:
        yield "cons", 0, 0, -1


def corner_columns():
    at = {"start": TS, "load": TL, "shift": TH, "coarse": TK, "cons": TC}
    for side in (0, 1):
        for kind, c, w, col in side_columns(side):
            yield side, kind, c, w, col, at[kind], CORNER[kind]
            at[kind] += CORNER[kind]


def join_kernel(first, ends, ea, code_o, on, off):
    odd = lax.axis_index("slab") % 2

    def join(low, high):
        lane = lax.broadcasted_iota(jnp.int32, (B, Z), 1)
        left = pltpu.roll(low.code[...], Z - 11, 1)
        right = pltpu.roll(high.code[...], 21, 1)
        code = jnp.where(lane < 5, left, jnp.where(lane < 21, ea[...], jnp.where(lane < 26, right, 0.0)))
        code_o[...] = code
        for on_top in (0, 1):

            @pl.when(odd == 1 - on_top)
            def _(on_top=on_top):
                for out, top in ((on, on_top), (off, 1 - on_top)):
                    out[TA : TA + 8, :] = code[8 * top : 8 * top + 8, :]
                    for side, kind, c, w, _, at, n in corner_columns():
                        out[at : at + n, :] = corner((low, high)[side], kind, c, w, top)

    by_side(Whole(first), Split(ends, None), join)


def smooth_kernel(
    on, off, on_corner, off_corner, first, ends, middle, es, el, eh, ec, ek, code_own,
    disp, rec, ind,
    fd, fr, fh, fc, fk, fx, fa, d0, d1, d2, d3, gx, ey, st,
):
    slab = lax.axis_index("slab")
    plane = lax.axis_index("plane")
    n_slab = lax.axis_size("slab")
    n_plane = lax.axis_size("plane")
    odd = slab % 2

    def aligned(index):
        return pl.multiple_of(index, 8)

    for c in range(3):
        fd[c, 5 * W : 21 * W, :] = es[384 * c : 384 * (c + 1), :]
        fr[c, 5 * W : 21 * W, :] = el[384 * c : 384 * (c + 1), :]
        fk[c, 64:192, :] = ek[128 * c : 128 * (c + 1), :]
    fh[5 * W : 21 * W, :] = eh[...]
    fc[5 * W : 21 * W, :] = ec[...]
    fa[8:24, :] = code_own[...]
    for src, below in ((on.at[1 - odd], odd), (off, 1 - odd)):
        above = 1 - below
        for c in range(3):
            fd[c, pl.ds(aligned(above * (21 * W)), 120), :] = src[QS + 120 * c : QS + 120 * (c + 1), :]
            fr[c, pl.ds(aligned(W + above * (20 * W)), 96), :] = src[QL + 96 * c : QL + 96 * (c + 1), :]
            fk[c, pl.ds(aligned(above * 192), 64), :] = src[QK + 64 * c : QK + 64 * (c + 1), :]
        fh[pl.ds(aligned(W + above * (20 * W)), 96), :] = src[QH : QH + 96, :]
        fc[pl.ds(aligned(4 * W + above * (17 * W)), 24), :] = src[QC : QC + 24, :]
    fa[pl.ds(aligned((1 - odd) * 24), 8), :] = on_corner[1 - odd, TA : TA + 8, :]
    fa[pl.ds(aligned(odd * 24), 8), :] = off_corner[TA : TA + 8, :]

    def put_column(kind, c, col, row, n, value):
        if kind == "coarse":
            fk[c, pl.ds(16 * (row + 4) + col + 4, n, stride=16), :] = value
        elif kind == "start" and col in (-5, 20):
            fx[2 * c + (col > 0), row + 8 : row + 8 + n, :] = value
        elif kind in ("start", "load"):
            {"start": fd, "load": fr}[kind][c, pl.ds((row + 5) * W + place(col), n, stride=W), :] = value
        else:
            {"shift": fh, "cons": fc}[kind][pl.ds((row + 5) * W + place(col), n, stride=W), :] = value

    def put_columns(low, high):
        for payload, side in ((low, 0), (high, 1)):
            for kind, c, w, col in side_columns(side):
                for ref, row, begin, n in payload.pieces(kind, c, w):
                    put_column(kind, c, col, begin, n, ref[row : row + n, :])

    by_side(Whole(first), Split(ends, middle), put_columns)
    for off_below in (0, 1):

        @pl.when(odd == 1 - off_below)
        def _(off_below=off_below):
            for src, below in ((on_corner.at[off_below], 1 - off_below), (off_corner, off_below)):
                for _, kind, c, _, col, at, n in corner_columns():
                    begin = -n if below else (CB if kind == "coarse" else B)
                    put_column(kind, c, col, begin, n, src[at : at + n, :])

    row = lax.broadcasted_iota(jnp.int32, (32, Z), 0)
    lane = lax.broadcasted_iota(jnp.int32, (32, Z), 1)
    code = fa[...]
    base = 16 * ((row - 8 + 16) // 2 - 8 + 3) + ((lane - 5 + 16) // 2 - 8 + 3) - 1
    inside = (row >= 3) & (row <= 28) & (lane < 26) & (code > 0.0)
    fa[...] = jnp.where(inside, code + base.astype(F32), -1.0)
    sub = lax.broadcasted_iota(jnp.int32, (W, Z), 0)
    lane_w = lax.broadcasted_iota(jnp.int32, (W, Z), 1)
    here = lane_w == 3 * (sub % 8) + sub // 8 + 1
    index = fa[...]
    spread = [jnp.where(here, jnp.broadcast_to(index[e + 3 : e + 4, :], (W, Z)), 0.0) for e in range(ROWS)]
    spread += [jnp.where(lane == 25 * q, index, 0.0) for q in range(2)]
    spread = jnp.concatenate(spread, axis=0).astype(jnp.bfloat16)
    columns = 2 * Z
    wide = jnp.dot(spread, jnp.ones((Z, columns), jnp.bfloat16), preferred_element_type=F32)
    count_nodes = ROWS * W + 64
    which = lax.broadcasted_iota(jnp.int32, (count_nodes, columns), 1).astype(F32)
    hot = (wide == which).astype(F32).astype(jnp.bfloat16)
    for c in range(3):
        table = fk[c, 0:256, :]
        high = table.astype(jnp.bfloat16)
        rest = table - high.astype(F32)
        mid = rest.astype(jnp.bfloat16)
        low = (rest - mid.astype(F32)).astype(jnp.bfloat16)
        moved = (
            jnp.dot(hot, high, preferred_element_type=F32)
            + jnp.dot(hot, mid, preferred_element_type=F32)
            + jnp.dot(hot, low, preferred_element_type=F32)
        )
        fd[c, 0 : ROWS * W, :] = fd[c, 0 : ROWS * W, :] + moved[0 : ROWS * W]
        for q in range(2):
            fx[2 * c + q] = fx[2 * c + q] + moved[ROWS * W + 32 * q : ROWS * W + 32 * (q + 1)]

    place_s = lax.broadcasted_iota(jnp.int32, (8, Z), 0)
    place_z = lax.broadcasted_iota(jnp.int32, (8, Z), 1)
    first_z = place_z == 0
    last_z = place_z == Z - 1
    cols = [plane * B + 3 * place_s + l - 4 for l in range(3)]
    total_y = n_plane * B
    total_x = n_slab * B
    col_in = [((g >= 0) & (g < total_y)).astype(F32) for g in cols]

    def boxed(src, c, e, extra):
        v0, v1, v2 = (src[c, pl.ds(aligned(e * W + 8 * l), 8), :] for l in range(3))
        up = pltpu.roll(v2, 1, 0)
        down = pltpu.roll(v0, 7, 0)
        if extra is not None:
            up = jnp.where(place_s == 0, extra[2 * c, pl.ds(e + 3, 1), :], up)
            down = jnp.where(place_s == 7, extra[2 * c + 1, pl.ds(e + 3, 1), :], down)
        pair = v0 + v1
        out = []
        for t in (pair + up, pair + v2, v1 + v2 + down):
            out.append(
                t
                + jnp.where(first_z, 0.0, pltpu.roll(t, 1, 1))
                + jnp.where(last_z, 0.0, pltpu.roll(t, Z - 1, 1))
            )
        return out

    def stage(src, dst, extra, first, last, keep, gain):
        def sums(e):
            return [boxed(src, c, e, extra) for c in range(3)]

        def step(e, carry):
            before, mid = carry
            after = sums(e + 1)
            row_in = jnp.where((slab * B + e - 5 >= 0) & (slab * B + e - 5 < total_x), gain, 0.0)
            for l in range(3):
                at = pl.ds(aligned(e * W + 8 * l), 8)
                diagonal = 3.0 + fh[at, :]
                weight = col_in[l] * row_in
                for c in range(3):
                    here_v = src[c, at, :]
                    box = before[c][l] + mid[c][l] + after[c][l]
                    r = fr[c, at, :] - (diagonal * here_v - box * (1.0 / 3.0))
                    fr[c, at, :] = r
                    if keep is None:
                        dst[c, at, :] = weight * r
                    else:
                        dst[c, at, :] = keep * here_v + weight * r
            return mid, after

        lax.fori_loop(first, last + 1, step, (sums(first - 1), sums(first)), unroll=8)

    sigma = THETA / DELTA_C
    rho = 1.0 / sigma
    steps = []
    for _ in range(DEGREE - 1):
        rho_new = 1.0 / (2.0 * sigma - rho)
        steps.append((rho_new * rho, 2.0 * rho_new / DELTA_C))
        rho = rho_new
    stage(fd, d0, fx, 1, 24, None, 1.0 / THETA)
    stage(d0, d1, None, 2, 23, *steps[0])
    stage(d1, d2, None, 3, 22, *steps[1])
    stage(d2, d3, None, 4, 21, *steps[2])

    def gather_row(e, carry):
        for c in range(3):
            v = []
            for l in range(3):
                at = pl.ds(aligned(e * W + 8 * l), 8)
                u = fd[c, at, :] + d0[c, at, :] + d1[c, at, :] + d2[c, at, :] + d3[c, at, :]
                st[c * 18 + e - 4, pl.ds(l, 8, stride=3), :] = u
                v.append(u)
            nxt = [v[1], v[2], pltpu.roll(v[0], 7, 0)]
            for l in range(3):
                both = v[l] + nxt[l]
                diff = nxt[l] - v[l]
                both_z = pltpu.roll(both, Z - 1, 1)
                at = pl.ds(aligned((e - 4) * W + 8 * l), 8)
                gx[c, at, :] = both + both_z
                gx[3 + c, at, :] = diff + pltpu.roll(diff, Z - 1, 1)
                gx[6 + c, at, :] = both_z - both
        return carry

    lax.fori_loop(4, 22, gather_row, 0, unroll=6)

    col_ok = [((g >= 0) & (g <= total_y - 2) & (place_z <= Z - 2)).astype(F32) for g in cols]

    def element_row(n, carry):
        gi = slab * B + n - 1
        row_ok = jnp.where((gi >= 0) & (gi <= total_x - 2), 1.0, 0.0)
        made = []
        for l in range(3):
            at = pl.ds(aligned(n * W + 8 * l), 8)
            at_next = pl.ds(aligned((n + 1) * W + 8 * l), 8)
            grad = [[None] * 3 for _ in range(3)]
            for c in range(3):
                grad[c][0] = gx[c, at_next, :] - gx[c, at, :]
                grad[c][1] = gx[3 + c, at_next, :] + gx[3 + c, at, :]
                grad[c][2] = gx[6 + c, at_next, :] + gx[6 + c, at, :]
            exx = 0.25 * grad[0][0]
            eyy = 0.25 * grad[1][1]
            ezz = 0.25 * grad[2][2]
            exy = 0.125 * (grad[0][1] + grad[1][0])
            eyz = 0.125 * (grad[1][2] + grad[2][1])
            ezx = 0.125 * (grad[2][0] + grad[0][2])
            trace = exx + eyy + ezz
            third = trace * (1.0 / 3.0)
            sxx, syy, szz = exx - third, eyy - third, ezz - third
            equiv = (2.0 / 3.0) * (
                sxx * sxx + syy * syy + szz * szz + 2.0 * (exy * exy + eyz * eyz + ezx * ezx)
            )
            ok = col_ok[l] * row_ok
            cons = fc[pl.ds(aligned((n + 4) * W + 8 * l), 8), :]
            power = jnp.exp(((0.15 - 1.0) / 2.0) * jnp.log(0.01 + 3.0 * equiv))
            visc = (2.0 * ok) * (cons * power)
            bulk = (4.0 * ok) * trace
            sig = [
                jnp.where(ok > 0.0, visc * sxx + bulk, 0.0),
                jnp.where(ok > 0.0, visc * syy + bulk, 0.0),
                jnp.where(ok > 0.0, visc * szz + bulk, 0.0),
                jnp.where(ok > 0.0, visc * exy, 0.0),
                jnp.where(ok > 0.0, visc * eyz, 0.0),
                jnp.where(ok > 0.0, visc * ezx, 0.0),
            ]
            norm = (
                sig[0] * sig[0]
                + sig[1] * sig[1]
                + sig[2] * sig[2]
                + 2.0 * (sig[3] * sig[3] + sig[4] * sig[4] + sig[5] * sig[5])
            )
            made.append(sig + [norm])
        for q in range(7):
            a, b, c_ = made[0][q], made[1][q], made[2][q]
            for l, t in enumerate((a + pltpu.roll(c_, 1, 0), a + b, b + c_)):
                ey[q, pl.ds(aligned(n * W + 8 * l), 8), :] = t + pltpu.roll(t, 1, 1)
        return carry

    lax.fori_loop(0, 17, element_row, 0, unroll=4)

    half_z = jnp.where(first_z | last_z, 1.0, 0.5)
    col_half = [jnp.where((g == 0) | (g == total_y - 1), half_z, 0.5 * half_z) for g in cols]

    def node_row(i, carry):
        gi = slab * B + i
        row_half = jnp.where((gi == 0) | (gi == total_x - 1), 1.0, 0.5)
        for l in range(3):
            inverse = col_half[l] * row_half
            at = pl.ds(aligned(i * W + 8 * l), 8)
            at_next = pl.ds(aligned((i + 1) * W + 8 * l), 8)
            mean = [(ey[q, at, :] + ey[q, at_next, :]) * inverse for q in range(7)]
            norm = (
                mean[0] * mean[0]
                + mean[1] * mean[1]
                + mean[2] * mean[2]
                + 2.0 * (mean[3] * mean[3] + mean[4] * mean[4] + mean[5] * mean[5])
            )
            mean[6] = mean[6] - norm
            for q in range(7):
                st[54 + q * 16 + i, pl.ds(l, 8, stride=3), :] = mean[q]
        return carry

    lax.fori_loop(0, B, node_row, 0, unroll=4)

    def put(i, carry):
        for c in range(3):
            disp[c * 16 + i] = st[c * 18 + i + 1, 4:20, :]
        for q in range(6):
            rec[q * 16 + i] = st[54 + q * 16 + i, 4:20, :]
        ind[i] = st[54 + 96 + i, 4:20, :]
        return carry

    lax.fori_loop(0, B, put, 0, unroll=2)


def call(kernel, outs, args, scratch=(), in_hbm=0, cost=0, vmem=48 * 1024 * 1024):
    hbm = pl.BlockSpec(memory_space=pltpu.HBM)
    whole = pl.BlockSpec(memory_space=pltpu.VMEM)
    return pl.pallas_call(
        kernel,
        out_shape=[jax.ShapeDtypeStruct(s, F32) for s in outs],
        in_specs=[hbm] * in_hbm + [whole] * (len(args) - in_hbm),
        out_specs=[whole] * len(outs),
        scratch_shapes=list(scratch),
        compiler_params=pltpu.CompilerParams(vmem_limit_bytes=vmem),
        cost_estimate=pl.CostEstimate(flops=cost, bytes_accessed=2_000_000, transcendentals=0),
    )(*args)


def landing(args, more=0):
    return [pltpu.VMEM((a.shape[0] + more, a.shape[1]), a.dtype) for a in args] + [pltpu.SemaphoreType.DMA((len(args),))]


def body(start_disp, load, shift, coarse, aggregate, consistency):
    fields = [
        start_disp.reshape(3 * B * B, Z),
        load.reshape(3 * B * B, Z),
        shift.reshape(B * B, Z),
        consistency.reshape(B * B, Z),
        coarse.reshape(3 * CB * CB, Z),
    ]
    n_plane = lax.axis_size("plane")
    n_slab = lax.axis_size("slab")

    def swaps(first, count):
        pairs = [(i, i + 1) for i in range(first, count - 1, 2)]
        return pairs + [(b, a) for a, b in pairs]

    args = [*fields, aggregate]
    first, ends, middle, code = call(
        pack_kernel,
        [(P_ROWS, Z), (U_ROWS, Z), (V_ROWS, Z), (16, Z)],
        args,
        landing(args),
        in_hbm=6,
        cost=1_000_000,
        vmem=FULL,
    )
    first = lax.ppermute(first, "plane", swaps(0, n_plane))
    ends = lax.ppermute(ends, "plane", swaps(1, n_plane))
    *own, on, off = call(
        own_kernel,
        [(1152, Z), (1152, Z), (384, Z), (384, Z), (384, Z), (16, Z), (Q_ROWS, Z), (Q_ROWS, Z)],
        [*fields, code],
        landing(fields, 8),
        in_hbm=5,
        cost=1_000_000,
    )
    cores = [[i, i + 1] for i in range(0, n_slab, 2)]
    off = lax.ppermute(off, "slab", swaps(1, n_slab))
    on = lax.all_gather(on, "slab", axis_index_groups=cores)
    middle = lax.ppermute(middle, "plane", swaps(1, n_plane))
    first, ends = lax.optimization_barrier((first, ends))
    code, on_corner, off_corner = call(
        join_kernel, [(16, Z), (T_ROWS, Z), (T_ROWS, Z)], [first, ends, own[5]], cost=1_000_000
    )
    off_corner = lax.ppermute(off_corner, "slab", swaps(1, n_slab))
    on_corner, on = lax.optimization_barrier((on_corner, on))
    on_corner = lax.all_gather(on_corner, "slab", axis_index_groups=cores)
    field = (3, ROWS * W, Z)
    longer = (ROWS * W + 96, Z)
    shapes = [(3, *longer), (3, *longer), longer, longer, (3, 256 + 64, Z), (6, 32, Z), (32, Z)]
    shapes += [field] * 4 + [(9, 18 * W, Z), (7, 17 * W, Z), (54 + 112, W, Z)]
    disp, rec, ind = call(
        smooth_kernel,
        [(48, B, Z), (96, B, Z), (B, B, Z)],
        [on, off, on_corner, off_corner, first, ends, middle, *own[:5], code],
        [pltpu.VMEM(shape, F32) for shape in shapes],
        cost=50_000_000,
    )
    return disp.reshape(3, B, B, Z), rec.reshape(6, B, B, Z), ind


def solution(mesh):
    in_specs = (
        P(None, "slab", "plane", None),
        P(None, "slab", "plane", None),
        P("slab", "plane", None),
        P(None, "slab", "plane", None),
        P("slab", "plane"),
        P("slab", "plane", None),
    )
    out_specs = (
        P(None, "slab", "plane", None),
        P(None, "slab", "plane", None),
        P("slab", "plane", None),
    )
    return jax.shard_map(body, mesh=mesh, in_specs=in_specs, out_specs=out_specs, check_vma=False)
```

```python
import jax
import jax.numpy as jnp
from jax import lax
from jax.experimental import pallas as pl
from jax.experimental.pallas import tpu as pltpu
from jax.sharding import PartitionSpec as P

B = 16
CB = 8
Z = 128
W = 24
ROWS = 26

DEGREE = 4
THETA = 4.5
DELTA_C = 3.5
F32 = jnp.float32
FULL = 60 * 1024 * 1024

PS, PL_, PH, PK, PA, PC = 0, 240, 432, 496, 592, 608
P_ROWS = 624
US, UL, UH, UK, UC, UA = 0, 152, 248, 280, 376, 384
U_ROWS = 400
VS, VL, VH, VC = 0, 96, 192, 224
V_ROWS = 240
CORNER = {"start": 5, "load": 4, "shift": 4, "cons": 1, "coarse": 4}

QS, QL, QH, QC, QK = 0, 360, 648, 744, 768
Q_ROWS = 960
TS, TL, TH, TK, TC, TA = 0, 152, 248, 280, 376, 384
T_ROWS = 392


def place(col):
    index = col + 4
    return (index % 3) * 8 + index // 3


def fetch(sources, targets, sems):
    copies = [pltpu.make_async_copy(a, b.at[0 : a.shape[0]], sems.at[k]) for k, (a, b) in enumerate(zip(sources, targets))]
    for copy in copies:
        copy.start()
    for copy in copies:
        copy.wait()


class Whole:
    def __init__(self, ref):
        self.ref = ref
        self.code = ref.at[PA : PA + 16]

    def pieces(self, kind, c, w):
        row = {"start": PS + 80 * c, "load": PL_ + 64 * c, "shift": PH, "cons": PC, "coarse": PK + 32 * c}[kind]
        size = CB if kind == "coarse" else B
        return [(self.ref, row + size * w, 0, size)]


class Split:
    def __init__(self, ends, middle):
        self.ends = ends
        self.middle = middle
        self.code = ends.at[UA : UA + 16]

    def pieces(self, kind, c, w):
        n = CORNER[kind]
        row = {"start": US + 50 * c, "load": UL + 32 * c, "shift": UH, "cons": UC, "coarse": UK + 32 * c}[kind]
        row += 2 * n * w
        if kind == "coarse":
            return [(self.ends, row, 0, CB)]
        between = {"start": VS + 30 * c, "load": VL + 32 * c, "shift": VH, "cons": VC}[kind]
        size = B - 2 * n
        return [
            (self.ends, row, 0, n),
            (self.ends, row + n, B - n, n),
            (self.middle, between + size * w, n, size),
        ]


def corner(payload, kind, c, w, top):
    n = CORNER[kind]
    want = ((CB if kind == "coarse" else B) - n) * top
    for ref, row, begin, size in payload.pieces(kind, c, w):
        if begin <= want and want + n <= begin + size:
            return ref[row + want - begin : row + want - begin + n, :]


def by_side(first, second, run):
    odd = lax.axis_index("plane") % 2
    for side in (0, 1):

        @pl.when(odd == side)
        def _(side=side):
            run(*((first, second) if side else (second, first)))


def pack_kernel(
    start_h, load_h, shift_h, cons_h, coarse_h, agg_h, first, ends, middle, code_o,
    start, load, shift, cons, coarse, agg, sems,
):
    slab = lax.axis_index("slab")
    plane = lax.axis_index("plane")
    coarse_cols = CB * lax.axis_size("plane")
    fetch(
        (start_h, load_h, shift_h, cons_h, coarse_h, agg_h), (start, load, shift, cons, coarse, agg), sems
    )
    value = agg[...]
    step_a = value // coarse_cols - (slab * CB + lax.broadcasted_iota(jnp.int32, (B, B), 0) // 2) + 1
    step_b = value % coarse_cols - (plane * CB + lax.broadcasted_iota(jnp.int32, (B, B), 1) // 2) + 1
    code = (1 + 16 * step_a + step_b).astype(F32)
    for out, row in ((first, PA), (ends, UA), (code_o, 0)):
        out[row : row + 16, :] = jnp.zeros((16, Z), F32)
        out[row : row + 16, 0:B] = code

    arrays = {"start": start, "load": load, "shift": shift, "cons": cons, "coarse": coarse}

    def pack(below, above):
        for payload, side in ((below, 1), (above, 0)):
            for kind, c, w, col in side_columns(side):
                size = CB if kind == "coarse" else B
                own_col = col - size if side else col + size
                column = arrays[kind][pl.ds(size * size * c + own_col, size, stride=size), :]
                for ref, row, begin, n in payload.pieces(kind, c, w):
                    ref[row : row + n, :] = column[begin : begin + n]

    by_side(Whole(first), Split(ends, middle), pack)


OWN = ((0, 2, 2, 5), (1, 1, 0, 6), (2, 1, 1, 5))


def top_rows(top, src, c, rows, width, size):
    return src[pl.ds(pl.multiple_of(c * rows * width + top * (rows * width - size), 8), size), :]


def own_kernel(
    start_h, load_h, shift_h, cons_h, coarse_h, code, es, el, eh, ec, ek, ea, on, off,
    start, load, shift, cons, coarse, sems,
):
    fetch((start_h, load_h, shift_h, cons_h, coarse_h), (start, load, shift, cons, coarse), sems)

    for ci in range(3 * B):
        for l, s0, j0, n in OWN:
            at = ci * W + 8 * l + s0
            for src, dst in ((start, es), (load, el)) + (((shift, eh), (cons, ec)) if ci < B else ()):
                dst[at : at + n, :] = src[pl.ds(ci * B + j0, n, stride=3), :]
    for ca in range(3 * CB):
        ek[16 * ca + 4 : 16 * ca + 12, :] = coarse[8 * ca : 8 * ca + 8, :]
    ea[...] = pltpu.roll(code[...], 5, 1)
    odd = lax.axis_index("slab") % 2
    for out, top in ((on, 1 - odd), (off, odd)):
        whole_rows(top, out, es, el, eh, ec, ek)


def whole_rows(top, out, es, el, eh, ec, ek):
    for c in range(3):
        out[QS + 120 * c : QS + 120 * (c + 1), :] = top_rows(top, es, c, B, W, 120)
        out[QL + 96 * c : QL + 96 * (c + 1), :] = top_rows(top, el, c, B, W, 96)
        out[QK + 64 * c : QK + 64 * (c + 1), :] = top_rows(top, ek, c, CB, 16, 64)
    out[QH : QH + 96, :] = top_rows(top, eh, 0, B, W, 96)
    out[QC : QC + 24, :] = top_rows(top, ec, 0, B, W, 24)


def side_columns(side):
    for c in range(3):
        for w in range(5):
            yield "start", c, w, w - 5 + 21 * side
        for w in range(4):
            yield "load", c, w, w - 4 + 20 * side
            yield "coarse", c, w, w - 4 + 12 * side
    for w in range(4):
        yield "shift", 0, w, w - 4 + 20 * side
    if side == 0:
        yield "cons", 0, 0, -1


def corner_columns():
    at = {"start": TS, "load": TL, "shift": TH, "coarse": TK, "cons": TC}
    for side in (0, 1):
        for kind, c, w, col in side_columns(side):
            yield side, kind, c, w, col, at[kind], CORNER[kind]
            at[kind] += CORNER[kind]


def join_kernel(first, ends, ea, code_o, on, off):
    odd = lax.axis_index("slab") % 2

    def join(low, high):
        lane = lax.broadcasted_iota(jnp.int32, (B, Z), 1)
        left = pltpu.roll(low.code[...], Z - 11, 1)
        right = pltpu.roll(high.code[...], 21, 1)
        code = jnp.where(lane < 5, left, jnp.where(lane < 21, ea[...], jnp.where(lane < 26, right, 0.0)))
        code_o[...] = code
        for on_top in (0, 1):

            @pl.when(odd == 1 - on_top)
            def _(on_top=on_top):
                for out, top in ((on, on_top), (off, 1 - on_top)):
                    out[TA : TA + 8, :] = code[8 * top : 8 * top + 8, :]
                    for side, kind, c, w, _, at, n in corner_columns():
                        out[at : at + n, :] = corner((low, high)[side], kind, c, w, top)

    by_side(Whole(first), Split(ends, None), join)


def smooth_kernel(
    on, off, on_corner, off_corner, first, ends, middle, es, el, eh, ec, ek, code_own,
    disp, rec, ind,
    fd, fr, fh, fc, fk, fx, fa, d0, d1, d2, d3, gx, ey, st,
):
    slab = lax.axis_index("slab")
    plane = lax.axis_index("plane")
    n_slab = lax.axis_size("slab")
    n_plane = lax.axis_size("plane")
    odd = slab % 2

    def aligned(index):
        return pl.multiple_of(index, 8)

    for c in range(3):
        fd[c, 5 * W : 21 * W, :] = es[384 * c : 384 * (c + 1), :]
        fr[c, 5 * W : 21 * W, :] = el[384 * c : 384 * (c + 1), :]
        fk[c, 64:192, :] = ek[128 * c : 128 * (c + 1), :]
    fh[5 * W : 21 * W, :] = eh[...]
    fc[5 * W : 21 * W, :] = ec[...]
    fa[8:24, :] = code_own[...]
    for src, below in ((on.at[1 - odd], odd), (off, 1 - odd)):
        above = 1 - below
        for c in range(3):
            fd[c, pl.ds(aligned(above * (21 * W)), 120), :] = src[QS + 120 * c : QS + 120 * (c + 1), :]
            fr[c, pl.ds(aligned(W + above * (20 * W)), 96), :] = src[QL + 96 * c : QL + 96 * (c + 1), :]
            fk[c, pl.ds(aligned(above * 192), 64), :] = src[QK + 64 * c : QK + 64 * (c + 1), :]
        fh[pl.ds(aligned(W + above * (20 * W)), 96), :] = src[QH : QH + 96, :]
        fc[pl.ds(aligned(4 * W + above * (17 * W)), 24), :] = src[QC : QC + 24, :]
    fa[pl.ds(aligned((1 - odd) * 24), 8), :] = on_corner[1 - odd, TA : TA + 8, :]
    fa[pl.ds(aligned(odd * 24), 8), :] = off_corner[TA : TA + 8, :]

    def put_column(kind, c, col, row, n, value):
        if kind == "coarse":
            fk[c, pl.ds(16 * (row + 4) + col + 4, n, stride=16), :] = value
        elif kind == "start" and col in (-5, 20):
            fx[2 * c + (col > 0), row + 8 : row + 8 + n, :] = value
        elif kind in ("start", "load"):
            {"start": fd, "load": fr}[kind][c, pl.ds((row + 5) * W + place(col), n, stride=W), :] = value
        else:
            {"shift": fh, "cons": fc}[kind][pl.ds((row + 5) * W + place(col), n, stride=W), :] = value

    def put_columns(low, high):
        for payload, side in ((low, 0), (high, 1)):
            for kind, c, w, col in side_columns(side):
                for ref, row, begin, n in payload.pieces(kind, c, w):
                    put_column(kind, c, col, begin, n, ref[row : row + n, :])

    by_side(Whole(first), Split(ends, middle), put_columns)
    for off_below in (0, 1):

        @pl.when(odd == 1 - off_below)
        def _(off_below=off_below):
            for src, below in ((on_corner.at[off_below], 1 - off_below), (off_corner, off_below)):
                for _, kind, c, _, col, at, n in corner_columns():
                    begin = -n if below else (CB if kind == "coarse" else B)
                    put_column(kind, c, col, begin, n, src[at : at + n, :])

    row = lax.broadcasted_iota(jnp.int32, (32, Z), 0)
    lane = lax.broadcasted_iota(jnp.int32, (32, Z), 1)
    code = fa[...]
    base = 16 * ((row - 8 + 16) // 2 - 8 + 3) + ((lane - 5 + 16) // 2 - 8 + 3) - 1
    inside = (row >= 3) & (row <= 28) & (lane < 26) & (code > 0.0)
    fa[...] = jnp.where(inside, code + base.astype(F32), -1.0)
    sub = lax.broadcasted_iota(jnp.int32, (W, Z), 0)
    lane_w = lax.broadcasted_iota(jnp.int32, (W, Z), 1)
    here = lane_w == 3 * (sub % 8) + sub // 8 + 1
    index = fa[...]
    spread = [jnp.where(here, jnp.broadcast_to(index[e + 3 : e + 4, :], (W, Z)), 0.0) for e in range(ROWS)]
    spread += [jnp.where(lane == 25 * q, index, 0.0) for q in range(2)]
    spread = jnp.concatenate(spread, axis=0).astype(jnp.bfloat16)
    columns = 2 * Z
    wide = jnp.dot(spread, jnp.ones((Z, columns), jnp.bfloat16), preferred_element_type=F32)
    count_nodes = ROWS * W + 64
    which = lax.broadcasted_iota(jnp.int32, (count_nodes, columns), 1).astype(F32)
    hot = (wide == which).astype(F32).astype(jnp.bfloat16)
    for c in range(3):
        table = fk[c, 0:256, :]
        high = table.astype(jnp.bfloat16)
        rest = table - high.astype(F32)
        mid = rest.astype(jnp.bfloat16)
        low = (rest - mid.astype(F32)).astype(jnp.bfloat16)
        moved = (
            jnp.dot(hot, high, preferred_element_type=F32)
            + jnp.dot(hot, mid, preferred_element_type=F32)
            + jnp.dot(hot, low, preferred_element_type=F32)
        )
        fd[c, 0 : ROWS * W, :] = fd[c, 0 : ROWS * W, :] + moved[0 : ROWS * W]
        for q in range(2):
            fx[2 * c + q] = fx[2 * c + q] + moved[ROWS * W + 32 * q : ROWS * W + 32 * (q + 1)]

    place_s = lax.broadcasted_iota(jnp.int32, (8, Z), 0)
    place_z = lax.broadcasted_iota(jnp.int32, (8, Z), 1)
    first_z = place_z == 0
    last_z = place_z == Z - 1
    cols = [plane * B + 3 * place_s + l - 4 for l in range(3)]
    total_y = n_plane * B
    total_x = n_slab * B
    col_in = [((g >= 0) & (g < total_y)).astype(F32) for g in cols]

    def boxed(src, c, e, extra):
        v0, v1, v2 = (src[c, pl.ds(aligned(e * W + 8 * l), 8), :] for l in range(3))
        up = pltpu.roll(v2, 1, 0)
        down = pltpu.roll(v0, 7, 0)
        if extra is not None:
            up = jnp.where(place_s == 0, extra[2 * c, pl.ds(e + 3, 1), :], up)
            down = jnp.where(place_s == 7, extra[2 * c + 1, pl.ds(e + 3, 1), :], down)
        pair = v0 + v1
        out = []
        for t in (pair + up, pair + v2, v1 + v2 + down):
            out.append(
                t
                + jnp.where(first_z, 0.0, pltpu.roll(t, 1, 1))
                + jnp.where(last_z, 0.0, pltpu.roll(t, Z - 1, 1))
            )
        return out

    def stage(src, dst, extra, first, last, keep, gain):
        def sums(e):
            return [boxed(src, c, e, extra) for c in range(3)]

        def step(e, carry):
            before, mid = carry
            after = sums(e + 1)
            row_in = jnp.where((slab * B + e - 5 >= 0) & (slab * B + e - 5 < total_x), gain, 0.0)
            for l in range(3):
                at = pl.ds(aligned(e * W + 8 * l), 8)
                diagonal = 3.0 + fh[at, :]
                weight = col_in[l] * row_in
                for c in range(3):
                    here_v = src[c, at, :]
                    box = before[c][l] + mid[c][l] + after[c][l]
                    r = fr[c, at, :] - (diagonal * here_v - box * (1.0 / 3.0))
                    fr[c, at, :] = r
                    if keep is None:
                        dst[c, at, :] = weight * r
                    else:
                        dst[c, at, :] = keep * here_v + weight * r
            return mid, after

        lax.fori_loop(first, last + 1, step, (sums(first - 1), sums(first)), unroll=(last + 1 - first) // 2)

    sigma = THETA / DELTA_C
    rho = 1.0 / sigma
    steps = []
    for _ in range(DEGREE - 1):
        rho_new = 1.0 / (2.0 * sigma - rho)
        steps.append((rho_new * rho, 2.0 * rho_new / DELTA_C))
        rho = rho_new
    stage(fd, d0, fx, 1, 24, None, 1.0 / THETA)
    stage(d0, d1, None, 2, 23, *steps[0])
    stage(d1, d2, None, 3, 22, *steps[1])
    stage(d2, d3, None, 4, 21, *steps[2])

    def gather_row(e, carry):
        for c in range(3):
            v = []
            for l in range(3):
                at = pl.ds(aligned(e * W + 8 * l), 8)
                u = fd[c, at, :] + d0[c, at, :] + d1[c, at, :] + d2[c, at, :] + d3[c, at, :]
                st[c * 18 + e - 4, pl.ds(l, 8, stride=3), :] = u
                v.append(u)
            nxt = [v[1], v[2], pltpu.roll(v[0], 7, 0)]
            for l in range(3):
                both = v[l] + nxt[l]
                diff = nxt[l] - v[l]
                both_z = pltpu.roll(both, Z - 1, 1)
                at = pl.ds(aligned((e - 4) * W + 8 * l), 8)
                gx[c, at, :] = both + both_z
                gx[3 + c, at, :] = diff + pltpu.roll(diff, Z - 1, 1)
                gx[6 + c, at, :] = both_z - both
        return carry

    lax.fori_loop(4, 22, gather_row, 0, unroll=9)

    col_ok = [((g >= 0) & (g <= total_y - 2) & (place_z <= Z - 2)).astype(F32) for g in cols]

    def element_row(n, carry):
        gi = slab * B + n - 1
        row_ok = jnp.where((gi >= 0) & (gi <= total_x - 2), 1.0, 0.0)
        made = []
        for l in range(3):
            at = pl.ds(aligned(n * W + 8 * l), 8)
            at_next = pl.ds(aligned((n + 1) * W + 8 * l), 8)
            grad = [[None] * 3 for _ in range(3)]
            for c in range(3):
                grad[c][0] = gx[c, at_next, :] - gx[c, at, :]
                grad[c][1] = gx[3 + c, at_next, :] + gx[3 + c, at, :]
                grad[c][2] = gx[6 + c, at_next, :] + gx[6 + c, at, :]
            exx = 0.25 * grad[0][0]
            eyy = 0.25 * grad[1][1]
            ezz = 0.25 * grad[2][2]
            exy = 0.125 * (grad[0][1] + grad[1][0])
            eyz = 0.125 * (grad[1][2] + grad[2][1])
            ezx = 0.125 * (grad[2][0] + grad[0][2])
            trace = exx + eyy + ezz
            third = trace * (1.0 / 3.0)
            sxx, syy, szz = exx - third, eyy - third, ezz - third
            equiv = (2.0 / 3.0) * (
                sxx * sxx + syy * syy + szz * szz + 2.0 * (exy * exy + eyz * eyz + ezx * ezx)
            )
            ok = col_ok[l] * row_ok
            cons = fc[pl.ds(aligned((n + 4) * W + 8 * l), 8), :]
            power = jnp.exp(((0.15 - 1.0) / 2.0) * jnp.log(0.01 + 3.0 * equiv))
            visc = (2.0 * ok) * (cons * power)
            bulk = (4.0 * ok) * trace
            sig = [
                jnp.where(ok > 0.0, visc * sxx + bulk, 0.0),
                jnp.where(ok > 0.0, visc * syy + bulk, 0.0),
                jnp.where(ok > 0.0, visc * szz + bulk, 0.0),
                jnp.where(ok > 0.0, visc * exy, 0.0),
                jnp.where(ok > 0.0, visc * eyz, 0.0),
                jnp.where(ok > 0.0, visc * ezx, 0.0),
            ]
            norm = (
                sig[0] * sig[0]
                + sig[1] * sig[1]
                + sig[2] * sig[2]
                + 2.0 * (sig[3] * sig[3] + sig[4] * sig[4] + sig[5] * sig[5])
            )
            made.append(sig + [norm])
        for q in range(7):
            a, b, c_ = made[0][q], made[1][q], made[2][q]
            for l, t in enumerate((a + pltpu.roll(c_, 1, 0), a + b, b + c_)):
                ey[q, pl.ds(aligned(n * W + 8 * l), 8), :] = t + pltpu.roll(t, 1, 1)
        return carry

    lax.fori_loop(0, 17, element_row, 0, unroll=17)

    half_z = jnp.where(first_z | last_z, 1.0, 0.5)
    col_half = [jnp.where((g == 0) | (g == total_y - 1), half_z, 0.5 * half_z) for g in cols]

    def node_row(i, carry):
        gi = slab * B + i
        row_half = jnp.where((gi == 0) | (gi == total_x - 1), 1.0, 0.5)
        for l in range(3):
            inverse = col_half[l] * row_half
            at = pl.ds(aligned(i * W + 8 * l), 8)
            at_next = pl.ds(aligned((i + 1) * W + 8 * l), 8)
            mean = [(ey[q, at, :] + ey[q, at_next, :]) * inverse for q in range(7)]
            norm = (
                mean[0] * mean[0]
                + mean[1] * mean[1]
                + mean[2] * mean[2]
                + 2.0 * (mean[3] * mean[3] + mean[4] * mean[4] + mean[5] * mean[5])
            )
            mean[6] = mean[6] - norm
            for q in range(7):
                st[54 + q * 16 + i, pl.ds(l, 8, stride=3), :] = mean[q]
        return carry

    lax.fori_loop(0, B, node_row, 0, unroll=16)

    def put(i, carry):
        for c in range(3):
            disp[c * 16 + i] = st[c * 18 + i + 1, 4:20, :]
        for q in range(6):
            rec[q * 16 + i] = st[54 + q * 16 + i, 4:20, :]
        ind[i] = st[54 + 96 + i, 4:20, :]
        return carry

    lax.fori_loop(0, B, put, 0, unroll=16)


def call(kernel, outs, args, scratch=(), in_hbm=0, cost=0, vmem=48 * 1024 * 1024):
    hbm = pl.BlockSpec(memory_space=pltpu.HBM)
    whole = pl.BlockSpec(memory_space=pltpu.VMEM)
    return pl.pallas_call(
        kernel,
        out_shape=[jax.ShapeDtypeStruct(s, F32) for s in outs],
        in_specs=[hbm] * in_hbm + [whole] * (len(args) - in_hbm),
        out_specs=[whole] * len(outs),
        scratch_shapes=list(scratch),
        compiler_params=pltpu.CompilerParams(vmem_limit_bytes=vmem),
        cost_estimate=pl.CostEstimate(flops=cost, bytes_accessed=2_000_000, transcendentals=0),
    )(*args)


def landing(args, more=0):
    return [pltpu.VMEM((a.shape[0] + more, a.shape[1]), a.dtype) for a in args] + [pltpu.SemaphoreType.DMA((len(args),))]


def body(start_disp, load, shift, coarse, aggregate, consistency):
    fields = [
        start_disp.reshape(3 * B * B, Z),
        load.reshape(3 * B * B, Z),
        shift.reshape(B * B, Z),
        consistency.reshape(B * B, Z),
        coarse.reshape(3 * CB * CB, Z),
    ]
    n_plane = lax.axis_size("plane")
    n_slab = lax.axis_size("slab")

    def swaps(first, count):
        pairs = [(i, i + 1) for i in range(first, count - 1, 2)]
        return pairs + [(b, a) for a, b in pairs]

    args = [*fields, aggregate]
    first, ends, middle, code = call(
        pack_kernel,
        [(P_ROWS, Z), (U_ROWS, Z), (V_ROWS, Z), (16, Z)],
        args,
        landing(args),
        in_hbm=6,
        cost=1_000_000,
        vmem=FULL,
    )
    first = lax.ppermute(first, "plane", swaps(0, n_plane))
    ends = lax.ppermute(ends, "plane", swaps(1, n_plane))
    *own, on, off = call(
        own_kernel,
        [(1152, Z), (1152, Z), (384, Z), (384, Z), (384, Z), (16, Z), (Q_ROWS, Z), (Q_ROWS, Z)],
        [*fields, code],
        landing(fields, 8),
        in_hbm=5,
        cost=1_000_000,
    )
    cores = [[i, i + 1] for i in range(0, n_slab, 2)]
    off = lax.ppermute(off, "slab", swaps(1, n_slab))
    on = lax.all_gather(on, "slab", axis_index_groups=cores)
    middle = lax.ppermute(middle, "plane", swaps(1, n_plane))
    first, ends = lax.optimization_barrier((first, ends))
    code, on_corner, off_corner = call(
        join_kernel, [(16, Z), (T_ROWS, Z), (T_ROWS, Z)], [first, ends, own[5]], cost=1_000_000
    )
    off_corner = lax.ppermute(off_corner, "slab", swaps(1, n_slab))
    on_corner, on = lax.optimization_barrier((on_corner, on))
    on_corner = lax.all_gather(on_corner, "slab", axis_index_groups=cores)
    field = (3, ROWS * W, Z)
    longer = (ROWS * W + 96, Z)
    shapes = [(3, *longer), (3, *longer), longer, longer, (3, 256 + 64, Z), (6, 32, Z), (32, Z)]
    shapes += [field] * 4 + [(9, 18 * W, Z), (7, 17 * W, Z), (54 + 112, W, Z)]
    disp, rec, ind = call(
        smooth_kernel,
        [(48, B, Z), (96, B, Z), (B, B, Z)],
        [on, off, on_corner, off_corner, first, ends, middle, *own[:5], code],
        [pltpu.VMEM(shape, F32) for shape in shapes],
        cost=50_000_000,
    )
    return disp.reshape(3, B, B, Z), rec.reshape(6, B, B, Z), ind


def solution(mesh):
    in_specs = (
        P(None, "slab", "plane", None),
        P(None, "slab", "plane", None),
        P("slab", "plane", None),
        P(None, "slab", "plane", None),
        P("slab", "plane"),
        P("slab", "plane", None),
    )
    out_specs = (
        P(None, "slab", "plane", None),
        P(None, "slab", "plane", None),
        P("slab", "plane", None),
    )
    return jax.shard_map(body, mesh=mesh, in_specs=in_specs, out_specs=out_specs, check_vma=False)
```

```python
import jax
import jax.numpy as jnp
from jax import lax
from jax.experimental import pallas as pl
from jax.experimental.pallas import tpu as pltpu
from jax.sharding import PartitionSpec as P

B = 16
CB = 8
Z = 128
W = 24
ROWS = 26

DEGREE = 4
THETA = 4.5
DELTA_C = 3.5
F32 = jnp.float32
FULL = 60 * 1024 * 1024

PS, PL_, PH, PK, PA, PC = 0, 240, 432, 496, 592, 608
P_ROWS = 624
US, UL, UH, UK, UC, UA = 0, 152, 248, 280, 376, 384
U_ROWS = 400
VS, VL, VH, VC = 0, 96, 192, 224
V_ROWS = 240
CORNER = {"start": 5, "load": 4, "shift": 4, "cons": 1, "coarse": 4}

QS, QL, QH, QC, QK = 0, 360, 648, 744, 768
Q_ROWS = 960
TS, TL, TH, TK, TC, TA = 0, 152, 248, 280, 376, 384
T_ROWS = 392


def place(col):
    index = col + 4
    return (index % 3) * 8 + index // 3


def fetch(sources, targets, sems):
    copies = [pltpu.make_async_copy(a, b.at[0 : a.shape[0]], sems.at[k]) for k, (a, b) in enumerate(zip(sources, targets))]
    for copy in copies:
        copy.start()
    for copy in copies:
        copy.wait()


class Whole:
    def __init__(self, ref):
        self.ref = ref
        self.code = ref.at[PA : PA + 16]

    def pieces(self, kind, c, w):
        row = {"start": PS + 80 * c, "load": PL_ + 64 * c, "shift": PH, "cons": PC, "coarse": PK + 32 * c}[kind]
        size = CB if kind == "coarse" else B
        return [(self.ref, row + size * w, 0, size)]


class Split:
    def __init__(self, ends, middle):
        self.ends = ends
        self.middle = middle
        self.code = ends.at[UA : UA + 16]

    def pieces(self, kind, c, w):
        n = CORNER[kind]
        row = {"start": US + 50 * c, "load": UL + 32 * c, "shift": UH, "cons": UC, "coarse": UK + 32 * c}[kind]
        row += 2 * n * w
        if kind == "coarse":
            return [(self.ends, row, 0, CB)]
        between = {"start": VS + 30 * c, "load": VL + 32 * c, "shift": VH, "cons": VC}[kind]
        size = B - 2 * n
        return [
            (self.ends, row, 0, n),
            (self.ends, row + n, B - n, n),
            (self.middle, between + size * w, n, size),
        ]


def corner(payload, kind, c, w, top):
    n = CORNER[kind]
    want = ((CB if kind == "coarse" else B) - n) * top
    for ref, row, begin, size in payload.pieces(kind, c, w):
        if begin <= want and want + n <= begin + size:
            return ref[row + want - begin : row + want - begin + n, :]


def by_side(first, second, run):
    odd = lax.axis_index("plane") % 2
    for side in (0, 1):

        @pl.when(odd == side)
        def _(side=side):
            run(*((first, second) if side else (second, first)))


def aggregate_code(agg):
    slab = lax.axis_index("slab")
    plane = lax.axis_index("plane")
    coarse_cols = CB * lax.axis_size("plane")
    value = agg[0:B, :]
    step_a = value // coarse_cols - (slab * CB + lax.broadcasted_iota(jnp.int32, (B, B), 0) // 2) + 1
    step_b = value % coarse_cols - (plane * CB + lax.broadcasted_iota(jnp.int32, (B, B), 1) // 2) + 1
    return (1 + 16 * step_a + step_b).astype(F32)


def pack_kernel(
    start_h, load_h, shift_h, cons_h, coarse_h, agg_h, first, ends, middle,
    start, load, shift, cons, coarse, agg, sems,
):
    fetch(
        (start_h, load_h, shift_h, cons_h, coarse_h, agg_h), (start, load, shift, cons, coarse, agg), sems
    )
    code = aggregate_code(agg)
    for out, row in ((first, PA), (ends, UA)):
        out[row : row + 16, :] = jnp.zeros((16, Z), F32)
        out[row : row + 16, 0:B] = code
    arrays = {"start": start, "load": load, "shift": shift, "cons": cons, "coarse": coarse}

    def pack(below, above):
        for payload, side in ((below, 1), (above, 0)):
            for kind, c, w, col in side_columns(side):
                size = CB if kind == "coarse" else B
                own_col = col - size if side else col + size
                column = arrays[kind][pl.ds(size * size * c + own_col, size, stride=size), :]
                for ref, row, begin, n in payload.pieces(kind, c, w):
                    ref[row : row + n, :] = column[begin : begin + n]

    by_side(Whole(first), Split(ends, middle), pack)


OWN = ((0, 2, 2, 5), (1, 1, 0, 6), (2, 1, 1, 5))


def top_rows(top, src, c, rows, width, size):
    return src[pl.ds(pl.multiple_of(c * rows * width + top * (rows * width - size), 8), size), :]


def own_kernel(
    start_h, load_h, shift_h, cons_h, coarse_h, agg_h, es, el, eh, ec, ek, ea, on, off,
    start, load, shift, cons, coarse, agg, sems,
):
    fetch(
        (start_h, load_h, shift_h, cons_h, coarse_h, agg_h), (start, load, shift, cons, coarse, agg), sems
    )

    for ci in range(3 * B):
        for l, s0, j0, n in OWN:
            at = ci * W + 8 * l + s0
            for src, dst in ((start, es), (load, el)) + (((shift, eh), (cons, ec)) if ci < B else ()):
                dst[at : at + n, :] = src[pl.ds(ci * B + j0, n, stride=3), :]
    for ca in range(3 * CB):
        ek[16 * ca + 4 : 16 * ca + 12, :] = coarse[8 * ca : 8 * ca + 8, :]
    ea[...] = jnp.zeros((B, Z), F32)
    ea[:, 0:B] = aggregate_code(agg)
    ea[...] = pltpu.roll(ea[...], 5, 1)
    odd = lax.axis_index("slab") % 2
    for out, top in ((on, 1 - odd), (off, odd)):
        whole_rows(top, out, es, el, eh, ec, ek)


def whole_rows(top, out, es, el, eh, ec, ek):
    for c in range(3):
        out[QS + 120 * c : QS + 120 * (c + 1), :] = top_rows(top, es, c, B, W, 120)
        out[QL + 96 * c : QL + 96 * (c + 1), :] = top_rows(top, el, c, B, W, 96)
        out[QK + 64 * c : QK + 64 * (c + 1), :] = top_rows(top, ek, c, CB, 16, 64)
    out[QH : QH + 96, :] = top_rows(top, eh, 0, B, W, 96)
    out[QC : QC + 24, :] = top_rows(top, ec, 0, B, W, 24)


def side_columns(side):
    for c in range(3):
        for w in range(5):
            yield "start", c, w, w - 5 + 21 * side
        for w in range(4):
            yield "load", c, w, w - 4 + 20 * side
            yield "coarse", c, w, w - 4 + 12 * side
    for w in range(4):
        yield "shift", 0, w, w - 4 + 20 * side
    if side == 0:
        yield "cons", 0, 0, -1


def corner_columns():
    at = {"start": TS, "load": TL, "shift": TH, "coarse": TK, "cons": TC}
    for side in (0, 1):
        for kind, c, w, col in side_columns(side):
            yield side, kind, c, w, col, at[kind], CORNER[kind]
            at[kind] += CORNER[kind]


def join_kernel(first, ends, ea, code_o, on, off):
    odd = lax.axis_index("slab") % 2

    def join(low, high):
        lane = lax.broadcasted_iota(jnp.int32, (B, Z), 1)
        left = pltpu.roll(low.code[...], Z - 11, 1)
        right = pltpu.roll(high.code[...], 21, 1)
        code = jnp.where(lane < 5, left, jnp.where(lane < 21, ea[...], jnp.where(lane < 26, right, 0.0)))
        code_o[...] = code
        for on_top in (0, 1):

            @pl.when(odd == 1 - on_top)
            def _(on_top=on_top):
                for out, top in ((on, on_top), (off, 1 - on_top)):
                    out[TA : TA + 8, :] = code[8 * top : 8 * top + 8, :]
                    for side, kind, c, w, _, at, n in corner_columns():
                        out[at : at + n, :] = corner((low, high)[side], kind, c, w, top)

    by_side(Whole(first), Split(ends, None), join)


def smooth_kernel(
    on, off, on_corner, off_corner, first, ends, middle, es, el, eh, ec, ek, code_own,
    disp, rec, ind,
    fd, fr, fh, fc, fk, fx, fa, d0, d1, d2, d3, gx, ey, st,
):
    slab = lax.axis_index("slab")
    plane = lax.axis_index("plane")
    n_slab = lax.axis_size("slab")
    n_plane = lax.axis_size("plane")
    odd = slab % 2

    def aligned(index):
        return pl.multiple_of(index, 8)

    for c in range(3):
        fd[c, 5 * W : 21 * W, :] = es[384 * c : 384 * (c + 1), :]
        fr[c, 5 * W : 21 * W, :] = el[384 * c : 384 * (c + 1), :]
        fk[c, 64:192, :] = ek[128 * c : 128 * (c + 1), :]
    fh[5 * W : 21 * W, :] = eh[...]
    fc[5 * W : 21 * W, :] = ec[...]
    fa[8:24, :] = code_own[...]
    for src, below in ((on.at[1 - odd], odd), (off, 1 - odd)):
        above = 1 - below
        for c in range(3):
            fd[c, pl.ds(aligned(above * (21 * W)), 120), :] = src[QS + 120 * c : QS + 120 * (c + 1), :]
            fr[c, pl.ds(aligned(W + above * (20 * W)), 96), :] = src[QL + 96 * c : QL + 96 * (c + 1), :]
            fk[c, pl.ds(aligned(above * 192), 64), :] = src[QK + 64 * c : QK + 64 * (c + 1), :]
        fh[pl.ds(aligned(W + above * (20 * W)), 96), :] = src[QH : QH + 96, :]
        fc[pl.ds(aligned(4 * W + above * (17 * W)), 24), :] = src[QC : QC + 24, :]
    fa[pl.ds(aligned((1 - odd) * 24), 8), :] = on_corner[1 - odd, TA : TA + 8, :]
    fa[pl.ds(aligned(odd * 24), 8), :] = off_corner[TA : TA + 8, :]

    def put_column(kind, c, col, row, n, value):
        if kind == "coarse":
            fk[c, pl.ds(16 * (row + 4) + col + 4, n, stride=16), :] = value
        elif kind == "start" and col in (-5, 20):
            fx[2 * c + (col > 0), row + 8 : row + 8 + n, :] = value
        elif kind in ("start", "load"):
            {"start": fd, "load": fr}[kind][c, pl.ds((row + 5) * W + place(col), n, stride=W), :] = value
        else:
            {"shift": fh, "cons": fc}[kind][pl.ds((row + 5) * W + place(col), n, stride=W), :] = value

    def put_columns(low, high):
        for payload, side in ((low, 0), (high, 1)):
            for kind, c, w, col in side_columns(side):
                for ref, row, begin, n in payload.pieces(kind, c, w):
                    put_column(kind, c, col, begin, n, ref[row : row + n, :])

    by_side(Whole(first), Split(ends, middle), put_columns)
    for off_below in (0, 1):

        @pl.when(odd == 1 - off_below)
        def _(off_below=off_below):
            for src, below in ((on_corner.at[off_below], 1 - off_below), (off_corner, off_below)):
                for _, kind, c, _, col, at, n in corner_columns():
                    begin = -n if below else (CB if kind == "coarse" else B)
                    put_column(kind, c, col, begin, n, src[at : at + n, :])

    row = lax.broadcasted_iota(jnp.int32, (32, Z), 0)
    lane = lax.broadcasted_iota(jnp.int32, (32, Z), 1)
    code = fa[...]
    base = 16 * ((row - 8 + 16) // 2 - 8 + 3) + ((lane - 5 + 16) // 2 - 8 + 3) - 1
    inside = (row >= 3) & (row <= 28) & (lane < 26) & (code > 0.0)
    fa[...] = jnp.where(inside, code + base.astype(F32), -1.0)
    sub = lax.broadcasted_iota(jnp.int32, (W, Z), 0)
    lane_w = lax.broadcasted_iota(jnp.int32, (W, Z), 1)
    here = lane_w == 3 * (sub % 8) + sub // 8 + 1
    index = fa[...]
    spread = [jnp.where(here, jnp.broadcast_to(index[e + 3 : e + 4, :], (W, Z)), 0.0) for e in range(ROWS)]
    spread += [jnp.where(lane == 25 * q, index, 0.0) for q in range(2)]
    spread = jnp.concatenate(spread, axis=0).astype(jnp.bfloat16)
    columns = 2 * Z
    wide = jnp.dot(spread, jnp.ones((Z, columns), jnp.bfloat16), preferred_element_type=F32)
    count_nodes = ROWS * W + 64
    which = lax.broadcasted_iota(jnp.int32, (count_nodes, columns), 1).astype(F32)
    hot = (wide == which).astype(F32).astype(jnp.bfloat16)
    for c in range(3):
        table = fk[c, 0:256, :]
        high = table.astype(jnp.bfloat16)
        rest = table - high.astype(F32)
        mid = rest.astype(jnp.bfloat16)
        low = (rest - mid.astype(F32)).astype(jnp.bfloat16)
        moved = (
            jnp.dot(hot, high, preferred_element_type=F32)
            + jnp.dot(hot, mid, preferred_element_type=F32)
            + jnp.dot(hot, low, preferred_element_type=F32)
        )
        fd[c, 0 : ROWS * W, :] = fd[c, 0 : ROWS * W, :] + moved[0 : ROWS * W]
        for q in range(2):
            fx[2 * c + q] = fx[2 * c + q] + moved[ROWS * W + 32 * q : ROWS * W + 32 * (q + 1)]

    place_s = lax.broadcasted_iota(jnp.int32, (8, Z), 0)
    place_z = lax.broadcasted_iota(jnp.int32, (8, Z), 1)
    first_z = place_z == 0
    last_z = place_z == Z - 1
    cols = [plane * B + 3 * place_s + l - 4 for l in range(3)]
    total_y = n_plane * B
    total_x = n_slab * B
    col_in = [((g >= 0) & (g < total_y)).astype(F32) for g in cols]

    def boxed(src, c, e, extra):
        v0, v1, v2 = (src[c, pl.ds(aligned(e * W + 8 * l), 8), :] for l in range(3))
        up = pltpu.roll(v2, 1, 0)
        down = pltpu.roll(v0, 7, 0)
        if extra is not None:
            up = jnp.where(place_s == 0, extra[2 * c, pl.ds(e + 3, 1), :], up)
            down = jnp.where(place_s == 7, extra[2 * c + 1, pl.ds(e + 3, 1), :], down)
        pair = v0 + v1
        out = []
        for t in (pair + up, pair + v2, v1 + v2 + down):
            out.append(
                t
                + jnp.where(first_z, 0.0, pltpu.roll(t, 1, 1))
                + jnp.where(last_z, 0.0, pltpu.roll(t, Z - 1, 1))
            )
        return out

    def stage(src, dst, extra, first, last, keep, gain):
        def sums(e):
            return [boxed(src, c, e, extra) for c in range(3)]

        def step(e, carry):
            before, mid = carry
            after = sums(e + 1)
            row_in = jnp.where((slab * B + e - 5 >= 0) & (slab * B + e - 5 < total_x), gain, 0.0)
            for l in range(3):
                at = pl.ds(aligned(e * W + 8 * l), 8)
                diagonal = 3.0 + fh[at, :]
                weight = col_in[l] * row_in
                for c in range(3):
                    here_v = src[c, at, :]
                    box = before[c][l] + mid[c][l] + after[c][l]
                    r = fr[c, at, :] - (diagonal * here_v - box * (1.0 / 3.0))
                    fr[c, at, :] = r
                    if keep is None:
                        dst[c, at, :] = weight * r
                    else:
                        dst[c, at, :] = keep * here_v + weight * r
            return mid, after

        lax.fori_loop(first, last + 1, step, (sums(first - 1), sums(first)), unroll=(last + 1 - first) // 2)

    sigma = THETA / DELTA_C
    rho = 1.0 / sigma
    steps = []
    for _ in range(DEGREE - 1):
        rho_new = 1.0 / (2.0 * sigma - rho)
        steps.append((rho_new * rho, 2.0 * rho_new / DELTA_C))
        rho = rho_new
    stage(fd, d0, fx, 1, 24, None, 1.0 / THETA)
    stage(d0, d1, None, 2, 23, *steps[0])
    stage(d1, d2, None, 3, 22, *steps[1])
    stage(d2, d3, None, 4, 21, *steps[2])

    def gather_row(e, carry):
        for c in range(3):
            v = []
            for l in range(3):
                at = pl.ds(aligned(e * W + 8 * l), 8)
                u = fd[c, at, :] + d0[c, at, :] + d1[c, at, :] + d2[c, at, :] + d3[c, at, :]
                st[c * 18 + e - 4, pl.ds(l, 8, stride=3), :] = u
                v.append(u)
            nxt = [v[1], v[2], pltpu.roll(v[0], 7, 0)]
            for l in range(3):
                both = v[l] + nxt[l]
                diff = nxt[l] - v[l]
                both_z = pltpu.roll(both, Z - 1, 1)
                at = pl.ds(aligned((e - 4) * W + 8 * l), 8)
                gx[c, at, :] = both + both_z
                gx[3 + c, at, :] = diff + pltpu.roll(diff, Z - 1, 1)
                gx[6 + c, at, :] = both_z - both
        return carry

    lax.fori_loop(4, 22, gather_row, 0, unroll=9)

    col_ok = [((g >= 0) & (g <= total_y - 2) & (place_z <= Z - 2)).astype(F32) for g in cols]

    def element_row(n, carry):
        gi = slab * B + n - 1
        row_ok = jnp.where((gi >= 0) & (gi <= total_x - 2), 1.0, 0.0)
        made = []
        for l in range(3):
            at = pl.ds(aligned(n * W + 8 * l), 8)
            at_next = pl.ds(aligned((n + 1) * W + 8 * l), 8)
            grad = [[None] * 3 for _ in range(3)]
            for c in range(3):
                grad[c][0] = gx[c, at_next, :] - gx[c, at, :]
                grad[c][1] = gx[3 + c, at_next, :] + gx[3 + c, at, :]
                grad[c][2] = gx[6 + c, at_next, :] + gx[6 + c, at, :]
            exx = 0.25 * grad[0][0]
            eyy = 0.25 * grad[1][1]
            ezz = 0.25 * grad[2][2]
            exy = 0.125 * (grad[0][1] + grad[1][0])
            eyz = 0.125 * (grad[1][2] + grad[2][1])
            ezx = 0.125 * (grad[2][0] + grad[0][2])
            trace = exx + eyy + ezz
            third = trace * (1.0 / 3.0)
            sxx, syy, szz = exx - third, eyy - third, ezz - third
            equiv = (2.0 / 3.0) * (
                sxx * sxx + syy * syy + szz * szz + 2.0 * (exy * exy + eyz * eyz + ezx * ezx)
            )
            ok = col_ok[l] * row_ok
            cons = fc[pl.ds(aligned((n + 4) * W + 8 * l), 8), :]
            power = jnp.exp(((0.15 - 1.0) / 2.0) * jnp.log(0.01 + 3.0 * equiv))
            visc = (2.0 * ok) * (cons * power)
            bulk = (4.0 * ok) * trace
            sig = [
                jnp.where(ok > 0.0, visc * sxx + bulk, 0.0),
                jnp.where(ok > 0.0, visc * syy + bulk, 0.0),
                jnp.where(ok > 0.0, visc * szz + bulk, 0.0),
                jnp.where(ok > 0.0, visc * exy, 0.0),
                jnp.where(ok > 0.0, visc * eyz, 0.0),
                jnp.where(ok > 0.0, visc * ezx, 0.0),
            ]
            norm = (
                sig[0] * sig[0]
                + sig[1] * sig[1]
                + sig[2] * sig[2]
                + 2.0 * (sig[3] * sig[3] + sig[4] * sig[4] + sig[5] * sig[5])
            )
            made.append(sig + [norm])
        for q in range(7):
            a, b, c_ = made[0][q], made[1][q], made[2][q]
            for l, t in enumerate((a + pltpu.roll(c_, 1, 0), a + b, b + c_)):
                ey[q, pl.ds(aligned(n * W + 8 * l), 8), :] = t + pltpu.roll(t, 1, 1)
        return carry

    lax.fori_loop(0, 17, element_row, 0, unroll=17)

    half_z = jnp.where(first_z | last_z, 1.0, 0.5)
    col_half = [jnp.where((g == 0) | (g == total_y - 1), half_z, 0.5 * half_z) for g in cols]

    def node_row(i, carry):
        gi = slab * B + i
        row_half = jnp.where((gi == 0) | (gi == total_x - 1), 1.0, 0.5)
        for l in range(3):
            inverse = col_half[l] * row_half
            at = pl.ds(aligned(i * W + 8 * l), 8)
            at_next = pl.ds(aligned((i + 1) * W + 8 * l), 8)
            mean = [(ey[q, at, :] + ey[q, at_next, :]) * inverse for q in range(7)]
            norm = (
                mean[0] * mean[0]
                + mean[1] * mean[1]
                + mean[2] * mean[2]
                + 2.0 * (mean[3] * mean[3] + mean[4] * mean[4] + mean[5] * mean[5])
            )
            mean[6] = mean[6] - norm
            for q in range(7):
                st[54 + q * 16 + i, pl.ds(l, 8, stride=3), :] = mean[q]
        return carry

    lax.fori_loop(0, B, node_row, 0, unroll=16)

    def put(i, carry):
        for c in range(3):
            disp[c * 16 + i] = st[c * 18 + i + 1, 4:20, :]
        for q in range(6):
            rec[q * 16 + i] = st[54 + q * 16 + i, 4:20, :]
        ind[i] = st[54 + 96 + i, 4:20, :]
        return carry

    lax.fori_loop(0, B, put, 0, unroll=16)


def call(kernel, outs, args, scratch=(), in_hbm=0, cost=0, vmem=48 * 1024 * 1024):
    hbm = pl.BlockSpec(memory_space=pltpu.HBM)
    whole = pl.BlockSpec(memory_space=pltpu.VMEM)
    return pl.pallas_call(
        kernel,
        out_shape=[jax.ShapeDtypeStruct(s, F32) for s in outs],
        in_specs=[hbm] * in_hbm + [whole] * (len(args) - in_hbm),
        out_specs=[whole] * len(outs),
        scratch_shapes=list(scratch),
        compiler_params=pltpu.CompilerParams(vmem_limit_bytes=vmem),
        cost_estimate=pl.CostEstimate(flops=cost, bytes_accessed=2_000_000, transcendentals=0),
    )(*args)


def landing(args, more=0):
    return [pltpu.VMEM((a.shape[0] + more, a.shape[1]), a.dtype) for a in args] + [pltpu.SemaphoreType.DMA((len(args),))]


def body(start_disp, load, shift, coarse, aggregate, consistency):
    fields = [
        start_disp.reshape(3 * B * B, Z),
        load.reshape(3 * B * B, Z),
        shift.reshape(B * B, Z),
        consistency.reshape(B * B, Z),
        coarse.reshape(3 * CB * CB, Z),
    ]
    n_plane = lax.axis_size("plane")
    n_slab = lax.axis_size("slab")

    def swaps(first, count):
        pairs = [(i, i + 1) for i in range(first, count - 1, 2)]
        return pairs + [(b, a) for a, b in pairs]

    args = [*fields, aggregate]
    first, ends, middle = call(
        pack_kernel,
        [(P_ROWS, Z), (U_ROWS, Z), (V_ROWS, Z)],
        args,
        landing(args),
        in_hbm=6,
        cost=1_000_000,
        vmem=FULL,
    )
    first = lax.ppermute(first, "plane", swaps(0, n_plane))
    ends = lax.ppermute(ends, "plane", swaps(1, n_plane))
    *own, on, off = call(
        own_kernel,
        [(1152, Z), (1152, Z), (384, Z), (384, Z), (384, Z), (16, Z), (Q_ROWS, Z), (Q_ROWS, Z)],
        args,
        landing(args, 8),
        in_hbm=6,
        cost=1_000_000,
    )
    cores = [[i, i + 1] for i in range(0, n_slab, 2)]
    off = lax.ppermute(off, "slab", swaps(1, n_slab))
    on = lax.all_gather(on, "slab", axis_index_groups=cores)
    middle = lax.ppermute(middle, "plane", swaps(1, n_plane))
    first, ends = lax.optimization_barrier((first, ends))
    code, on_corner, off_corner = call(
        join_kernel, [(16, Z), (T_ROWS, Z), (T_ROWS, Z)], [first, ends, own[5]], cost=1_000_000
    )
    off_corner = lax.ppermute(off_corner, "slab", swaps(1, n_slab))
    on_corner, on = lax.optimization_barrier((on_corner, on))
    on_corner = lax.all_gather(on_corner, "slab", axis_index_groups=cores)
    field = (3, ROWS * W, Z)
    longer = (ROWS * W + 96, Z)
    shapes = [(3, *longer), (3, *longer), longer, longer, (3, 256 + 64, Z), (6, 32, Z), (32, Z)]
    shapes += [field] * 4 + [(9, 18 * W, Z), (7, 17 * W, Z), (54 + 112, W, Z)]
    disp, rec, ind = call(
        smooth_kernel,
        [(48, B, Z), (96, B, Z), (B, B, Z)],
        [on, off, on_corner, off_corner, first, ends, middle, *own[:5], code],
        [pltpu.VMEM(shape, F32) for shape in shapes],
        cost=50_000_000,
    )
    return disp.reshape(3, B, B, Z), rec.reshape(6, B, B, Z), ind


def solution(mesh):
    in_specs = (
        P(None, "slab", "plane", None),
        P(None, "slab", "plane", None),
        P("slab", "plane", None),
        P(None, "slab", "plane", None),
        P("slab", "plane"),
        P("slab", "plane", None),
    )
    out_specs = (
        P(None, "slab", "plane", None),
        P(None, "slab", "plane", None),
        P("slab", "plane", None),
    )
    return jax.shard_map(body, mesh=mesh, in_specs=in_specs, out_specs=out_specs, check_vma=False)
```

```python
import jax
import jax.numpy as jnp
from jax import lax
from jax.experimental import pallas as pl
from jax.experimental.pallas import tpu as pltpu
from jax.sharding import PartitionSpec as P

B = 16
CB = 8
Z = 128
W = 24
ROWS = 26

DEGREE = 4
THETA = 4.5
DELTA_C = 3.5
F32 = jnp.float32
FULL = 60 * 1024 * 1024

PS, PL_, PH, PK, PA, PC = 0, 240, 432, 496, 592, 608
P_ROWS = 624
US, UL, UH, UK, UC, UA = 0, 152, 248, 280, 376, 384
U_ROWS = 400
VS, VL, VH, VC = 0, 96, 192, 224
V_ROWS = 240
CORNER = {"start": 5, "load": 4, "shift": 4, "cons": 1, "coarse": 4}

QS, QL, QH, QC, QK = 0, 360, 648, 744, 768
Q_ROWS = 960
TS, TL, TH, TK, TC, TA = 0, 152, 248, 280, 376, 384
T_ROWS = 392


def place(col):
    index = col + 4
    return (index % 3) * 8 + index // 3


def fetch(sources, targets, sems):
    copies = [pltpu.make_async_copy(a, b.at[0 : a.shape[0]], sems.at[k]) for k, (a, b) in enumerate(zip(sources, targets))]
    for copy in copies:
        copy.start()
    for copy in copies:
        copy.wait()


class Whole:
    def __init__(self, ref):
        self.ref = ref
        self.code = ref.at[PA : PA + 16]

    def pieces(self, kind, c, w):
        row = {"start": PS + 80 * c, "load": PL_ + 64 * c, "shift": PH, "cons": PC, "coarse": PK + 32 * c}[kind]
        size = CB if kind == "coarse" else B
        return [(self.ref, row + size * w, 0, size)]


class Split:
    def __init__(self, ends, middle):
        self.ends = ends
        self.middle = middle
        self.code = ends.at[UA : UA + 16]

    def pieces(self, kind, c, w):
        n = CORNER[kind]
        row = {"start": US + 50 * c, "load": UL + 32 * c, "shift": UH, "cons": UC, "coarse": UK + 32 * c}[kind]
        row += 2 * n * w
        if kind == "coarse":
            return [(self.ends, row, 0, CB)]
        between = {"start": VS + 30 * c, "load": VL + 32 * c, "shift": VH, "cons": VC}[kind]
        size = B - 2 * n
        return [
            (self.ends, row, 0, n),
            (self.ends, row + n, B - n, n),
            (self.middle, between + size * w, n, size),
        ]


def corner(payload, kind, c, w, top):
    n = CORNER[kind]
    want = ((CB if kind == "coarse" else B) - n) * top
    for ref, row, begin, size in payload.pieces(kind, c, w):
        if begin <= want and want + n <= begin + size:
            return ref[row + want - begin : row + want - begin + n, :]


def by_side(first, second, run):
    odd = lax.axis_index("plane") % 2
    for side in (0, 1):

        @pl.when(odd == side)
        def _(side=side):
            run(*((first, second) if side else (second, first)))


def aggregate_code(agg):
    slab = lax.axis_index("slab")
    plane = lax.axis_index("plane")
    coarse_cols = CB * lax.axis_size("plane")
    value = agg[0:B, :]
    step_a = value // coarse_cols - (slab * CB + lax.broadcasted_iota(jnp.int32, (B, B), 0) // 2) + 1
    step_b = value % coarse_cols - (plane * CB + lax.broadcasted_iota(jnp.int32, (B, B), 1) // 2) + 1
    return (1 + 16 * step_a + step_b).astype(F32)


def pack_kernel(
    start_h, load_h, shift_h, cons_h, coarse_h, agg_h, first, ends, middle,
    start, load, shift, cons, coarse, agg, sems,
):
    fetch(
        (start_h, load_h, shift_h, cons_h, coarse_h, agg_h), (start, load, shift, cons, coarse, agg), sems
    )
    code = aggregate_code(agg)
    for out, row in ((first, PA), (ends, UA)):
        out[row : row + 16, :] = jnp.zeros((16, Z), F32)
        out[row : row + 16, 0:B] = code
    arrays = {"start": start, "load": load, "shift": shift, "cons": cons, "coarse": coarse}

    def pack(below, above):
        for payload, side in ((below, 1), (above, 0)):
            for kind, c, w, col in side_columns(side):
                size = CB if kind == "coarse" else B
                own_col = col - size if side else col + size
                column = arrays[kind][pl.ds(size * size * c + own_col, size, stride=size), :]
                for ref, row, begin, n in payload.pieces(kind, c, w):
                    ref[row : row + n, :] = column[begin : begin + n]

    by_side(Whole(first), Split(ends, middle), pack)


OWN = ((0, 2, 2, 5), (1, 1, 0, 6), (2, 1, 1, 5))


def top_rows(top, src, c, rows, width, size):
    return src[pl.ds(pl.multiple_of(c * rows * width + top * (rows * width - size), 8), size), :]


def own_kernel(
    start_h, load_h, shift_h, cons_h, coarse_h, agg_h, es, el, eh, ec, ek, ea, on, off,
    start, load, shift, cons, coarse, agg, sems,
):
    fetch(
        (start_h, load_h, shift_h, cons_h, coarse_h, agg_h), (start, load, shift, cons, coarse, agg), sems
    )

    for ci in range(3 * B):
        for l, s0, j0, n in OWN:
            at = ci * W + 8 * l + s0
            for src, dst in ((start, es), (load, el)) + (((shift, eh), (cons, ec)) if ci < B else ()):
                dst[at : at + n, :] = src[pl.ds(ci * B + j0, n, stride=3), :]
    for ca in range(3 * CB):
        ek[16 * ca + 4 : 16 * ca + 12, :] = coarse[8 * ca : 8 * ca + 8, :]
    ea[...] = jnp.zeros((B, Z), F32)
    ea[:, 0:B] = aggregate_code(agg)
    ea[...] = pltpu.roll(ea[...], 5, 1)
    odd = lax.axis_index("slab") % 2
    for out, top in ((on, 1 - odd), (off, odd)):
        whole_rows(top, out, es, el, eh, ec, ek)


def whole_rows(top, out, es, el, eh, ec, ek):
    for c in range(3):
        out[QS + 120 * c : QS + 120 * (c + 1), :] = top_rows(top, es, c, B, W, 120)
        out[QL + 96 * c : QL + 96 * (c + 1), :] = top_rows(top, el, c, B, W, 96)
        out[QK + 64 * c : QK + 64 * (c + 1), :] = top_rows(top, ek, c, CB, 16, 64)
    out[QH : QH + 96, :] = top_rows(top, eh, 0, B, W, 96)
    out[QC : QC + 24, :] = top_rows(top, ec, 0, B, W, 24)


def side_columns(side):
    for c in range(3):
        for w in range(5):
            yield "start", c, w, w - 5 + 21 * side
        for w in range(4):
            yield "load", c, w, w - 4 + 20 * side
            yield "coarse", c, w, w - 4 + 12 * side
    for w in range(4):
        yield "shift", 0, w, w - 4 + 20 * side
    if side == 0:
        yield "cons", 0, 0, -1


def corner_columns():
    at = {"start": TS, "load": TL, "shift": TH, "coarse": TK, "cons": TC}
    for side in (0, 1):
        for kind, c, w, col in side_columns(side):
            yield side, kind, c, w, col, at[kind], CORNER[kind]
            at[kind] += CORNER[kind]


def join_kernel(first, ends, ea, code_o, on, off):
    odd = lax.axis_index("slab") % 2

    def join(low, high):
        lane = lax.broadcasted_iota(jnp.int32, (B, Z), 1)
        left = pltpu.roll(low.code[...], Z - 11, 1)
        right = pltpu.roll(high.code[...], 21, 1)
        code = jnp.where(lane < 5, left, jnp.where(lane < 21, ea[...], jnp.where(lane < 26, right, 0.0)))
        code_o[...] = code
        for on_top in (0, 1):

            @pl.when(odd == 1 - on_top)
            def _(on_top=on_top):
                for out, top in ((on, on_top), (off, 1 - on_top)):
                    out[TA : TA + 8, :] = code[8 * top : 8 * top + 8, :]
                    for side, kind, c, w, _, at, n in corner_columns():
                        out[at : at + n, :] = corner((low, high)[side], kind, c, w, top)

    by_side(Whole(first), Split(ends, None), join)


def smooth_kernel(
    on, off, on_corner, off_corner, first, ends, middle, es, el, eh, ec, ek, code_own,
    disp, rec, ind,
    fd, fr, fh, fc, fk, fx, fa, d0, d1, d2, d3, gx, ey, st,
):
    slab = lax.axis_index("slab")
    plane = lax.axis_index("plane")
    n_slab = lax.axis_size("slab")
    n_plane = lax.axis_size("plane")
    odd = slab % 2

    def aligned(index):
        return pl.multiple_of(index, 8)

    for c in range(3):
        fd[c, 5 * W : 21 * W, :] = es[384 * c : 384 * (c + 1), :]
        fr[c, 5 * W : 21 * W, :] = el[384 * c : 384 * (c + 1), :]
        fk[c, 64:192, :] = ek[128 * c : 128 * (c + 1), :]
    fh[5 * W : 21 * W, :] = eh[...]
    fc[5 * W : 21 * W, :] = ec[...]
    fa[8:24, :] = code_own[...]
    for src, below in ((on.at[1 - odd], odd), (off, 1 - odd)):
        above = 1 - below
        for c in range(3):
            fd[c, pl.ds(aligned(above * (21 * W)), 120), :] = src[QS + 120 * c : QS + 120 * (c + 1), :]
            fr[c, pl.ds(aligned(W + above * (20 * W)), 96), :] = src[QL + 96 * c : QL + 96 * (c + 1), :]
            fk[c, pl.ds(aligned(above * 192), 64), :] = src[QK + 64 * c : QK + 64 * (c + 1), :]
        fh[pl.ds(aligned(W + above * (20 * W)), 96), :] = src[QH : QH + 96, :]
        fc[pl.ds(aligned(4 * W + above * (17 * W)), 24), :] = src[QC : QC + 24, :]
    fa[pl.ds(aligned((1 - odd) * 24), 8), :] = on_corner[1 - odd, TA : TA + 8, :]
    fa[pl.ds(aligned(odd * 24), 8), :] = off_corner[TA : TA + 8, :]

    def put_column(kind, c, col, row, n, value):
        if kind == "coarse":
            fk[c, pl.ds(16 * (row + 4) + col + 4, n, stride=16), :] = value
        elif kind == "start" and col in (-5, 20):
            fx[2 * c + (col > 0), row + 8 : row + 8 + n, :] = value
        elif kind in ("start", "load"):
            {"start": fd, "load": fr}[kind][c, pl.ds((row + 5) * W + place(col), n, stride=W), :] = value
        else:
            {"shift": fh, "cons": fc}[kind][pl.ds((row + 5) * W + place(col), n, stride=W), :] = value

    def put_columns(low, high):
        for payload, side in ((low, 0), (high, 1)):
            for kind, c, w, col in side_columns(side):
                for ref, row, begin, n in payload.pieces(kind, c, w):
                    put_column(kind, c, col, begin, n, ref[row : row + n, :])

    by_side(Whole(first), Split(ends, middle), put_columns)
    for off_below in (0, 1):

        @pl.when(odd == 1 - off_below)
        def _(off_below=off_below):
            for src, below in ((on_corner.at[off_below], 1 - off_below), (off_corner, off_below)):
                for _, kind, c, _, col, at, n in corner_columns():
                    begin = -n if below else (CB if kind == "coarse" else B)
                    put_column(kind, c, col, begin, n, src[at : at + n, :])

    row = lax.broadcasted_iota(jnp.int32, (32, Z), 0)
    lane = lax.broadcasted_iota(jnp.int32, (32, Z), 1)
    code = fa[...]
    base = 16 * ((row - 8 + 16) // 2 - 8 + 3) + ((lane - 5 + 16) // 2 - 8 + 3) - 1
    inside = (row >= 3) & (row <= 28) & (lane < 26) & (code > 0.0)
    fa[...] = jnp.where(inside, code + base.astype(F32), -1.0)
    sub = lax.broadcasted_iota(jnp.int32, (W, Z), 0)
    lane_w = lax.broadcasted_iota(jnp.int32, (W, Z), 1)
    here = lane_w == 3 * (sub % 8) + sub // 8 + 1
    index = fa[...]
    spread = [jnp.where(here, jnp.broadcast_to(index[e + 3 : e + 4, :], (W, Z)), 0.0) for e in range(ROWS)]
    spread += [jnp.where(lane == 25 * q, index, 0.0) for q in range(2)]
    spread = jnp.concatenate(spread, axis=0).astype(jnp.bfloat16)
    columns = 2 * Z
    wide = jnp.dot(spread, jnp.ones((Z, columns), jnp.bfloat16), preferred_element_type=F32)
    count_nodes = ROWS * W + 64
    which = lax.broadcasted_iota(jnp.int32, (count_nodes, columns), 1).astype(F32)
    hot = (wide == which).astype(F32).astype(jnp.bfloat16)
    for c in range(3):
        table = fk[c, 0:256, :]
        high = table.astype(jnp.bfloat16)
        rest = table - high.astype(F32)
        mid = rest.astype(jnp.bfloat16)
        low = (rest - mid.astype(F32)).astype(jnp.bfloat16)
        moved = (
            jnp.dot(hot, high, preferred_element_type=F32)
            + jnp.dot(hot, mid, preferred_element_type=F32)
            + jnp.dot(hot, low, preferred_element_type=F32)
        )
        fd[c, 0 : ROWS * W, :] = fd[c, 0 : ROWS * W, :] + moved[0 : ROWS * W]
        for q in range(2):
            fx[2 * c + q] = fx[2 * c + q] + moved[ROWS * W + 32 * q : ROWS * W + 32 * (q + 1)]

    place_s = lax.broadcasted_iota(jnp.int32, (8, Z), 0)
    place_z = lax.broadcasted_iota(jnp.int32, (8, Z), 1)
    first_z = place_z == 0
    last_z = place_z == Z - 1
    cols = [plane * B + 3 * place_s + l - 4 for l in range(3)]
    total_y = n_plane * B
    total_x = n_slab * B
    col_in = [((g >= 0) & (g < total_y)).astype(F32) for g in cols]

    def boxed(src, c, e, extra):
        v0, v1, v2 = (src[c, pl.ds(aligned(e * W + 8 * l), 8), :] for l in range(3))
        up = pltpu.roll(v2, 1, 0)
        down = pltpu.roll(v0, 7, 0)
        if extra is not None:
            up = jnp.where(place_s == 0, extra[2 * c, pl.ds(e + 3, 1), :], up)
            down = jnp.where(place_s == 7, extra[2 * c + 1, pl.ds(e + 3, 1), :], down)
        pair = v0 + v1
        out = []
        for t in (pair + up, pair + v2, v1 + v2 + down):
            out.append(
                t
                + jnp.where(first_z, 0.0, pltpu.roll(t, 1, 1))
                + jnp.where(last_z, 0.0, pltpu.roll(t, Z - 1, 1))
            )
        return out

    def stage(src, dst, extra, first, last, keep, gain):
        def sums(e):
            return [boxed(src, c, e, extra) for c in range(3)]

        def step(e, carry):
            before, mid = carry
            after = sums(e + 1)
            row_in = jnp.where((slab * B + e - 5 >= 0) & (slab * B + e - 5 < total_x), gain, 0.0)
            for l in range(3):
                at = pl.ds(aligned(e * W + 8 * l), 8)
                diagonal = 3.0 + fh[at, :]
                weight = col_in[l] * row_in
                for c in range(3):
                    here_v = src[c, at, :]
                    box = before[c][l] + mid[c][l] + after[c][l]
                    r = fr[c, at, :] - (diagonal * here_v - box * (1.0 / 3.0))
                    fr[c, at, :] = r
                    if keep is None:
                        dst[c, at, :] = weight * r
                    else:
                        dst[c, at, :] = keep * here_v + weight * r
            return mid, after

        lax.fori_loop(first, last + 1, step, (sums(first - 1), sums(first)), unroll=(last + 1 - first) // 2)

    sigma = THETA / DELTA_C
    rho = 1.0 / sigma
    steps = []
    for _ in range(DEGREE - 1):
        rho_new = 1.0 / (2.0 * sigma - rho)
        steps.append((rho_new * rho, 2.0 * rho_new / DELTA_C))
        rho = rho_new
    stage(fd, d0, fx, 1, 24, None, 1.0 / THETA)
    stage(d0, d1, None, 2, 23, *steps[0])
    stage(d1, d2, None, 3, 22, *steps[1])
    stage(d2, d3, None, 4, 21, *steps[2])

    def gather_row(e, carry):
        for c in range(3):
            v = []
            for l in range(3):
                at = pl.ds(aligned(e * W + 8 * l), 8)
                u = fd[c, at, :] + d0[c, at, :] + d1[c, at, :] + d2[c, at, :] + d3[c, at, :]
                st[c * 18 + e - 4, pl.ds(l, 8, stride=3), :] = u
                v.append(u)
            nxt = [v[1], v[2], pltpu.roll(v[0], 7, 0)]
            for l in range(3):
                both = v[l] + nxt[l]
                diff = nxt[l] - v[l]
                both_z = pltpu.roll(both, Z - 1, 1)
                at = pl.ds(aligned((e - 4) * W + 8 * l), 8)
                gx[c, at, :] = both + both_z
                gx[3 + c, at, :] = diff + pltpu.roll(diff, Z - 1, 1)
                gx[6 + c, at, :] = both_z - both
        return carry

    lax.fori_loop(4, 22, gather_row, 0, unroll=9)

    col_ok = [((g >= 0) & (g <= total_y - 2) & (place_z <= Z - 2)).astype(F32) for g in cols]

    def element_row(n, carry):
        gi = slab * B + n - 1
        row_ok = jnp.where((gi >= 0) & (gi <= total_x - 2), 1.0, 0.0)
        made = []
        for l in range(3):
            at = pl.ds(aligned(n * W + 8 * l), 8)
            at_next = pl.ds(aligned((n + 1) * W + 8 * l), 8)
            grad = [[None] * 3 for _ in range(3)]
            for c in range(3):
                grad[c][0] = gx[c, at_next, :] - gx[c, at, :]
                grad[c][1] = gx[3 + c, at_next, :] + gx[3 + c, at, :]
                grad[c][2] = gx[6 + c, at_next, :] + gx[6 + c, at, :]
            exx = 0.25 * grad[0][0]
            eyy = 0.25 * grad[1][1]
            ezz = 0.25 * grad[2][2]
            exy = 0.125 * (grad[0][1] + grad[1][0])
            eyz = 0.125 * (grad[1][2] + grad[2][1])
            ezx = 0.125 * (grad[2][0] + grad[0][2])
            trace = exx + eyy + ezz
            third = trace * (1.0 / 3.0)
            sxx, syy, szz = exx - third, eyy - third, ezz - third
            equiv = (2.0 / 3.0) * (
                sxx * sxx + syy * syy + szz * szz + 2.0 * (exy * exy + eyz * eyz + ezx * ezx)
            )
            ok = col_ok[l] * row_ok
            cons = fc[pl.ds(aligned((n + 4) * W + 8 * l), 8), :]
            power = jnp.exp(((0.15 - 1.0) / 2.0) * jnp.log(0.01 + 3.0 * equiv))
            visc = (2.0 * ok) * (cons * power)
            bulk = (4.0 * ok) * trace
            sig = [
                jnp.where(ok > 0.0, visc * sxx + bulk, 0.0),
                jnp.where(ok > 0.0, visc * syy + bulk, 0.0),
                jnp.where(ok > 0.0, visc * szz + bulk, 0.0),
                jnp.where(ok > 0.0, visc * exy, 0.0),
                jnp.where(ok > 0.0, visc * eyz, 0.0),
                jnp.where(ok > 0.0, visc * ezx, 0.0),
            ]
            norm = (
                sig[0] * sig[0]
                + sig[1] * sig[1]
                + sig[2] * sig[2]
                + 2.0 * (sig[3] * sig[3] + sig[4] * sig[4] + sig[5] * sig[5])
            )
            made.append(sig + [norm])
        for q in range(7):
            a, b, c_ = made[0][q], made[1][q], made[2][q]
            for l, t in enumerate((a + pltpu.roll(c_, 1, 0), a + b, b + c_)):
                ey[q, pl.ds(aligned(n * W + 8 * l), 8), :] = t + pltpu.roll(t, 1, 1)
        return carry

    lax.fori_loop(0, 17, element_row, 0, unroll=17)

    half_z = jnp.where(first_z | last_z, 1.0, 0.5)
    col_half = [jnp.where((g == 0) | (g == total_y - 1), half_z, 0.5 * half_z) for g in cols]

    def node_row(i, carry):
        gi = slab * B + i
        row_half = jnp.where((gi == 0) | (gi == total_x - 1), 1.0, 0.5)
        for l in range(3):
            inverse = col_half[l] * row_half
            at = pl.ds(aligned(i * W + 8 * l), 8)
            at_next = pl.ds(aligned((i + 1) * W + 8 * l), 8)
            mean = [(ey[q, at, :] + ey[q, at_next, :]) * inverse for q in range(7)]
            norm = (
                mean[0] * mean[0]
                + mean[1] * mean[1]
                + mean[2] * mean[2]
                + 2.0 * (mean[3] * mean[3] + mean[4] * mean[4] + mean[5] * mean[5])
            )
            mean[6] = mean[6] - norm
            for q in range(7):
                st[54 + q * 16 + i, pl.ds(l, 8, stride=3), :] = mean[q]
        return carry

    lax.fori_loop(0, B, node_row, 0, unroll=16)

    def put(i, carry):
        for c in range(3):
            disp[c * 16 + i] = st[c * 18 + i + 1, 4:20, :]
        for q in range(6):
            rec[q * 16 + i] = st[54 + q * 16 + i, 4:20, :]
        ind[i] = st[54 + 96 + i, 4:20, :]
        return carry

    lax.fori_loop(0, B, put, 0, unroll=16)


def call(kernel, outs, args, scratch=(), in_hbm=0, cost=0, vmem=48 * 1024 * 1024):
    hbm = pl.BlockSpec(memory_space=pltpu.HBM)
    whole = pl.BlockSpec(memory_space=pltpu.VMEM)
    return pl.pallas_call(
        kernel,
        out_shape=[jax.ShapeDtypeStruct(s, F32) for s in outs],
        in_specs=[hbm] * in_hbm + [whole] * (len(args) - in_hbm),
        out_specs=[whole] * len(outs),
        scratch_shapes=list(scratch),
        compiler_params=pltpu.CompilerParams(vmem_limit_bytes=vmem),
        cost_estimate=pl.CostEstimate(flops=cost, bytes_accessed=2_000_000, transcendentals=0),
    )(*args)


def landing(args, more=0):
    return [pltpu.VMEM((a.shape[0] + more, a.shape[1]), a.dtype) for a in args] + [pltpu.SemaphoreType.DMA((len(args),))]


def body(start_disp, load, shift, coarse, aggregate, consistency):
    fields = [
        start_disp.reshape(3 * B * B, Z),
        load.reshape(3 * B * B, Z),
        shift.reshape(B * B, Z),
        consistency.reshape(B * B, Z),
        coarse.reshape(3 * CB * CB, Z),
    ]
    n_plane = lax.axis_size("plane")
    n_slab = lax.axis_size("slab")

    def swaps(first, count):
        pairs = [(i, i + 1) for i in range(first, count - 1, 2)]
        return pairs + [(b, a) for a, b in pairs]

    args = [*fields, aggregate]
    first, ends, middle = call(
        pack_kernel,
        [(P_ROWS, Z), (U_ROWS, Z), (V_ROWS, Z)],
        args,
        landing(args),
        in_hbm=6,
        cost=1_000_000,
        vmem=FULL,
    )
    first = lax.ppermute(first, "plane", swaps(0, n_plane))
    ends = lax.ppermute(ends, "plane", swaps(1, n_plane))
    *own, on, off = call(
        own_kernel,
        [(1152, Z), (1152, Z), (384, Z), (384, Z), (384, Z), (16, Z), (Q_ROWS, Z), (Q_ROWS, Z)],
        args,
        landing(args, 8),
        in_hbm=6,
        cost=1_000_000,
    )
    cores = [[i, i + 1] for i in range(0, n_slab, 2)]
    off, first = lax.optimization_barrier((off, first))
    off = lax.ppermute(off, "slab", swaps(1, n_slab))
    on = lax.all_gather(on, "slab", axis_index_groups=cores)
    middle = lax.ppermute(middle, "plane", swaps(1, n_plane))
    first, ends = lax.optimization_barrier((first, ends))
    code, on_corner, off_corner = call(
        join_kernel, [(16, Z), (T_ROWS, Z), (T_ROWS, Z)], [first, ends, own[5]], cost=1_000_000
    )
    off_corner = lax.ppermute(off_corner, "slab", swaps(1, n_slab))
    on_corner, on = lax.optimization_barrier((on_corner, on))
    on_corner = lax.all_gather(on_corner, "slab", axis_index_groups=cores)
    field = (3, ROWS * W, Z)
    longer = (ROWS * W + 96, Z)
    shapes = [(3, *longer), (3, *longer), longer, longer, (3, 256 + 64, Z), (6, 32, Z), (32, Z)]
    shapes += [field] * 4 + [(9, 18 * W, Z), (7, 17 * W, Z), (54 + 112, W, Z)]
    disp, rec, ind = call(
        smooth_kernel,
        [(48, B, Z), (96, B, Z), (B, B, Z)],
        [on, off, on_corner, off_corner, first, ends, middle, *own[:5], code],
        [pltpu.VMEM(shape, F32) for shape in shapes],
        cost=50_000_000,
    )
    return disp.reshape(3, B, B, Z), rec.reshape(6, B, B, Z), ind


def solution(mesh):
    in_specs = (
        P(None, "slab", "plane", None),
        P(None, "slab", "plane", None),
        P("slab", "plane", None),
        P(None, "slab", "plane", None),
        P("slab", "plane"),
        P("slab", "plane", None),
    )
    out_specs = (
        P(None, "slab", "plane", None),
        P(None, "slab", "plane", None),
        P("slab", "plane", None),
    )
    return jax.shard_map(body, mesh=mesh, in_specs=in_specs, out_specs=out_specs, check_vma=False)
```
